128 devices in a mesh: dp: 8 (over y_lo, x), ctx: 16 (over y_hi, z, core).
Axes of the slice: x: 4, y: 4 (y_hi: 2, y_lo: 2; y = y_hi * 2 + y_lo), z: 4, core: 2. Of those that a mesh axis runs over, the one named last changes fastest.
Arguments:
- tokens: bfloat16 [32768, 1024], P(('dp', 'ctx')), may hold values from -6 to 6
- cotangent: bfloat16 [32768, 1024], P(('dp', 'ctx')), may hold values from -6 to 6
- in_proj: bfloat16 [1024, 2048], replicated, may hold values from -0.1875 to 0.1875
- out_proj: bfloat16 [512, 1024], replicated, may hold values from -0.25 to 0.25
- rab_time: float32 [12, 4], replicated, may hold values from -3 to 3
- seq_lengths: int32 [8, 3], P('dp'), may hold values from 1 to 2048, 4096 in all within a row
- block_mask: int32 [8, 32, 32], P('dp', 'ctx'), may hold values 0 or 1
- time_bucket: int32 [32768], P(('dp', 'ctx')), may hold values from 0 to 28665, as said below
Outputs:
- output: bfloat16 [32768, 1024], P(('dp', 'ctx'))
- grad_in: bfloat16 [32768, 1024], P(('dp', 'ctx'))
- proj_grad: float32 [512, 1024], P(('dp', 'ctx'))
- rab_grad: float32 [12, 4], replicated
The draws below stay inside these ranges and needn't reach their ends.
Inputs may be any that keep to these rules, and one draw needn't show every extreme that they name: `seq_lengths`: each row holds the lengths of the 3 sequences of one group, laid end to end from the group's position 0; a row sums to 4096. `time_bucket`: within each group the values never fall as the position pos(r) rises; position 0 has 0 and position 4095 has 28665.
All inputs are finite; a program needn't handle non-finite values. No bound on the sum of `block_mask` on one device may be relied on, other than what follows from the above.
Results may differ from the reference program's by a relative error of at most 0.009.
Values may be sent and summed in bfloat16 or wider, within the bound.
No kernel may reach another device: no remote copies, remote signals or barrier semaphores. Data moves between devices by JAX's collectives and lax.ppermute only.
A program may use at most 128 MiB of HBM per device.

```python
import math
import jax
import jax.numpy as jnp
import numpy as np
from jax import lax

D = 1024
HEADS = 4
NB = 12
TILE = 128
SEQS = 3
TOK = 256
HA = 512
GROUPS = 8
GROUP_TOK = 4096
TOKENS = 32768
NT = 32
LONGEST = 2048
N_CTX = 16


def draw_time_bucket(key, part):
    key = jax.random.fold_in(key, 11)
    increments = jax.random.randint(key, (GROUPS, GROUP_TOK), 0, 8)
    positions = jnp.arange(GROUP_TOK)[None, :]
    increments = jnp.where(positions > 0, increments, 0)
    running = jnp.cumsum(increments, axis=1)
    running = jnp.where(positions == GROUP_TOK - 1, 7 * (GROUP_TOK - 1), running)
    rows = jnp.arange(GROUP_TOK)
    half_rows = TOK // 2
    device_id = rows // TOK
    within = rows % TOK
    dev_count = GROUP_TOK // TOK
    place = jnp.where(within < half_rows, device_id * half_rows + within, (2 * dev_count - 1 - device_id) * half_rows + within - half_rows)
    laid = running[:, place]
    return laid.reshape(GROUPS * GROUP_TOK).astype(jnp.int32)


def plant(entries, rng, least, top_value):
    extent = entries.shape
    index_at = [jax.random.randint(jax.random.fold_in(rng, axis), (), 0, extent[axis]) for axis in range(len(extent))]
    entries = entries.at[tuple(index_at)].set(least)
    longest = extent.index(max(extent))
    index_at[longest] = (index_at[longest] + 1) % extent[longest]
    return entries.at[tuple(index_at)].set(top_value)


def levels(own_key, shape, shards, smallest, high):
    factor_of = 1.0
    for dim, blocks in shards:
        heights = jax.random.uniform(jax.random.fold_in(jax.random.fold_in(own_key, 6), dim), (blocks,), jnp.float32, smallest / len(shards), high / len(shards))
        factor_of = factor_of * jnp.repeat(jnp.exp(heights), shape[dim] // blocks).reshape((-1,) + (1,) * (len(shape) - 1 - dim))
    return factor_of


def length_profile(number_of, total, limit, skew):
    portions = [(1 << 20) // math.isqrt(rank ** skew) + 1 for rank in range(2, number_of + 1)]
    spare, holding = total - limit - (number_of - 1), [1] * (number_of - 1)
    while spare > 0:
        free = [i for i in range(number_of - 1) if holding[i] < limit]
        mass, left = sum([portions[i] for i in free]), spare
        for i in free:
            addition = min(limit - holding[i], max(1, left * portions[i] // mass), spare)
            holding[i] = holding[i] + addition
            spare = spare - addition
    return np.array([limit] + holding)


def uneven(own_key, number_of, total, reach, slope):
    if number_of == 2:
        one = jax.random.randint(own_key, (), max(1, total - reach), min(reach, total - 1) + 1)
        return jnp.stack([one, total - one])
    sizes = jnp.asarray(length_profile(number_of, total, reach, slope), jnp.int32)
    twos = (number_of - 1) // 2
    giver, sink = sizes[1:1 + 2 * twos:2], sizes[2:2 + 2 * twos:2]
    margin = jnp.minimum(giver - 1, reach - sink)
    moved = jax.random.randint(jax.random.fold_in(own_key, 1), (twos,), 0, 1 << 20) % (margin + 1)
    sizes = sizes.at[1:1 + 2 * twos:2].set(giver - moved).at[2:2 + 2 * twos:2].set(sink + moved)
    return sizes[jax.random.permutation(jax.random.fold_in(own_key, 2), number_of)]


def gaussian(own_key, dims, scale, most, pieces=(), kind=jnp.bfloat16):
    values = scale * jax.random.normal(own_key, dims, jnp.float32)
    if pieces:
        values = values * levels(own_key, dims, pieces, -0.22, 0.18)
    return jnp.clip(values, -most, most).astype(kind)


def setup_inputs(seed: int = 0) -> dict:
    key_of = jax.random.split(jax.random.key(seed), 9)
    return {
        "tokens": gaussian(key_of[0], (TOKENS, D), 1.0, 6.0, ((0, 128),)),
        "cotangent": gaussian(key_of[1], (TOKENS, D), 1.0, 6.0, ((0, 128),)),
        "in_proj": gaussian(key_of[2], (D, 4 * HA), D ** -0.5, 0.1875),
        "out_proj": gaussian(key_of[3], (HA, D), HA ** -0.5, 0.25),
        "rab_time": gaussian(key_of[4], (NB, HEADS), 0.5, 3.0, (), jnp.float32),
        "seq_lengths": jax.vmap(lambda own: uneven(own, SEQS, GROUP_TOK, LONGEST, 1))(jax.random.split(key_of[5], GROUPS)).reshape((GROUPS, SEQS)).astype(jnp.int32),
        "block_mask": plant((jax.random.randint(key_of[6], (GROUPS, NT, NT), 0, 4) < 3).astype(jnp.int32), jax.random.fold_in(key_of[6], 1), 0, 1),
        "time_bucket": draw_time_bucket(jax.random.fold_in(key_of[8], 71), 0),
    }


norm_eps = 1e-05

def norm_rows(values):
    centre = lax.optimization_barrier(jnp.mean(values, axis=-1, keepdims=True))
    shifted = values - centre
    spread = lax.optimization_barrier(jnp.mean(shifted * shifted, axis=-1, keepdims=True))
    inverse = lax.rsqrt(spread + norm_eps)
    return (shifted * inverse, inverse)

def norm_back(upstream, normed, inverse):
    first_mean = lax.optimization_barrier(jnp.mean(upstream, axis=-1, keepdims=True))
    second_mean = lax.optimization_barrier(jnp.mean(upstream * normed, axis=-1, keepdims=True))
    return inverse * (upstream - first_mean - normed * second_mean)

def silu_slope(values):
    sigmoid = jax.nn.sigmoid(values)
    return sigmoid * (1.0 + values * (1.0 - sigmoid))

def rounded(values):
    return lax.optimization_barrier(values.astype(jnp.bfloat16)).astype(jnp.float32)

def row_position(rows, dev_rows, dev_count):
    half_rows = dev_rows // 2
    device_id = rows // dev_rows
    within = rows % dev_rows
    early = device_id * half_rows + within
    late = (2 * dev_count - 1 - device_id) * half_rows + within - half_rows
    return jnp.where(within < half_rows, early, late).astype(jnp.int32)

def segment_of(positions, seq_ends):
    return lax.optimization_barrier(jnp.sum((positions[:, None] >= seq_ends[None, :]).astype(jnp.int32), axis=1))

def gap_level(query_time, key_time, bucket_count):
    time_gap = jnp.maximum(query_time[:, None] - key_time[None, :], 0)
    bucket_ids = jnp.zeros(time_gap.shape, jnp.int32)
    for doubling in range(1, bucket_count):
        bucket_ids = bucket_ids + (time_gap + 1 >= 2 ** doubling).astype(jnp.int32)
    return bucket_ids

def block_scores(query, key, times, seq_ends, tile_mask, rab_time, row_start, block_rows, head_count, score_scale):
    group_rows, inner_width = key.shape
    head_width = inner_width // head_count
    key_rows = jnp.arange(group_rows, dtype=jnp.int32)
    query_rows = row_start + jnp.arange(block_rows, dtype=jnp.int32)
    key_pos = row_position(key_rows, TOK, N_CTX)
    query_pos = row_position(query_rows, TOK, N_CTX)
    query_heads = lax.dynamic_slice_in_dim(query, row_start, block_rows, 0).astype(jnp.float32).reshape(block_rows, head_count, head_width)
    key_heads = key.astype(jnp.float32).reshape(group_rows, head_count, head_width)
    query_time = lax.dynamic_slice_in_dim(times, row_start, block_rows, 0)
    bucket_ids = gap_level(query_time, times, rab_time.shape[0])
    bias_terms = jnp.moveaxis(rab_time[bucket_ids], -1, 0)
    scores = jnp.einsum('qhd,khd->hqk', query_heads, key_heads) * score_scale + bias_terms
    key_seg = segment_of(key_pos, seq_ends)
    query_seg = segment_of(query_pos, seq_ends)
    tiles = tile_mask[query_rows // TILE][:, key_rows // TILE]
    allowed = (key_pos[None, :] <= query_pos[:, None]) & (key_seg[None, :] == query_seg[:, None]) & (tiles > 0)
    return (query_heads, key_heads, scores, allowed.astype(jnp.float32), bucket_ids)

def group_forward(group_args, rab_time, head_count, score_scale):
    query, key, value, times, lengths, tile_mask = group_args
    seq_ends = jnp.cumsum(lengths, dtype=jnp.int32)
    group_rows, inner_width = key.shape
    block_rows = math.gcd(group_rows, 512)
    value_heads = value.astype(jnp.float32).reshape(group_rows, head_count, inner_width // head_count)

    def one_block(block_id):
        row_start = block_id * block_rows
        parts = block_scores(query, key, times, seq_ends, tile_mask, rab_time, row_start, block_rows, head_count, score_scale)
        scores, keep_mask = (parts[2], parts[3])
        weights = rounded(jax.nn.silu(scores) * keep_mask[None])
        return jnp.einsum('hqk,khd->qhd', weights, value_heads).reshape(block_rows, inner_width)
    blocks = lax.map(one_block, jnp.arange(group_rows // block_rows, dtype=jnp.int32))
    return blocks.reshape(group_rows, inner_width)

def group_backward(group_args, rab_time, head_count, score_scale):
    query, key, value, grad_attn, times, lengths, tile_mask = group_args
    seq_ends = jnp.cumsum(lengths, dtype=jnp.int32)
    group_rows, inner_width = key.shape
    head_width = inner_width // head_count
    block_rows = math.gcd(group_rows, 512)
    value_heads = value.astype(jnp.float32).reshape(group_rows, head_count, head_width)

    def one_block(running, block_id):
        key_sum, value_sum, rab_sum = running
        row_start = block_id * block_rows
        query_heads, key_heads, scores, keep_mask, bucket_ids = block_scores(query, key, times, seq_ends, tile_mask, rab_time, row_start, block_rows, head_count, score_scale)
        grad_heads = lax.dynamic_slice_in_dim(grad_attn, row_start, block_rows, 0).astype(jnp.float32).reshape(block_rows, head_count, head_width)
        weights = rounded(jax.nn.silu(scores) * keep_mask[None])
        d_weight = jnp.einsum('qhd,khd->hqk', grad_heads, value_heads)
        d_score = d_weight * keep_mask[None] * silu_slope(scores)
        rab_part = jax.ops.segment_sum(jnp.moveaxis(d_score, 0, -1).reshape(-1, head_count), bucket_ids.reshape(-1), num_segments=rab_time.shape[0])
        score_half = rounded(d_score)
        grad_query = jnp.einsum('hqk,khd->qhd', score_half, key_heads)
        grad_key = jnp.einsum('hqk,qhd->khd', score_half, query_heads)
        grad_value = jnp.einsum('hqk,qhd->khd', weights, grad_heads)
        updated = (key_sum + grad_key.reshape(group_rows, inner_width), value_sum + grad_value.reshape(group_rows, inner_width), rab_sum + rab_part)
        return (updated, grad_query.reshape(block_rows, inner_width))
    start_totals = (jnp.zeros((group_rows, inner_width), jnp.float32), jnp.zeros((group_rows, inner_width), jnp.float32), jnp.zeros(rab_time.shape, jnp.float32))
    totals, query_blocks = lax.scan(one_block, start_totals, jnp.arange(group_rows // block_rows, dtype=jnp.int32))
    return (query_blocks.reshape(group_rows, inner_width), totals[0], totals[1], totals[2])

def reference(tokens, cotangent, in_proj, out_proj, rab_time, seq_lengths, block_mask, time_bucket):
    inner_width = out_proj.shape[0]
    head_count = rab_time.shape[1]
    score_scale = 1.0 / math.sqrt(inner_width // head_count)
    group_count = seq_lengths.shape[0]
    group_rows = tokens.shape[0] // group_count

    def grouped(values):
        return values.reshape((group_count, group_rows) + values.shape[1:])
    token_wide = tokens.astype(jnp.float32)
    normed, inverse_x = norm_rows(token_wide)
    pre_act = jnp.dot(normed.astype(jnp.bfloat16), in_proj, preferred_element_type=jnp.float32)
    activated = jax.nn.silu(pre_act).astype(jnp.bfloat16)
    gate_u = activated[:, :inner_width]
    value_act = activated[:, inner_width:2 * inner_width]
    query_act = activated[:, 2 * inner_width:3 * inner_width]
    key_act = activated[:, 3 * inner_width:]
    attention = lax.map(lambda group_args: group_forward(group_args, rab_time, head_count, score_scale), (grouped(query_act), grouped(key_act), grouped(value_act), grouped(time_bucket), seq_lengths, block_mask)).reshape(-1, inner_width)
    attn_norm, inverse_a = norm_rows(attention)
    mixed = (attn_norm * gate_u.astype(jnp.float32)).astype(jnp.bfloat16)
    output = (token_wide + jnp.dot(mixed, out_proj, preferred_element_type=jnp.float32)).astype(jnp.bfloat16)
    proj_grad = jnp.dot(mixed.T, cotangent, preferred_element_type=jnp.float32)
    grad_mix = jnp.dot(cotangent, out_proj.T, preferred_element_type=jnp.float32)
    grad_gate = grad_mix * attn_norm
    grad_attn = norm_back(grad_mix * gate_u.astype(jnp.float32), attn_norm, inverse_a).astype(jnp.bfloat16)
    query_sum, key_sum, value_sum, rab_sums = lax.map(lambda group_args: group_backward(group_args, rab_time, head_count, score_scale), (grouped(query_act), grouped(key_act), grouped(value_act), grouped(grad_attn), grouped(time_bucket), seq_lengths, block_mask))
    rab_grad = lax.optimization_barrier(jnp.sum(rab_sums, axis=0))
    grad_act = jnp.concatenate([grad_gate, value_sum.reshape(-1, inner_width), query_sum.reshape(-1, inner_width) * score_scale, key_sum.reshape(-1, inner_width) * score_scale], axis=1)
    grad_pre = (grad_act * silu_slope(pre_act)).astype(jnp.bfloat16)
    grad_normed = jnp.dot(grad_pre, in_proj.T, preferred_element_type=jnp.float32)
    grad_in = (cotangent.astype(jnp.float32) + norm_back(grad_normed, normed, inverse_x)).astype(jnp.bfloat16)
    return (output, grad_in, proj_grad, rab_grad)
```

```python
import math

import jax
import jax.numpy as jnp
from jax import lax
from jax.experimental import pallas as pl
from jax.experimental.pallas import tpu as pltpu
from jax.sharding import PartitionSpec as P

f32 = jnp.float32
bf16 = jnp.bfloat16
i32 = jnp.int32
T = 128
EPS = 1e-05
HEADS = 4
BUCKETS = 12
DEVS = 16
TILES = 32
QT = 8
SCALE = 1.0 / math.sqrt(128.0)
LIST = 160
UNROLL = 2
VMEM = pl.BlockSpec(memory_space=pltpu.VMEM)
SMEM = pl.BlockSpec(memory_space=pltpu.SMEM)
NT_DIMS = (((1,), (1,)), ((), ()))
TN_DIMS = (((0,), (0,)), ((), ()))


def params(mib=56):
    return pltpu.CompilerParams(vmem_limit_bytes=mib * 1024 * 1024)


def cost(flops, size):
    return pl.CostEstimate(flops=int(flops), bytes_accessed=int(size), transcendentals=0)


def sds(shape, dtype):
    return jax.ShapeDtypeStruct(shape, dtype)


def norm_rows(values):
    centre = jnp.mean(values, axis=-1, keepdims=True)
    shifted = values - centre
    spread = jnp.mean(shifted * shifted, axis=-1, keepdims=True)
    inverse = lax.rsqrt(spread + EPS)
    return shifted * inverse, inverse


def norm_back(upstream, normed, inverse):
    first = jnp.mean(upstream, axis=-1, keepdims=True)
    second = jnp.mean(upstream * normed, axis=-1, keepdims=True)
    return inverse * (upstream - first - normed * second)


def project_kernel(ids, tokens, w_gate, w_value, w_query, w_key, gate, slope, *rest):
    outs, normed = rest[:8], rest[8]
    step = pl.program_id(0)

    @pl.when(step == 0)
    def _():
        normed[...] = norm_rows(tokens[...].astype(f32))[0].astype(bf16)

    weights = jnp.concatenate([w_gate[...], w_value[...], w_query[...], w_key[...]], axis=1)
    pre = jnp.dot(normed[...], weights, preferred_element_type=f32)
    sig = 0.5 * jnp.tanh(0.5 * pre) + 0.5
    act = (pre * sig).astype(bf16)
    slopes = (sig * (1.0 + pre * (1.0 - sig))).astype(bf16)
    for kind in range(4):
        slope[kind, 0] = slopes[:, kind * T : (kind + 1) * T]
    gate[0] = act[:, :T]
    value, query, key = act[:, T : 2 * T], act[:, 2 * T : 3 * T], act[:, 3 * T :]
    for which in range(4):

        @pl.when(step == which)
        def _(which=which):
            outs[which][:, 0:T] = key
            outs[which][:, T : 2 * T] = value
            outs[which][:, 2 * T :] = query
            outs[4 + which][:, 0:T] = key
            outs[4 + which][:, T : 2 * T] = value


def project(ids, tokens, in_proj):
    def column(kind):
        return pl.BlockSpec((1024, T), lambda s, ids: (0, kind * HEADS + (ids[1] + s) % HEADS))

    whole = lambda shape: pl.BlockSpec(shape, lambda s, ids: (0,) * len(shape))
    head_of = lambda s, ids: (ids[1] + s) % HEADS
    return pl.pallas_call(
        project_kernel,
        grid_spec=pltpu.PrefetchScalarGridSpec(
            num_scalar_prefetch=1,
            grid=(4,),
            in_specs=[whole((256, 1024))] + [column(kind) for kind in range(4)],
            out_specs=[
                pl.BlockSpec((1, 256, T), lambda s, ids: (head_of(s, ids), 0, 0)),
                pl.BlockSpec((4, 1, 256, T), lambda s, ids: (0, head_of(s, ids), 0, 0)),
            ]
            + [whole((256, 384))] * 4
            + [whole((256, 256))] * 4,
            scratch_shapes=[pltpu.VMEM((256, 1024), bf16)],
        ),
        out_shape=[sds((4, 256, T), bf16), sds((4, 4, 256, T), bf16)]
        + [sds((256, 384), bf16)] * 4
        + [sds((256, 256), bf16)] * 4,
        compiler_params=params(),
        cost_estimate=cost(2 * 256 * 1024 * 2048, 7 << 20),
        name="project",
    )(ids, tokens, in_proj, in_proj, in_proj, in_proj)


def list_kernel(ids, meta, lengths, far, near, counts):
    y, z, core = ids[0], ids[1], ids[2]
    end0 = lengths[0]
    end1 = lengths[0] + lengths[1]

    def start_of(pos):
        return jnp.where(pos >= end1, end1, jnp.where(pos >= end0, end0, 0))

    def time_at(tile, lane):
        first = tile < DEVS
        dev = jnp.where(first, tile, 2 * DEVS - 1 - tile)
        return meta[dev * 384 + jnp.where(first, 0, T) + lane]

    def level(gap):
        total = jnp.int32(0)
        for j in range(1, BUCKETS):
            total = total + jnp.where(gap + 1 >= 2**j, 1, 0).astype(i32)
        return total

    counts[0] = 0
    counts[1] = 0

    def query_step(jj, _):
        dev = y * 8 + (jj // 2) * 2 + core
        half = jj % 2
        tile = jnp.where(half == 0, dev, 2 * DEVS - 1 - dev)
        low = start_of(tile * T)
        high = start_of(tile * T + T - 1)
        q_first = time_at(tile, 0)
        q_last = time_at(tile, T - 1)
        base = dev * 384 + 256 + half * TILES

        def key_step(k, _):
            row_tile = jnp.where(k < DEVS, 2 * k, 2 * (2 * DEVS - 1 - k) + 1)

            @pl.when(meta[base + row_tile] != 0)
            def _():
                bottom = level(jnp.maximum(q_first - time_at(k, T - 1), 0))
                top = level(q_last - time_at(k, 0))
                entry = jj + 16 * k
                plain = (k < tile) & (k * T >= high) & (top - bottom <= 2)

                @pl.when(plain)
                def _():
                    n = counts[0]
                    far[n] = entry + 1024 * bottom
                    counts[0] = n + 1

                @pl.when(jnp.logical_not(plain))
                def _():
                    n = counts[1]
                    near[n] = entry
                    counts[1] = n + 1

            return 0

        lax.fori_loop(low // T, tile + 1, key_step, 0)
        return 0

    lax.fori_loop(0, QT, query_step, 0)
    for index, ref in ((0, far), (1, near)):
        for pad in range(UNROLL - 1):
            ref[counts[index] + pad] = QT + 16 * TILES
        counts[index] = (counts[index] + UNROLL - 1) // UNROLL


def make_lists(ids, meta, lengths):
    return pl.pallas_call(
        list_kernel,
        in_specs=[SMEM] * 3,
        out_specs=[SMEM] * 3,
        out_shape=[sds((LIST,), i32), sds((LIST,), i32), sds((8,), i32)],
        cost_estimate=cost(1 << 20, 1 << 20),
        name="pair_lists",
    )(ids, meta, lengths)


def bias_far(gap, table, bottom):
    first = table[bottom]
    second = table[bottom + 1]
    third = table[bottom + 2]
    limit1 = table[16 + bottom + 1]
    limit2 = table[16 + bottom + 2]
    over1 = gap >= limit1
    over2 = gap >= limit2
    return jnp.where(over2, third, jnp.where(over1, second, first)), over1, over2


def bias_near(gap, table):
    bias = jnp.full(gap.shape, table[0], f32)
    for j in range(1, BUCKETS):
        bias = jnp.where(gap >= float(2**j - 1), table[j], bias)
    return bias


def keep_near(ids, start, jj, k):
    dev = ids[0] * 8 + (jj // 2) * 2 + ids[2]
    tile = jnp.where(jj % 2 == 0, dev, 2 * DEVS - 1 - dev)
    row = lax.broadcasted_iota(i32, (T, T), 0)
    col = lax.broadcasted_iota(i32, (T, T), 1)
    later = (col - row) <= (tile - k) * T
    return later & ((col + k * T) >= start)


def forward_kernel(ids, table, far, near, counts, lengths, times, *refs):
    ins, outs = refs[:16], refs[16:]
    o_refs, (keys, values, queries, tq, tk, start, acc) = outs[:4], outs[4:]
    y, z, core = ids[0], ids[1], ids[2]
    end0 = lengths[0]
    end1 = lengths[0] + lengths[1]
    for group in range(4):
        for t in range(4):
            ref = ins[group * 4 + t]
            zz = (z + 4 - t) % 4
            dev = (y if group < 2 else 1 - y) * 8 + zz * 2 + (core if group % 2 == 0 else 1 - core)
            keys[dev] = ref[0:T, 0:T]
            values[dev] = ref[0:T, T : 2 * T]
            keys[2 * DEVS - 1 - dev] = ref[T:, 0:T]
            values[2 * DEVS - 1 - dev] = ref[T:, T : 2 * T]
            if group == 0:
                queries[2 * zz] = ref[0:T, 2 * T :]
                queries[2 * zz + 1] = ref[T:, 2 * T :]
    keys[TILES] = jnp.zeros((T, T), bf16)
    values[TILES] = jnp.zeros((T, T), bf16)
    queries[QT] = jnp.zeros((T, T), bf16)
    for dev in range(DEVS):
        tk[dev] = jnp.broadcast_to(times[dev : dev + 1, 0:T].astype(f32), (8, T))
        tk[2 * DEVS - 1 - dev] = jnp.broadcast_to(times[dev : dev + 1, T : 2 * T].astype(f32), (8, T))
    tk[TILES] = jnp.zeros((8, T), f32)
    tq[QT] = jnp.zeros((T, T), f32)
    start[QT] = jnp.zeros((T, T), i32)
    rows = lax.broadcasted_iota(i32, (T, T), 0)
    for jj in range(QT):
        dev = y * 8 + (jj // 2) * 2 + core
        tile = dev if jj % 2 == 0 else 2 * DEVS - 1 - dev
        tq[jj] = jnp.transpose(jnp.broadcast_to(tk[tile][0:1, :], (T, T)))
        pos = rows + tile * T
        start[jj] = jnp.where(pos >= end1, end1, jnp.where(pos >= end0, end0, 0))
    acc[...] = jnp.zeros(acc.shape, f32)

    def far_step(i, _):
        for u in range(UNROLL):
            entry = far[i * UNROLL + u]
            jj = entry % 16
            k = (entry // 16) % 64
            dots = lax.dot_general(queries[jj], keys[k], NT_DIMS, preferred_element_type=f32)
            gap = tq[jj] - tk[k][0:1, :]
            bias, _, _ = bias_far(gap, table, entry // 1024)
            half = dots * (0.5 * SCALE) + bias
            weight = (half * jnp.tanh(half) + half).astype(bf16)
            acc[jj] += jnp.dot(weight, values[k], preferred_element_type=f32)
        return 0

    def near_step(i, _):
        for u in range(UNROLL):
            entry = near[i * UNROLL + u]
            jj = entry % 16
            k = entry // 16
            dots = lax.dot_general(queries[jj], keys[k], NT_DIMS, preferred_element_type=f32)
            gap = tq[jj] - tk[k][0:1, :]
            half = dots * (0.5 * SCALE) + bias_near(gap, table)
            weight = half * jnp.tanh(half) + half
            weight = jnp.where(keep_near(ids, start[jj], jj, k), weight, 0.0).astype(bf16)
            acc[jj] += jnp.dot(weight, values[k], preferred_element_type=f32)
        return 0

    lax.fori_loop(0, counts[0], far_step, 0)
    lax.fori_loop(0, counts[1], near_step, 0)
    for s in range(4):
        zz = (z + s) % 4
        o_refs[s][0:T] = acc[2 * zz]
        o_refs[s][T:] = acc[2 * zz + 1]


def attend(ids, table, far, near, counts, lengths, times, parts):
    return pl.pallas_call(
        forward_kernel,
        in_specs=[SMEM] * 6 + [VMEM] * 17,
        out_specs=[VMEM] * 10,
        out_shape=[sds((256, T), f32)] * 4
        + [
            sds((TILES + 1, T, T), bf16),
            sds((TILES + 1, T, T), bf16),
            sds((QT + 1, T, T), bf16),
            sds((QT + 1, T, T), f32),
            sds((TILES + 1, 8, T), f32),
            sds((QT + 1, T, T), i32),
        ],
        scratch_shapes=[pltpu.VMEM((QT + 1, T, T), f32)],
        compiler_params=params(),
        cost_estimate=cost(1e9 * 6, 6 << 20),
        name="attend",
    )(ids, table, far, near, counts, lengths, times, *parts)


def middle_kernel(ids, cot, out_proj, gate, slope, *refs):
    ins, (mixed, grad_gate), g_refs = refs[:4], refs[4:6], refs[6:10]
    att, back = refs[10], refs[11]
    z = ids[1]
    for t in range(4):
        att[(z + 4 - t) % 4] = ins[t][...]
    whole = jnp.concatenate([att[h] for h in range(4)], axis=1)
    normed, inverse = norm_rows(whole)
    gates = jnp.concatenate([gate[h] for h in range(4)], axis=1).astype(f32)
    mixed[...] = (normed * gates).astype(bf16)
    grad_mix = lax.dot_general(cot[...], out_proj[...], NT_DIMS, preferred_element_type=f32)
    gate_slope = jnp.concatenate([slope[h] for h in range(4)], axis=1).astype(f32)
    grad_gate[...] = (grad_mix * normed * gate_slope).astype(bf16)
    grad = norm_back(grad_mix * gates, normed, inverse).astype(bf16)
    for h in range(4):
        back[h] = grad[:, h * T : (h + 1) * T]
    for s in range(4):
        g_refs[s][...] = back[(z + s) % 4]


def middle(ids, cot, out_proj, gate, slope, parts):
    return pl.pallas_call(
        middle_kernel,
        grid=(1,),
        in_specs=[
            SMEM,
            pl.BlockSpec((256, 1024), lambda i: (0, 0)),
            pl.BlockSpec((512, 1024), lambda i: (0, 0)),
            pl.BlockSpec((4, 256, T), lambda i: (0, 0, 0)),
            pl.BlockSpec((None, 4, 256, T), lambda i: (0, 0, 0, 0)),
        ]
        + [pl.BlockSpec((256, T), lambda i: (0, 0))] * 4,
        out_specs=[pl.BlockSpec((256, 512), lambda i: (0, 0))] * 2
        + [pl.BlockSpec((256, T), lambda i: (0, 0))] * 4,
        out_shape=[sds((256, 512), bf16)] * 2 + [sds((256, T), bf16)] * 4,
        scratch_shapes=[pltpu.VMEM((4, 256, T), f32), pltpu.VMEM((4, 256, T), bf16)],
        compiler_params=params(),
        cost_estimate=cost(2 * 256 * 512 * 1024, 4 << 20),
        name="middle",
    )(ids, cot, out_proj, gate, slope, *parts)


def output_kernel(ids, tokens, cot, out_proj, mixed, output, mine, theirs):
    y, z, core, dp = ids[0], ids[1], ids[2], ids[3]
    output[...] = (
        tokens[...].astype(f32) + jnp.dot(mixed[...], out_proj[...], preferred_element_type=f32)
    ).astype(bf16)
    r = lax.broadcasted_iota(i32, (512, 512), 1)
    c = lax.broadcasted_iota(i32, (512, 512), 0)
    r_core = (r // 256) ^ core
    r_z = (((r // 64) % 4) + z) % 4
    r_y = ((r // 32) % 2) ^ y
    r_dp = ((r // 4) % 8) ^ dp
    source = r_dp * 64 + r_y * 32 + r_z * 8 + r_core * 4 + r % 4
    pick = jnp.where(c == source, 1.0, 0.0).astype(bf16)
    moved = jnp.dot(mixed[...], pick, preferred_element_type=f32).astype(bf16)
    part = lax.dot_general(moved, cot[...], TN_DIMS, preferred_element_type=f32)
    mine[...] = part[:256]
    theirs[...] = part[256:].astype(bf16)


def finish_output(ids, tokens, cot, out_proj, mixed):
    return pl.pallas_call(
        output_kernel,
        in_specs=[SMEM] + [VMEM] * 4,
        out_specs=[VMEM] * 3,
        out_shape=[sds((256, 1024), bf16), sds((256, 1024), f32), sds((256, 1024), bf16)],
        compiler_params=params(),
        cost_estimate=cost(6 * 256 * 512 * 1024, 5 << 20),
        name="finish_output",
    )(ids, tokens, cot, out_proj, mixed)


def backward_kernel(ids, table, far, near, counts, keys, values, queries, tq, tk, start, *refs):
    ins, outs = refs[:4], refs[4:10]
    mine_s, mine_o, theirs_s, theirs_o, dq_out, rab_out = outs
    grads, grads_t, queries_t, dq, dkt, dvt, rab = refs[10:]
    y, z, core = ids[0], ids[1], ids[2]
    for t in range(4):
        zz = (z + 4 - t) % 4
        for half in range(2):
            block = ins[t][half * T : (half + 1) * T, :].astype(f32) * 0.5
            grads[2 * zz + half] = block.astype(bf16)
            grads_t[2 * zz + half] = jnp.transpose(block).astype(bf16)
    for jj in range(QT):
        queries_t[jj] = jnp.transpose(queries[jj].astype(f32)).astype(bf16)
    grads[QT] = jnp.zeros((T, T), bf16)
    grads_t[QT] = jnp.zeros((T, T), bf16)
    queries_t[QT] = jnp.zeros((T, T), bf16)
    dq[...] = jnp.zeros(dq.shape, f32)
    dkt[...] = jnp.zeros(dkt.shape, f32)
    dvt[...] = jnp.zeros(dvt.shape, f32)
    rab[...] = jnp.zeros(rab.shape, f32)

    def fold(values_):
        return jnp.sum(values_.reshape(T // 8, 8, T), axis=0)

    def pair(jj, k, half, keep):
        t = jnp.tanh(half)
        weight = half * t + half
        d_weight = lax.dot_general(grads[jj], values[k], NT_DIMS, preferred_element_type=f32)
        d_score = d_weight * ((1.0 + t) * (1.0 + half * (1.0 - t)))
        if keep is not None:
            weight = jnp.where(keep, weight, 0.0)
            d_score = jnp.where(keep, d_score, 0.0)
        score_half = d_score.astype(bf16)
        dq[jj] += jnp.dot(score_half, keys[k], preferred_element_type=f32)
        dkt[k] += jnp.dot(queries_t[jj], score_half, preferred_element_type=f32)
        dvt[k] += jnp.dot(grads_t[jj], weight.astype(bf16), preferred_element_type=f32)
        return d_score

    def far_step(i, _):
        for u in range(UNROLL):
            entry = far[i * UNROLL + u]
            jj = entry % 16
            k = (entry // 16) % 64
            bottom = entry // 1024
            dots = lax.dot_general(queries[jj], keys[k], NT_DIMS, preferred_element_type=f32)
            gap = tq[jj] - tk[k][0:1, :]
            bias, over1, over2 = bias_far(gap, table, bottom)
            d_score = pair(jj, k, dots * (0.5 * SCALE) + bias, None)
            sum0 = fold(d_score)
            sum1 = fold(jnp.where(over1, d_score, 0.0))
            sum2 = fold(jnp.where(over2, d_score, 0.0))
            rab[bottom] += sum0 - sum1
            rab[bottom + 1] += sum1 - sum2
            rab[bottom + 2] += sum2
        return 0

    def near_step(i, _):
        for u in range(UNROLL):
            entry = near[i * UNROLL + u]
            jj = entry % 16
            k = entry // 16
            dots = lax.dot_general(queries[jj], keys[k], NT_DIMS, preferred_element_type=f32)
            gap = tq[jj] - tk[k][0:1, :]
            half = dots * (0.5 * SCALE) + bias_near(gap, table)
            d_score = pair(jj, k, half, keep_near(ids, start[jj], jj, k))
            last = fold(d_score)
            for j in range(1, BUCKETS):
                now = fold(jnp.where(gap >= float(2**j - 1), d_score, 0.0))
                rab[j - 1] += last - now
                last = now
            rab[BUCKETS - 1] += last
        return 0

    lax.fori_loop(0, counts[0], far_step, 0)
    lax.fori_loop(0, counts[1], near_step, 0)
    for other in range(2):
        for s in range(4):
            base = (y if other == 0 else 1 - y) * 8 + ((z + s) % 4) * 2
            for side in range(2):
                dev = base + (core if side == 0 else 1 - core)
                ref = ((mine_s, theirs_s), (mine_o, theirs_o))[other][side]
                for half in range(2):
                    tile = dev if half == 0 else 2 * DEVS - 1 - dev
                    ref[s, 0:T, half * T : (half + 1) * T] = (dkt[tile] * SCALE).astype(bf16)
                    ref[s, T:, half * T : (half + 1) * T] = (dvt[tile] * 2.0).astype(bf16)
    for s in range(4):
        zz = (z + s) % 4
        for half in range(2):
            dq_out[s, :, half * T : (half + 1) * T] = (dq[2 * zz + half] * SCALE).astype(bf16)
    for b in range(16):
        if b < BUCKETS:
            rab_out[b : b + 1, :] = jnp.sum(rab[b], axis=0, keepdims=True)
        else:
            rab_out[b : b + 1, :] = jnp.zeros((1, T), f32)


def attend_back(ids, table, far, near, counts, saved, parts):
    return pl.pallas_call(
        backward_kernel,
        in_specs=[SMEM] * 5 + [VMEM] * 10,
        out_specs=[VMEM] * 6,
        out_shape=[sds((4, 256, 256), bf16)] * 4 + [sds((4, T, 256), bf16), sds((16, T), f32)],
        scratch_shapes=[
            pltpu.VMEM((QT + 1, T, T), bf16),
            pltpu.VMEM((QT + 1, T, T), bf16),
            pltpu.VMEM((QT + 1, T, T), bf16),
            pltpu.VMEM((QT + 1, T, T), f32),
            pltpu.VMEM((TILES + 1, T, T), f32),
            pltpu.VMEM((TILES + 1, T, T), f32),
            pltpu.VMEM((16, 8, T), f32),
        ],
        compiler_params=params(),
        cost_estimate=cost(1e9 * 12, 8 << 20),
        name="attend_back",
    )(ids, table, far, near, counts, *saved, *parts)


def combine_kernel(mine_s, mine_o, got_s, got_o, dq, *outs):
    for s in range(4):
        outs[s][0:256, :] = (mine_s[s].astype(f32) + got_s[s].astype(f32)).astype(bf16)
        outs[s][256:, :] = dq[s]
        outs[4 + s][...] = (mine_o[s].astype(f32) + got_o[s].astype(f32)).astype(bf16)


def combine(mine_s, mine_o, got_s, got_o, dq):
    return pl.pallas_call(
        combine_kernel,
        in_specs=[VMEM] * 5,
        out_specs=[VMEM] * 8,
        out_shape=[sds((384, 256), bf16)] * 4 + [sds((256, 256), bf16)] * 4,
        compiler_params=params(),
        cost_estimate=cost(1 << 20, 5 << 20),
        name="combine",
    )(mine_s, mine_o, got_s, got_o, dq)


def final_kernel(ids, tokens, cot, in_proj, slope, grad_gate, *refs):
    same, other, grad_in, grad_pre, grad_normed = refs[:4], refs[4:8], refs[8], refs[9], refs[10]
    step = pl.program_id(0)
    z = ids[1]

    @pl.when(step == 0)
    def _():
        grad_pre[:, 0:512] = grad_gate[...]
        for t in range(4):
            head = (z + 4 - t) % 4
            column = lambda kind: pl.ds(pl.multiple_of(kind * 512 + head * T, T), T)
            total = same[t][0:256, :].astype(f32) + other[t][...].astype(f32)
            for half in range(2):
                rows = slice(half * T, (half + 1) * T)
                key = jnp.transpose(total[0:T, rows])
                value = jnp.transpose(total[T:, rows])
                query = same[t][256:, rows].astype(f32)
                for kind, part in ((1, value), (2, query), (3, key)):
                    grad_pre[rows, column(kind)] = (
                        part * slope[kind, head, rows, :].astype(f32)
                    ).astype(bf16)

    grad_normed[step] = lax.dot_general(
        grad_pre[...], in_proj[...], NT_DIMS, preferred_element_type=f32
    )

    @pl.when(step == 3)
    def _():
        normed, inverse = norm_rows(tokens[...].astype(f32))
        upstream = jnp.concatenate([grad_normed[i] for i in range(4)], axis=1)
        grad_in[...] = (cot[...].astype(f32) + norm_back(upstream, normed, inverse)).astype(bf16)


def finish_grad(ids, tokens, cot, in_proj, slope, grad_gate, same, other):
    whole = lambda shape: pl.BlockSpec(shape, lambda s: (0,) * len(shape))
    return pl.pallas_call(
        final_kernel,
        grid=(4,),
        in_specs=[
            SMEM,
            whole((256, 1024)),
            whole((256, 1024)),
            pl.BlockSpec((256, 2048), lambda s: (s, 0)),
            whole((4, 4, 256, T)),
            whole((256, 512)),
        ]
        + [whole((384, 256))] * 4
        + [whole((256, 256))] * 4,
        out_specs=whole((256, 1024)),
        out_shape=sds((256, 1024), bf16),
        scratch_shapes=[pltpu.VMEM((256, 2048), bf16), pltpu.VMEM((4, 256, 256), f32)],
        compiler_params=params(),
        cost_estimate=cost(2 * 256 * 1024 * 2048, 8 << 20),
        name="finish_grad",
    )(ids, tokens, cot, in_proj, slope, grad_gate, *same, *other)


def move(y_xor, z_shift, core_xor):
    pairs = []
    for dev in range(DEVS):
        y, z, core = dev // 8, (dev // 2) % 4, dev % 2
        target = (y ^ y_xor) * 8 + ((z + z_shift) % 4) * 2 + (core ^ core_xor)
        pairs.append((dev, target))
    return pairs


def send(x, y_xor, z_shift, core_xor):
    return lax.ppermute(x, "ctx", move(y_xor, z_shift, core_xor))


def send_dp(x, mask):
    return lax.ppermute(x, "dp", [(dev, dev ^ mask) for dev in range(8)])


def gather_meta(payload, y, z, core):
    other = send(payload, 0, 0, 1)
    pair = jnp.where(core == 0, jnp.stack([payload, other]), jnp.stack([other, payload]))
    line = [pair] + [send(pair, 0, s, 0) for s in (1, 2, 3)]
    column = jnp.zeros((4, 2, 384), i32)
    index = jnp.arange(4, dtype=i32)[:, None, None]
    for t in range(4):
        column = column + jnp.where(index == (z + 4 - t) % 4, line[t][None], 0)
    column = column.reshape(8, 384)
    far_side = send(column, 1, 0, 0)
    return jnp.where(
        y == 0,
        jnp.concatenate([column, far_side], axis=0),
        jnp.concatenate([far_side, column], axis=0),
    )


def sum_rab(part, z):
    part = part + send(part, 0, 0, 1)
    terms = [part] + [send_dp(part, mask) for mask in range(1, 8)]
    while len(terms) > 1:
        terms = [terms[i] + terms[i + 1] for i in range(0, len(terms), 2)]
    part = terms[0]
    part = part + send(part, 1, 0, 0)
    line = [part] + [send(part, 0, s, 0) for s in (1, 2, 3)]
    sums = jnp.sum(jnp.stack(line), axis=-1)[:, :BUCKETS]
    slot = (z + 4 - jnp.arange(4, dtype=i32)) % 4
    pick = slot[None, :, None] == jnp.arange(4, dtype=i32)[:, None, None]
    return jnp.sum(jnp.where(pick, sums[None], 0.0), axis=1).T


def sum_proj(mine, theirs):
    total = mine + send(theirs, 0, 0, 1).astype(f32)
    pieces = total.reshape(4, 64, 1024)
    total = pieces[0]
    for s in (1, 2, 3):
        total = total + send(pieces[s].astype(bf16), 0, s, 0).astype(f32)
    pieces = total.reshape(2, 32, 1024)
    total = pieces[0] + send(pieces[1].astype(bf16), 1, 0, 0).astype(f32)
    pieces = total.reshape(8, 4, 1024)
    total = pieces[0]
    for mask in range(1, 8):
        total = total + send_dp(pieces[mask], mask)
    return total


def on_device(tokens, cotangent, in_proj, out_proj, rab_time, seq_lengths, block_mask, time_bucket):
    ctx = lax.axis_index("ctx")
    dp = lax.axis_index("dp")
    y, z, core = ctx // 8, (ctx // 2) % 4, ctx % 2
    ids = jnp.stack([y, z, core, dp]).astype(i32)
    lengths = seq_lengths.reshape(3)
    payload = jnp.concatenate([time_bucket, block_mask.reshape(64), jnp.zeros((64,), i32)])
    meta = gather_meta(payload, y, z, core)
    limits = [2.0**j - 1.0 for j in range(BUCKETS)] + [1e9] * 4
    head_bias = lax.dynamic_slice_in_dim(rab_time, z, 1, 1).reshape(BUCKETS) * 0.5
    table = jnp.concatenate([head_bias, jnp.zeros((4,), f32), jnp.array(limits, f32)])
    far, near, counts = make_lists(ids, meta.reshape(-1), lengths)

    made = project(ids, tokens, in_proj)
    gate, slope, full, pairs = made[0], made[1], made[2:6], made[6:10]
    own = [full[0]] + [send(full[s], 0, s, 0) for s in (1, 2, 3)]
    across = [send(pairs[s], 1, s, 0) for s in range(4)]
    own_twin = [send(part, 0, 0, 1) for part in own]
    across_twin = [send(part, 0, 0, 1) for part in across]
    parts = own + own_twin + across + across_twin
    done = attend(ids, table, far, near, counts, lengths, meta[:, :256], parts)
    blocks, saved = done[:4], done[4:]

    heads = [blocks[0]] + [send(blocks[s], 0, s, 0) for s in (1, 2, 3)]
    between = middle(ids, cotangent, out_proj, gate, slope, heads)
    mixed, grad_gate, grads = between[0], between[1], between[2:]
    grads = [grads[0]] + [send(grads[s], 0, s, 0) for s in (1, 2, 3)]
    output, proj_mine, proj_theirs = finish_output(ids, tokens, cotangent, out_proj, mixed)
    proj_grad = sum_proj(proj_mine, proj_theirs)

    mine_s, mine_o, theirs_s, theirs_o, dq, rab = attend_back(
        ids, table, far, near, counts, saved, grads
    )
    got_o = send(theirs_o, 0, 0, 1)
    got_s = send(theirs_s, 0, 0, 1)
    messages = combine(mine_s, mine_o, got_s, got_o, dq)
    same = [messages[0]] + [send(messages[s], 0, s, 0) for s in (1, 2, 3)]
    other = [send(messages[4 + s], 1, s, 0) for s in range(4)]
    rab_grad = sum_rab(rab, z)
    grad_in = finish_grad(ids, tokens, cotangent, in_proj, slope, grad_gate, same, other)
    return output, grad_in, proj_grad, rab_grad


def solution(mesh):
    rows = P(("dp", "ctx"), None)
    placed = (rows, rows, P(), P(), P(), P("dp", None), P("dp", "ctx", None), P(("dp", "ctx")))
    return jax.shard_map(
        on_device,
        mesh=mesh,
        in_specs=placed,
        out_specs=(rows, rows, rows, P()),
        check_vma=False,
    )
```

```python
import math

import jax
import jax.numpy as jnp
from jax import lax
from jax.experimental import pallas as pl
from jax.experimental.pallas import tpu as pltpu
from jax.sharding import PartitionSpec as P

f32 = jnp.float32
bf16 = jnp.bfloat16
i32 = jnp.int32
T = 128
EPS = 1e-05
HEADS = 4
BUCKETS = 12
DEVS = 16
TILES = 32
QT = 8
SCALE = 1.0 / math.sqrt(128.0)
LIST = 160
FAR_U = 8
NEAR_U = 4
NEAR_FLAG = 32768
DUMMY = QT + 16 * TILES
VMEM = pl.BlockSpec(memory_space=pltpu.VMEM)
SMEM = pl.BlockSpec(memory_space=pltpu.SMEM)
NT_DIMS = (((1,), (1,)), ((), ()))
TN_DIMS = (((0,), (0,)), ((), ()))


def params(mib=56):
    return pltpu.CompilerParams(vmem_limit_bytes=mib * 1024 * 1024)


def cost(flops, size):
    return pl.CostEstimate(flops=int(flops), bytes_accessed=int(size), transcendentals=0)


def sds(shape, dtype):
    return jax.ShapeDtypeStruct(shape, dtype)


def norm_rows(values):
    centre = jnp.mean(values, axis=-1, keepdims=True)
    shifted = values - centre
    spread = jnp.mean(shifted * shifted, axis=-1, keepdims=True)
    inverse = lax.rsqrt(spread + EPS)
    return shifted * inverse, inverse


def norm_back(upstream, normed, inverse):
    first = jnp.mean(upstream, axis=-1, keepdims=True)
    second = jnp.mean(upstream * normed, axis=-1, keepdims=True)
    return inverse * (upstream - first - normed * second)


def project_kernel(ids, tokens, meta, w_gate, w_value, w_query, w_key, gate, slope, *rest):
    outs, normed = rest[:8], rest[8]
    step = pl.program_id(0)

    @pl.when(step == 0)
    def _():
        normed[...] = norm_rows(tokens[...].astype(f32))[0].astype(bf16)

    weights = jnp.concatenate([w_gate[...], w_value[...], w_query[...], w_key[...]], axis=1)
    pre = jnp.dot(normed[...], weights, preferred_element_type=f32)
    sig = 0.5 * jnp.tanh(0.5 * pre) + 0.5
    act = (pre * sig).astype(bf16)
    slopes = (sig * (1.0 + pre * (1.0 - sig))).astype(bf16)
    for kind in range(4):
        slope[kind, 0] = slopes[:, kind * T : (kind + 1) * T]
    gate[0] = act[:, :T]
    value, query, key = act[:, T : 2 * T], act[:, 2 * T : 3 * T], act[:, 3 * T :]
    for which in range(4):

        @pl.when(step == which)
        def _(which=which):
            for ref in (outs[which], outs[4 + which]):
                ref[0:256, 0:T] = key
                ref[0:256, T : 2 * T] = value
                ref[256:, 0:256] = meta[...]
            outs[which][0:256, 2 * T :] = query
            outs[which][256:, 2 * T :] = jnp.zeros((16, T), bf16)


def project(ids, tokens, meta, in_proj):
    def column(kind):
        return pl.BlockSpec((1024, T), lambda s, ids: (0, kind * HEADS + (ids[1] + s) % HEADS))

    whole = lambda shape: pl.BlockSpec(shape, lambda s, ids: (0,) * len(shape))
    head_of = lambda s, ids: (ids[1] + s) % HEADS
    return pl.pallas_call(
        project_kernel,
        grid_spec=pltpu.PrefetchScalarGridSpec(
            num_scalar_prefetch=1,
            grid=(4,),
            in_specs=[whole((256, 1024)), whole((16, 256))] + [column(kind) for kind in range(4)],
            out_specs=[
                pl.BlockSpec((1, 256, T), lambda s, ids: (head_of(s, ids), 0, 0)),
                pl.BlockSpec((4, 1, 256, T), lambda s, ids: (0, head_of(s, ids), 0, 0)),
            ]
            + [whole((272, 384))] * 4
            + [whole((272, 256))] * 4,
            scratch_shapes=[pltpu.VMEM((256, 1024), bf16)],
        ),
        out_shape=[sds((4, 256, T), bf16), sds((4, 4, 256, T), bf16)]
        + [sds((272, 384), bf16)] * 4
        + [sds((272, 256), bf16)] * 4,
        compiler_params=params(),
        cost_estimate=cost(2 * 256 * 1024 * 2048, 7 << 20),
        name="project",
    )(ids, tokens, meta, in_proj, in_proj, in_proj, in_proj)


def bias_far(gap, table, bottom):
    first = table[bottom]
    second = table[bottom + 1]
    third = table[bottom + 2]
    limit1 = table[16 + bottom + 1]
    limit2 = table[16 + bottom + 2]
    over1 = gap >= limit1
    over2 = gap >= limit2
    return jnp.where(over2, third, jnp.where(over1, second, first)), over1, over2


def bias_near(gap, table):
    bias = jnp.full(gap.shape, table[0], f32)
    for j in range(1, BUCKETS):
        bias = jnp.where(gap >= float(2**j - 1), table[j], bias)
    return bias


def keep_near(ids, start, jj, k):
    tile = query_tile(ids, jj)
    row = lax.broadcasted_iota(i32, (T, T), 0)
    col = lax.broadcasted_iota(i32, (T, T), 1)
    later = (col - row) <= (tile - k) * T
    return later & ((col + k * T) >= start)


STAGE = [
    pltpu.VMEM((TILES + 1, T, T), bf16),
    pltpu.VMEM((TILES + 1, T, T), bf16),
    pltpu.VMEM((QT + 1, T, T), bf16),
    pltpu.VMEM((QT + 1, T, T), f32),
    pltpu.VMEM((TILES + 1, 8, T), f32),
    pltpu.VMEM((QT + 1, T, T), i32),
]


def query_tile(ids, jj):
    dev = ids[0] * 8 + (jj // 2) * 2 + ids[2]
    return jnp.where(jj % 2 == 0, dev, 2 * DEVS - 1 - dev)


def starts_of(lengths, pos):
    end0 = lengths[0]
    end1 = lengths[0] + lengths[1]
    return jnp.where(pos >= end1, end1, jnp.where(pos >= end0, end0, 0))


def stage(ids, lengths, ins, keys, values, queries, tq, tk, start, flags=None, times=None):
    y, z, core = ids[0], ids[1], ids[2]
    for group in range(4):
        for t in range(4):
            ref = ins[group * 4 + t]
            zz = (z + 4 - t) % 4
            dev = (y if group < 2 else 1 - y) * 8 + zz * 2 + (core if group % 2 == 0 else 1 - core)
            keys[dev] = ref[0:T, 0:T]
            values[dev] = ref[0:T, T : 2 * T]
            keys[2 * DEVS - 1 - dev] = ref[T : 2 * T, 0:T]
            values[2 * DEVS - 1 - dev] = ref[T : 2 * T, T : 2 * T]
            head = ref[256:272, 0:256].astype(f32)
            moments = head[0:1] * 128.0 + head[1:2]
            tk[dev] = jnp.broadcast_to(moments[:, :T], (8, T))
            tk[2 * DEVS - 1 - dev] = jnp.broadcast_to(moments[:, T:], (8, T))
            if times is not None:
                times[pl.ds(dev, 1), :] = moments[:, :T]
                times[pl.ds(2 * DEVS - 1 - dev, 1), :] = moments[:, T:]
            if group == 0:
                queries[2 * zz] = ref[0:T, 2 * T :]
                queries[2 * zz + 1] = ref[T : 2 * T, 2 * T :]
                if flags is not None:
                    flags[pl.ds(2 * zz, 1), :] = head[2:3, :T]
                    flags[pl.ds(2 * zz + 1, 1), :] = head[2:3, T:]
    keys[TILES] = jnp.zeros((T, T), bf16)
    values[TILES] = jnp.zeros((T, T), bf16)
    queries[QT] = jnp.zeros((T, T), bf16)
    tk[TILES] = jnp.zeros((8, T), f32)
    tq[QT] = jnp.zeros((T, T), f32)
    start[QT] = jnp.zeros((T, T), i32)
    rows = lax.broadcasted_iota(i32, (T, T), 0)
    for jj in range(QT):
        tile = query_tile(ids, jj)
        tq[jj] = jnp.transpose(jnp.broadcast_to(tk[tile][0:1, :], (T, T)))
        start[jj] = starts_of(lengths, rows + tile * T)


def make_lists(ids, lengths, flags, times, q_times, codes, codes_smem, sem, far, near, counts):
    def level(gap):
        total = jnp.zeros(gap.shape, i32)
        for j in range(1, BUCKETS):
            total = total + jnp.where(gap >= float(2**j - 1), 1, 0)
        return total

    for jj in range(QT):
        q_times[jj : jj + 1, :] = times[pl.ds(query_tile(ids, jj), 1), :]
    turned = jnp.transpose(times[...])
    k_first, k_last = turned[0:1, :], turned[T - 1 :, :]
    q_first, q_last = q_times[:, 0:1], q_times[:, T - 1 :]
    jj = lax.broadcasted_iota(i32, (8, T), 0)
    kk = lax.broadcasted_iota(i32, (8, T), 1)
    tile = query_tile(ids, jj)
    low = starts_of(lengths, tile * T)
    high = starts_of(lengths, tile * T + T - 1)
    bottom = level(jnp.maximum(q_first - k_last, 0.0))
    top = level(q_last - k_first)
    allowed = (flags[...] > 0.5) & (kk <= tile) & (kk * T + T - 1 >= low)
    plain = (kk < tile) & (kk * T >= high) & (top - bottom <= 2)
    entry = jj + 16 * kk
    codes[...] = jnp.where(
        allowed, jnp.where(plain, entry + 1024 * bottom, entry + NEAR_FLAG), -1
    )
    copy = pltpu.make_async_copy(codes, codes_smem, sem)
    copy.start()
    copy.wait()

    def query_step(jj, sizes):
        tile = query_tile(ids, jj)

        def key_step(k, sizes):
            n_far, n_near = sizes
            code = codes_smem[jj, k]
            far[n_far] = code
            near[n_near] = code & (NEAR_FLAG - 1)
            is_near = code >= NEAR_FLAG
            is_far = (code >= 0) & jnp.logical_not(is_near)
            return n_far + is_far.astype(i32), n_near + is_near.astype(i32)

        return lax.fori_loop(starts_of(lengths, tile * T) // T, tile + 1, key_step, sizes)

    n_far, n_near = lax.fori_loop(0, QT, query_step, (jnp.int32(0), jnp.int32(0)))
    for pad in range(FAR_U):
        far[n_far + pad] = DUMMY
    for pad in range(NEAR_U):
        near[n_near + pad] = DUMMY
    counts[0] = (n_far + FAR_U - 1) // FAR_U
    counts[1] = (n_near + NEAR_U - 1) // NEAR_U


def unpack(ref, i, count):
    got = []
    for u in range(count):
        entry = ref[i * count + u]
        got.append((entry & 15, (entry >> 4) & 63, entry >> 10))
    return got


def forward_kernel(ids, table, lengths, *refs):
    ins, o_refs, (far, near, counts) = refs[:16], refs[16:20], refs[20:23]
    keys, values, queries, tq, tk, start, acc, flags, times, q_times, codes, codes_smem, sem = refs[23:]
    z = ids[1]
    times[...] = jnp.zeros(times.shape, f32)
    stage(ids, lengths, ins, keys, values, queries, tq, tk, start, flags, times)
    make_lists(ids, lengths, flags, times, q_times, codes, codes_smem, sem, far, near, counts)
    acc[...] = jnp.zeros(acc.shape, f32)

    def far_step(i, _):
        got = unpack(far, i, FAR_U)
        dots = [lax.dot_general(queries[j], keys[k], NT_DIMS, preferred_element_type=f32) for j, k, _ in got]
        weights = []
        for u, (jj, k, bottom) in enumerate(got):
            bias, _, _ = bias_far(tq[jj] - tk[k][0:1, :], table, bottom)
            half = dots[u] * (0.5 * SCALE) + bias
            weights.append((half * jnp.tanh(half) + half).astype(bf16))
        adds = [jnp.dot(weights[u], values[got[u][1]], preferred_element_type=f32) for u in range(len(got))]
        for u in range(len(got)):
            acc[got[u][0]] += adds[u]
        return 0

    def near_step(i, _):
        got = unpack(near, i, NEAR_U)
        dots = [lax.dot_general(queries[j], keys[k], NT_DIMS, preferred_element_type=f32) for j, k, _ in got]
        weights = []
        for u, (jj, k, _) in enumerate(got):
            half = dots[u] * (0.5 * SCALE) + bias_near(tq[jj] - tk[k][0:1, :], table)
            weight = half * jnp.tanh(half) + half
            weights.append(jnp.where(keep_near(ids, start[jj], jj, k), weight, 0.0).astype(bf16))
        adds = [jnp.dot(weights[u], values[got[u][1]], preferred_element_type=f32) for u in range(len(got))]
        for u in range(len(got)):
            acc[got[u][0]] += adds[u]
        return 0

    lax.fori_loop(0, counts[0], far_step, 0)
    lax.fori_loop(0, counts[1], near_step, 0)
    for s in range(4):
        zz = (z + s) % 4
        o_refs[s][0:T] = acc[2 * zz]
        o_refs[s][T:] = acc[2 * zz + 1]


def attend(ids, table, lengths, parts):
    return pl.pallas_call(
        forward_kernel,
        in_specs=[SMEM] * 3 + [VMEM] * 16,
        out_specs=[VMEM] * 4 + [SMEM] * 3,
        out_shape=[sds((256, T), f32)] * 4 + [sds((LIST,), i32), sds((LIST,), i32), sds((8,), i32)],
        scratch_shapes=STAGE
        + [
            pltpu.VMEM((QT + 1, T, T), f32),
            pltpu.VMEM((8, T), f32),
            pltpu.VMEM((T, T), f32),
            pltpu.VMEM((8, T), f32),
            pltpu.VMEM((8, T), i32),
            pltpu.SMEM((8, T), i32),
            pltpu.SemaphoreType.DMA,
        ],
        compiler_params=params(),
        cost_estimate=cost(1e9 * 6, 6 << 20),
        name="attend",
    )(ids, table, lengths, *parts)


def middle_kernel(ids, cot, out_proj, gate, slope, *refs):
    ins, (mixed, grad_gate), g_refs = refs[:4], refs[4:6], refs[6:10]
    att, back = refs[10], refs[11]
    z = ids[1]
    for t in range(4):
        att[(z + 4 - t) % 4] = ins[t][...]
    whole = jnp.concatenate([att[h] for h in range(4)], axis=1)
    normed, inverse = norm_rows(whole)
    gates = jnp.concatenate([gate[h] for h in range(4)], axis=1).astype(f32)
    mixed[...] = (normed * gates).astype(bf16)
    grad_mix = lax.dot_general(cot[...], out_proj[...], NT_DIMS, preferred_element_type=f32)
    gate_slope = jnp.concatenate([slope[h] for h in range(4)], axis=1).astype(f32)
    grad_gate[...] = (grad_mix * normed * gate_slope).astype(bf16)
    grad = norm_back(grad_mix * gates, normed, inverse).astype(bf16)
    for h in range(4):
        back[h] = grad[:, h * T : (h + 1) * T]
    for s in range(4):
        g_refs[s][...] = back[(z + s) % 4]


def middle(ids, cot, out_proj, gate, slope, parts):
    return pl.pallas_call(
        middle_kernel,
        grid=(1,),
        in_specs=[
            SMEM,
            pl.BlockSpec((256, 1024), lambda i: (0, 0)),
            pl.BlockSpec((512, 1024), lambda i: (0, 0)),
            pl.BlockSpec((4, 256, T), lambda i: (0, 0, 0)),
            pl.BlockSpec((None, 4, 256, T), lambda i: (0, 0, 0, 0)),
        ]
        + [pl.BlockSpec((256, T), lambda i: (0, 0))] * 4,
        out_specs=[pl.BlockSpec((256, 512), lambda i: (0, 0))] * 2
        + [pl.BlockSpec((256, T), lambda i: (0, 0))] * 4,
        out_shape=[sds((256, 512), bf16)] * 2 + [sds((256, T), bf16)] * 4,
        scratch_shapes=[pltpu.VMEM((4, 256, T), f32), pltpu.VMEM((4, 256, T), bf16)],
        compiler_params=params(),
        cost_estimate=cost(2 * 256 * 512 * 1024, 4 << 20),
        name="middle",
    )(ids, cot, out_proj, gate, slope, *parts)


def output_kernel(ids, tokens, cot, out_proj, mixed, output, mine, *theirs):
    y, z, core, low, x = ids[0], ids[1], ids[2], ids[3] // 4, ids[3] % 4
    output[...] = (
        tokens[...].astype(f32) + jnp.dot(mixed[...], out_proj[...], preferred_element_type=f32)
    ).astype(bf16)
    r = lax.broadcasted_iota(i32, (512, 512), 1)
    c = lax.broadcasted_iota(i32, (512, 512), 0)
    r_x = ((r // 128) + x) % 4
    r_core = ((r // 64) % 2) ^ core
    r_z = (((r // 16) % 4) + z) % 4
    r_y = ((r // 8) % 2) ^ y
    r_low = ((r // 4) % 2) ^ low
    source = (r_low * 4 + r_x) * 64 + r_y * 32 + r_z * 8 + r_core * 4 + r % 4
    pick = jnp.where(c == source, 1.0, 0.0).astype(bf16)
    moved = jnp.dot(mixed[...], pick, preferred_element_type=f32).astype(bf16)
    part = lax.dot_general(moved, cot[...], TN_DIMS, preferred_element_type=f32)
    mine[...] = part[:T]
    for i in range(3):
        theirs[i][...] = part[(i + 1) * T : (i + 2) * T].astype(bf16)


def finish_output(ids, tokens, cot, out_proj, mixed):
    return pl.pallas_call(
        output_kernel,
        in_specs=[SMEM] + [VMEM] * 4,
        out_specs=[VMEM] * 5,
        out_shape=[sds((256, 1024), bf16), sds((T, 1024), f32)] + [sds((T, 1024), bf16)] * 3,
        compiler_params=params(),
        cost_estimate=cost(6 * 256 * 512 * 1024, 5 << 20),
        name="finish_output",
    )(ids, tokens, cot, out_proj, mixed)


def backward_kernel(ids, table, lengths, far, near, counts, *refs):
    ins, got_grads, outs = refs[:16], refs[16:20], refs[20:26]
    mine_s, mine_o, theirs_s, theirs_o, dq_out, rab_out = outs
    keys, values, queries, tq, tk, start, grads, grads_t, queries_t, dq, dkt, dvt, rab = refs[26:]
    y, z, core = ids[0], ids[1], ids[2]
    stage(ids, lengths, ins, keys, values, queries, tq, tk, start)
    for t in range(4):
        zz = (z + 4 - t) % 4
        for half in range(2):
            block = got_grads[t][half * T : (half + 1) * T, :].astype(f32) * 0.5
            grads[2 * zz + half] = block.astype(bf16)
            grads_t[2 * zz + half] = jnp.transpose(block).astype(bf16)
    for jj in range(QT):
        queries_t[jj] = jnp.transpose(queries[jj].astype(f32)).astype(bf16)
    grads[QT] = jnp.zeros((T, T), bf16)
    grads_t[QT] = jnp.zeros((T, T), bf16)
    queries_t[QT] = jnp.zeros((T, T), bf16)
    dq[...] = jnp.zeros(dq.shape, f32)
    dkt[...] = jnp.zeros(dkt.shape, f32)
    dvt[...] = jnp.zeros(dvt.shape, f32)
    rab[...] = jnp.zeros(rab.shape, f32)

    def fold(values_):
        return jnp.sum(values_.reshape(T // 8, 8, T), axis=0)

    def front(got):
        dots = [lax.dot_general(queries[j], keys[k], NT_DIMS, preferred_element_type=f32) for j, k, _ in got]
        wides = [lax.dot_general(grads[j], values[k], NT_DIMS, preferred_element_type=f32) for j, k, _ in got]
        return dots, wides

    def score(half, wide, keep):
        t = jnp.tanh(half)
        weight = half * t + half
        d_score = wide * ((1.0 + t) * (1.0 + half * (1.0 - t)))
        if keep is not None:
            weight = jnp.where(keep, weight, 0.0)
            d_score = jnp.where(keep, d_score, 0.0)
        return weight.astype(bf16), d_score

    def back(got, weights, scores):
        a = [jnp.dot(scores[u], keys[got[u][1]], preferred_element_type=f32) for u in range(len(got))]
        b = [jnp.dot(queries_t[got[u][0]], scores[u], preferred_element_type=f32) for u in range(len(got))]
        c = [jnp.dot(grads_t[got[u][0]], weights[u], preferred_element_type=f32) for u in range(len(got))]
        for u, (jj, k, _) in enumerate(got):
            dq[jj] += a[u]
            dkt[k] += b[u]
            dvt[k] += c[u]

    def far_step(i, _):
        got = unpack(far, i, FAR_U)
        dots, wides = front(got)
        weights, scores, sums = [], [], []
        for u, (jj, k, bottom) in enumerate(got):
            bias, over1, over2 = bias_far(tq[jj] - tk[k][0:1, :], table, bottom)
            weight, d_score = score(dots[u] * (0.5 * SCALE) + bias, wides[u], None)
            weights.append(weight)
            scores.append(d_score.astype(bf16))
            sums.append((fold(d_score), fold(jnp.where(over1, d_score, 0.0)), fold(jnp.where(over2, d_score, 0.0))))
        back(got, weights, scores)
        for (jj, k, bottom), (sum0, sum1, sum2) in zip(got, sums):
            rab[bottom] += sum0 - sum1
            rab[bottom + 1] += sum1 - sum2
            rab[bottom + 2] += sum2
        return 0

    def near_step(i, _):
        got = unpack(near, i, NEAR_U)
        dots, wides = front(got)
        weights, scores = [], []
        sums = [jnp.zeros((8, T), f32)] * BUCKETS
        for u, (jj, k, _) in enumerate(got):
            gap = tq[jj] - tk[k][0:1, :]
            half = dots[u] * (0.5 * SCALE) + bias_near(gap, table)
            weight, d_score = score(half, wides[u], keep_near(ids, start[jj], jj, k))
            weights.append(weight)
            scores.append(d_score.astype(bf16))
            sums[0] = sums[0] + fold(d_score)
            for j in range(1, BUCKETS):
                sums[j] = sums[j] + fold(jnp.where(gap >= float(2**j - 1), d_score, 0.0))
        back(got, weights, scores)
        for j in range(BUCKETS - 1):
            rab[j] += sums[j] - sums[j + 1]
        rab[BUCKETS - 1] += sums[BUCKETS - 1]
        return 0

    lax.fori_loop(0, counts[0], far_step, 0)
    lax.fori_loop(0, counts[1], near_step, 0)
    for other in range(2):
        for s in range(4):
            base = (y if other == 0 else 1 - y) * 8 + ((z + s) % 4) * 2
            for side in range(2):
                dev = base + (core if side == 0 else 1 - core)
                ref = ((mine_s, theirs_s), (mine_o, theirs_o))[other][side]
                for half in range(2):
                    tile = dev if half == 0 else 2 * DEVS - 1 - dev
                    ref[s, 0:T, half * T : (half + 1) * T] = (dkt[tile] * SCALE).astype(bf16)
                    ref[s, T:, half * T : (half + 1) * T] = (dvt[tile] * 2.0).astype(bf16)
    for s in range(4):
        zz = (z + s) % 4
        for half in range(2):
            dq_out[s, :, half * T : (half + 1) * T] = (dq[2 * zz + half] * SCALE).astype(bf16)
    for b in range(16):
        if b < BUCKETS:
            rab_out[b : b + 1, :] = jnp.sum(rab[b], axis=0, keepdims=True)
        else:
            rab_out[b : b + 1, :] = jnp.zeros((1, T), f32)


def attend_back(ids, table, lengths, lists, parts, grads):
    return pl.pallas_call(
        backward_kernel,
        in_specs=[SMEM] * 6 + [VMEM] * 20,
        out_specs=[VMEM] * 6,
        out_shape=[sds((4, 256, 256), bf16)] * 4 + [sds((4, T, 256), bf16), sds((16, T), f32)],
        scratch_shapes=STAGE
        + [
            pltpu.VMEM((QT + 1, T, T), bf16),
            pltpu.VMEM((QT + 1, T, T), bf16),
            pltpu.VMEM((QT + 1, T, T), bf16),
            pltpu.VMEM((QT + 1, T, T), f32),
            pltpu.VMEM((TILES + 1, T, T), f32),
            pltpu.VMEM((TILES + 1, T, T), f32),
            pltpu.VMEM((16, 8, T), f32),
        ],
        compiler_params=params(),
        cost_estimate=cost(1e9 * 12, 8 << 20),
        name="attend_back",
    )(ids, table, lengths, *lists, *parts, *grads)


def combine_kernel(mine_s, mine_o, got_s, got_o, dq, proj_own, proj_got, *outs):
    proj = proj_own[...] + proj_got[...].astype(f32)
    for s in range(4):
        outs[s][0:256, :] = (mine_s[s].astype(f32) + got_s[s].astype(f32)).astype(bf16)
        outs[s][256:384, :] = dq[s]
        outs[4 + s][0:256, :] = (mine_o[s].astype(f32) + got_o[s].astype(f32)).astype(bf16)
        for other in range(2):
            block = proj[s * 16 + other * 8 : s * 16 + other * 8 + 8, :]
            block = jnp.concatenate([block[:, c * 256 : (c + 1) * 256] for c in range(4)], axis=0)
            outs[4 * other + s][384 - 128 * other :, :] = block.astype(bf16)


def combine(mine_s, mine_o, got_s, got_o, dq, proj_own, proj_got):
    return pl.pallas_call(
        combine_kernel,
        in_specs=[VMEM] * 7,
        out_specs=[VMEM] * 8,
        out_shape=[sds((416, 256), bf16)] * 4 + [sds((288, 256), bf16)] * 4,
        compiler_params=params(),
        cost_estimate=cost(1 << 20, 5 << 20),
        name="combine",
    )(mine_s, mine_o, got_s, got_o, dq, proj_own, proj_got)


def collect_kernel(*refs):
    ins, keep, give = refs[:8], refs[8], refs[9]
    total = ins[0][...].astype(f32)
    for ref in ins[1:]:
        total = total + ref[...].astype(f32)
    for c in range(4):
        keep[:, c * 256 : (c + 1) * 256] = total[c * 8 : c * 8 + 4, :]
        give[:, c * 256 : (c + 1) * 256] = total[c * 8 + 4 : c * 8 + 8, :]


def collect(same, other):
    return pl.pallas_call(
        collect_kernel,
        grid=(1,),
        in_specs=[pl.BlockSpec((32, 256), lambda i: (12, 0))] * 4
        + [pl.BlockSpec((32, 256), lambda i: (8, 0))] * 4,
        out_specs=[pl.BlockSpec((4, 1024), lambda i: (0, 0))] * 2,
        out_shape=[sds((4, 1024), f32)] * 2,
        cost_estimate=cost(1 << 16, 1 << 18),
        name="collect",
    )(*same, *other)


def final_kernel(ids, tokens, cot, in_proj, slope, grad_gate, *refs):
    same, other, grad_in, grad_pre, grad_normed = refs[:4], refs[4:8], refs[8], refs[9], refs[10]
    step = pl.program_id(0)
    z = ids[1]

    @pl.when(step == 0)
    def _():
        grad_pre[:, 0:512] = grad_gate[...]
        for t in range(4):
            head = (z + 4 - t) % 4
            column = lambda kind: pl.ds(pl.multiple_of(kind * 512 + head * T, T), T)
            total = same[t][0:256, :].astype(f32) + other[t][0:256, :].astype(f32)
            for half in range(2):
                rows = slice(half * T, (half + 1) * T)
                key = jnp.transpose(total[0:T, rows])
                value = jnp.transpose(total[T:, rows])
                query = same[t][256:384, rows].astype(f32)
                for kind, part in ((1, value), (2, query), (3, key)):
                    grad_pre[rows, column(kind)] = (
                        part * slope[kind, head, rows, :].astype(f32)
                    ).astype(bf16)

    grad_normed[step] = lax.dot_general(
        grad_pre[...], in_proj[...], NT_DIMS, preferred_element_type=f32
    )

    @pl.when(step == 3)
    def _():
        normed, inverse = norm_rows(tokens[...].astype(f32))
        upstream = jnp.concatenate([grad_normed[i] for i in range(4)], axis=1)
        grad_in[...] = (cot[...].astype(f32) + norm_back(upstream, normed, inverse)).astype(bf16)


def finish_grad(ids, tokens, cot, in_proj, slope, grad_gate, same, other):
    whole = lambda shape: pl.BlockSpec(shape, lambda s: (0,) * len(shape))
    return pl.pallas_call(
        final_kernel,
        grid=(4,),
        in_specs=[
            SMEM,
            whole((256, 1024)),
            whole((256, 1024)),
            pl.BlockSpec((256, 2048), lambda s: (s, 0)),
            whole((4, 4, 256, T)),
            whole((256, 512)),
        ]
        + [whole((384, 256))] * 4
        + [whole((256, 256))] * 4,
        out_specs=whole((256, 1024)),
        out_shape=sds((256, 1024), bf16),
        scratch_shapes=[pltpu.VMEM((256, 2048), bf16), pltpu.VMEM((4, 256, 256), f32)],
        compiler_params=params(),
        cost_estimate=cost(2 * 256 * 1024 * 2048, 8 << 20),
        name="finish_grad",
    )(ids, tokens, cot, in_proj, slope, grad_gate, *same, *other)


def move(y_xor, z_shift, core_xor):
    pairs = []
    for dev in range(DEVS):
        y, z, core = dev // 8, (dev // 2) % 4, dev % 2
        target = (y ^ y_xor) * 8 + ((z + z_shift) % 4) * 2 + (core ^ core_xor)
        pairs.append((dev, target))
    return pairs


def send(x, y_xor, z_shift, core_xor):
    return lax.ppermute(x, "ctx", move(y_xor, z_shift, core_xor))


def send_x(part, shift):
    return lax.ppermute(part, "dp", [(d, d // 4 * 4 + (d + shift) % 4) for d in range(8)])


def sum_rab(part):
    row = jnp.sum(part, axis=1)
    row = jnp.concatenate([row, jnp.zeros((T - 16,), f32)])
    every = lax.all_to_all(jnp.broadcast_to(row[None], (T, T)), ("dp", "ctx"), 0, 0, tiled=True)
    sums = jnp.sum(every.reshape(8, 2, 4, 2, T)[..., :BUCKETS], axis=(0, 1, 3))
    return sums.T


def on_device(tokens, cotangent, in_proj, out_proj, rab_time, seq_lengths, block_mask, time_bucket):
    ctx = lax.axis_index("ctx")
    dp = lax.axis_index("dp")
    y, z, core = ctx // 8, (ctx // 2) % 4, ctx % 2
    ids = jnp.stack([y, z, core, dp]).astype(i32)
    lengths = seq_lengths.reshape(3)
    limits = [2.0**j - 1.0 for j in range(BUCKETS)] + [1e9] * 4
    head_bias = lax.dynamic_slice_in_dim(rab_time, z, 1, 1).reshape(BUCKETS) * 0.5
    table = jnp.concatenate([head_bias, jnp.zeros((4,), f32), jnp.array(limits, f32)])
    mask = block_mask.reshape(2, 16, 2)
    mask = jnp.concatenate([mask[:, :, 0], mask[:, ::-1, 1], jnp.zeros((2, 96), i32)], axis=1)
    meta = jnp.stack([time_bucket // 128, time_bucket % 128, mask.reshape(256)])
    meta = jnp.pad(meta, ((0, 13), (0, 0))).astype(bf16)

    made = project(ids, tokens, meta, in_proj)
    gate, slope, full, pairs = made[0], made[1], made[2:6], made[6:10]
    own = [full[0]] + [send(full[s], 0, s, 0) for s in (1, 2, 3)]
    across = [send(pairs[s], 1, s, 0) for s in range(4)]
    own_twin = [send(part, 0, 0, 1) for part in own]
    across_twin = [send(part, 0, 0, 1) for part in across]
    parts = own + own_twin + across + across_twin
    done = attend(ids, table, lengths, parts)
    blocks, lists = done[:4], done[4:]

    heads = [blocks[0]] + [send(blocks[s], 0, s, 0) for s in (1, 2, 3)]
    between = middle(ids, cotangent, out_proj, gate, slope, heads)
    mixed, grad_gate, grads = between[0], between[1], between[2:]
    grads = [grads[0]] + [send(grads[s], 0, s, 0) for s in (1, 2, 3)]
    made = finish_output(ids, tokens, cotangent, out_proj, mixed)
    output, proj = made[0], made[1]
    for s in (1, 2, 3):
        proj = proj + send_x(made[1 + s], s).astype(f32)
    proj_own = proj[:64]
    proj_got = send(proj[64:].astype(bf16), 0, 0, 1)

    mine_s, mine_o, theirs_s, theirs_o, dq, rab = attend_back(ids, table, lengths, lists, parts, grads)
    got_o = send(theirs_o, 0, 0, 1)
    got_s = send(theirs_s, 0, 0, 1)
    messages = combine(mine_s, mine_o, got_s, got_o, dq, proj_own, proj_got)
    messages, rab = lax.optimization_barrier((messages, rab))
    same = [messages[0]] + [send(messages[s], 0, s, 0) for s in (1, 2, 3)]
    other = [send(messages[4 + s], 1, s, 0) for s in range(4)]
    rab_grad = sum_rab(rab)
    keep, give = collect(same, other)
    proj_grad = keep + lax.ppermute(give, "dp", [(d, d ^ 4) for d in range(8)])
    grad_in = finish_grad(ids, tokens, cotangent, in_proj, slope, grad_gate, same, other)
    return output, grad_in, proj_grad, rab_grad


def solution(mesh):
    rows = P(("dp", "ctx"), None)
    placed = (rows, rows, P(), P(), P(), P("dp", None), P("dp", "ctx", None), P(("dp", "ctx")))
    return jax.shard_map(
        on_device,
        mesh=mesh,
        in_specs=placed,
        out_specs=(rows, rows, rows, P()),
        check_vma=False,
    )
```

```python
import functools
import math

import jax
import jax.numpy as jnp
from jax import lax
from jax.experimental import pallas as pl
from jax.experimental.pallas import tpu as pltpu
from jax.sharding import PartitionSpec as P

f32 = jnp.float32
bf16 = jnp.bfloat16
i32 = jnp.int32
T = 128
EPS = 1e-05
HEADS = 4
BUCKETS = 12
DEVS = 16
TILES = 32
QT = 8
SCALE = 1.0 / math.sqrt(128.0)
LIST = 160
FAR_U = 8
NEAR_U = 4
NEAR_FLAG = 32768
DUMMY = QT + 16 * TILES
VM_ATTEND = 20
VM_BACK = 24
VMEM = pl.BlockSpec(memory_space=pltpu.VMEM)
SMEM = pl.BlockSpec(memory_space=pltpu.SMEM)
NT_DIMS = (((1,), (1,)), ((), ()))
TN_DIMS = (((0,), (0,)), ((), ()))


def params(mib=24):
    return pltpu.CompilerParams(vmem_limit_bytes=mib * 1024 * 1024)


def cost(flops, size):
    return pl.CostEstimate(flops=int(flops), bytes_accessed=int(size), transcendentals=0)


def sds(shape, dtype):
    return jax.ShapeDtypeStruct(shape, dtype)


def norm_rows(values):
    centre = jnp.mean(values, axis=-1, keepdims=True)
    shifted = values - centre
    spread = jnp.mean(shifted * shifted, axis=-1, keepdims=True)
    inverse = lax.rsqrt(spread + EPS)
    return shifted * inverse, inverse


def norm_back(upstream, normed, inverse):
    first = jnp.mean(upstream, axis=-1, keepdims=True)
    second = jnp.mean(upstream * normed, axis=-1, keepdims=True)
    return inverse * (upstream - first - normed * second)


def in_hbm(part):
    return pltpu.with_memory_space_constraint(part, pltpu.HBM)


def project_kernel(own, tokens, *refs):
    weights, outs, normed = refs[own : 2 * own + 2], refs[2 * own + 2 : -1], refs[-1]
    head = pl.program_id(0)
    shift = (head + 4 - (lax.axis_index("ctx") // 2) % 4) % 4

    @pl.when(head == 0)
    def _():
        normed[...] = norm_rows(tokens[0:256, :].astype(f32))[0].astype(bf16)

    wide = jnp.concatenate([w[...] for w in weights], axis=1)
    half = 0.5 * jnp.dot(normed[...], wide, preferred_element_type=f32)
    act = (half * jnp.tanh(half) + half).astype(bf16)
    meta = tokens[256:, 0:256]
    if own:
        mask, blank = refs[0], jnp.zeros((1, T - TILES), f32)
        row = [mask[0, 0:1].astype(f32), blank, mask[0, 1:2].astype(f32), blank]
        rows = [meta[0:2].astype(f32), jnp.concatenate(row, axis=1), jnp.zeros((13, 256), f32)]
        meta = jnp.concatenate(rows, axis=0).astype(bf16)
    for which in range(4):

        @pl.when(shift == which)
        def _(which=which):
            outs[which][0:256, :] = act
            outs[which][256:, 0:256] = meta
            if own:
                outs[which][256:, 256:] = jnp.zeros((16, T), bf16)


def project(tokens, in_proj, mask=None):
    own = mask is not None
    width = 384 if own else 256

    def column(kind):
        return pl.BlockSpec((1024, T), lambda h: (0, kind * HEADS + h))

    whole = lambda shape: pl.BlockSpec(shape, lambda h: (0,) * len(shape))
    kinds = (3, 1, 2) if own else (3, 1)
    return pl.pallas_call(
        functools.partial(project_kernel, int(own)),
        grid=(HEADS,),
        in_specs=[whole((272, 1024))] + [whole((1, 2, TILES))] * own + [column(kind) for kind in kinds],
        out_specs=[whole((272, width))] * 4,
        out_shape=[sds((272, width), bf16)] * 4,
        scratch_shapes=[pltpu.VMEM((256, 1024), bf16)],
        compiler_params=params(12),
        cost_estimate=cost(2 * 256 * 1024 * 4 * width, 5 << 20),
        name="project_own" if own else "project_other",
    )(tokens, *([in_hbm(mask)] if own else []), *[in_hbm(in_proj)] * len(kinds))


def gates_kernel(tokens, in_proj, cot, out_proj, gate, slope, grad_mix, normed):
    kind = pl.program_id(0)

    @pl.when(kind == 0)
    def _():
        normed[...] = norm_rows(tokens[...].astype(f32))[0].astype(bf16)
        grad_mix[...] = lax.dot_general(cot[...], out_proj[...], NT_DIMS, preferred_element_type=f32)

    pre = jnp.dot(normed[...], in_proj[...], preferred_element_type=f32)
    sig = 0.5 * jnp.tanh(0.5 * pre) + 0.5
    slope[...] = (sig * (1.0 + pre * (1.0 - sig))).astype(bf16)

    @pl.when(kind == 0)
    def _():
        gate[...] = (pre * sig).astype(bf16)


def make_gates(tokens, in_proj, cot, out_proj):
    whole = lambda shape: pl.BlockSpec(shape, lambda s: (0,) * len(shape))
    return pl.pallas_call(
        gates_kernel,
        grid=(4,),
        in_specs=[
            whole((256, 1024)),
            pl.BlockSpec((1024, 512), lambda s: (0, s)),
            whole((256, 1024)),
            whole((512, 1024)),
        ],
        out_specs=[whole((256, 512)), pl.BlockSpec((256, 512), lambda s: (0, s)), whole((256, 512))],
        out_shape=[sds((256, 512), bf16), sds((256, 2048), bf16), sds((256, 512), f32)],
        scratch_shapes=[pltpu.VMEM((256, 1024), bf16)],
        compiler_params=params(16),
        cost_estimate=cost(2 * 256 * 1024 * 2048, 7 << 20),
        name="gates",
    )(in_hbm(tokens), in_hbm(in_proj), in_hbm(cot), in_hbm(out_proj))


def bias_far(gap, table, bottom):
    first = table[bottom]
    second = table[bottom + 1]
    third = table[bottom + 2]
    limit1 = table[16 + bottom + 1]
    limit2 = table[16 + bottom + 2]
    over1 = gap >= limit1
    over2 = gap >= limit2
    return jnp.where(over2, third, jnp.where(over1, second, first)), over1, over2


def bias_near(gap, table):
    bias = jnp.full(gap.shape, table[0], f32)
    for j in range(1, BUCKETS):
        bias = jnp.where(gap >= float(2**j - 1), table[j], bias)
    return bias


def keep_near(ids, start, jj, k):
    tile = query_tile(ids, jj)
    row = lax.broadcasted_iota(i32, (T, T), 0)
    col = lax.broadcasted_iota(i32, (T, T), 1)
    later = (col - row) <= (tile - k) * T
    return later & ((col + k * T) >= start)


STAGE = [pltpu.VMEM((QT + 1, T, T), f32), pltpu.VMEM((QT + 1, T, T), i32)]


def query_tile(ids, jj):
    dev = ids[0] * 8 + (jj // 2) * 2 + ids[2]
    return jnp.where(jj % 2 == 0, dev, 2 * DEVS - 1 - dev)


def starts_of(lengths, pos):
    end0 = lengths[0]
    end1 = lengths[0] + lengths[1]
    return jnp.where(pos >= end1, end1, jnp.where(pos >= end0, end0, 0))


def stage(ids, ins, keys, values, queries, tk, flags, times):
    y, z, core = ids[0], ids[1], ids[2]
    for group in range(4):
        for t in range(4):
            ref = ins[group * 4 + t]
            zz = (z + 4 - t) % 4
            dev = (y if group < 2 else 1 - y) * 8 + zz * 2 + (core if group % 2 == 0 else 1 - core)
            keys[dev] = ref[0:T, 0:T]
            values[dev] = ref[0:T, T : 2 * T]
            keys[2 * DEVS - 1 - dev] = ref[T : 2 * T, 0:T]
            values[2 * DEVS - 1 - dev] = ref[T : 2 * T, T : 2 * T]
            head = ref[256:272, 0:256].astype(f32)
            moments = head[0:1] * 128.0 + head[1:2]
            tk[dev] = jnp.broadcast_to(moments[:, :T], (8, T))
            tk[2 * DEVS - 1 - dev] = jnp.broadcast_to(moments[:, T:], (8, T))
            times[pl.ds(dev, 1), :] = moments[:, :T]
            times[pl.ds(2 * DEVS - 1 - dev, 1), :] = moments[:, T:]
            if group == 0:
                queries[2 * zz] = ref[0:T, 2 * T :]
                queries[2 * zz + 1] = ref[T : 2 * T, 2 * T :]
                flags[pl.ds(2 * zz, 1), :] = head[2:3, :T]
                flags[pl.ds(2 * zz + 1, 1), :] = head[2:3, T:]
    keys[TILES] = jnp.zeros((T, T), bf16)
    values[TILES] = jnp.zeros((T, T), bf16)
    queries[QT] = jnp.zeros((T, T), bf16)
    tk[TILES] = jnp.zeros((8, T), f32)


def stage_times(ids, lengths, tq, tk, start):
    tq[QT] = jnp.zeros((T, T), f32)
    start[QT] = jnp.zeros((T, T), i32)
    rows = lax.broadcasted_iota(i32, (T, T), 0)
    for jj in range(QT):
        tile = query_tile(ids, jj)
        tq[jj] = jnp.transpose(jnp.broadcast_to(tk[tile][0:1, :], (T, T)))
        start[jj] = starts_of(lengths, rows + tile * T)


def make_lists(ids, lengths, flags, times, q_times, codes, codes_smem, sem, far, near, counts):
    def level(gap):
        total = jnp.zeros(gap.shape, i32)
        for j in range(1, BUCKETS):
            total = total + jnp.where(gap >= float(2**j - 1), 1, 0)
        return total

    for jj in range(QT):
        q_times[jj : jj + 1, :] = times[pl.ds(query_tile(ids, jj), 1), :]
    turned = jnp.transpose(times[...])
    k_first, k_last = turned[0:1, :], turned[T - 1 :, :]
    q_first, q_last = q_times[:, 0:1], q_times[:, T - 1 :]
    jj = lax.broadcasted_iota(i32, (8, T), 0)
    kk = lax.broadcasted_iota(i32, (8, T), 1)
    tile = query_tile(ids, jj)
    low = starts_of(lengths, tile * T)
    high = starts_of(lengths, tile * T + T - 1)
    bottom = level(jnp.maximum(q_first - k_last, 0.0))
    top = level(q_last - k_first)
    row = lax.broadcasted_iota(i32, (T, T), 0)
    col = lax.broadcasted_iota(i32, (T, T), 1)
    turn = jnp.where(row == jnp.where(col < DEVS, 2 * col, 4 * DEVS - 1 - 2 * col), 1.0, 0.0).astype(bf16)
    ordered = jnp.dot(flags[...].astype(bf16), turn, preferred_element_type=f32)
    allowed = (ordered > 0.5) & (kk <= tile) & (kk * T + T - 1 >= low)
    plain = (kk < tile) & (kk * T >= high) & (top - bottom <= 2)
    entry = jj + 16 * kk
    codes[...] = jnp.where(
        allowed, jnp.where(plain, entry + 1024 * bottom, entry + NEAR_FLAG), -1
    )
    copy = pltpu.make_async_copy(codes, codes_smem, sem)
    copy.start()
    copy.wait()

    def query_step(jj, sizes):
        tile = query_tile(ids, jj)

        def key_step(k, sizes):
            n_far, n_near = sizes
            code = codes_smem[jj, k]
            far[n_far] = code
            near[n_near] = code & (NEAR_FLAG - 1)
            is_near = code >= NEAR_FLAG
            is_far = (code >= 0) & jnp.logical_not(is_near)
            return n_far + is_far.astype(i32), n_near + is_near.astype(i32)

        return lax.fori_loop(starts_of(lengths, tile * T) // T, tile + 1, key_step, sizes)

    n_far, n_near = lax.fori_loop(0, QT, query_step, (jnp.int32(0), jnp.int32(0)))
    for pad in range(FAR_U):
        far[n_far + pad] = DUMMY
    for pad in range(NEAR_U):
        near[n_near + pad] = DUMMY
    counts[0] = (n_far + FAR_U - 1) // FAR_U
    counts[1] = (n_near + NEAR_U - 1) // NEAR_U


def unpack(ref, i, count):
    got = []
    for u in range(count):
        entry = ref[i * count + u]
        got.append((entry & 15, (entry >> 4) & 63, entry >> 10))
    return got


def forward_kernel(ids, table, lengths, *refs):
    ins, (out, far, near, counts, keys, values, queries, tk) = refs[:16], refs[16:24]
    tq, start, acc, flags, times, q_times, codes, codes_smem, sem = refs[24:]
    times[...] = jnp.zeros(times.shape, f32)
    stage(ids, ins, keys, values, queries, tk, flags, times)
    stage_times(ids, lengths, tq, tk, start)
    make_lists(ids, lengths, flags, times, q_times, codes, codes_smem, sem, far, near, counts)
    acc[...] = jnp.zeros(acc.shape, f32)

    def far_step(i, _):
        got = unpack(far, i, FAR_U)
        dots = [lax.dot_general(queries[j], keys[k], NT_DIMS, preferred_element_type=f32) for j, k, _ in got]
        weights = []
        for u, (jj, k, bottom) in enumerate(got):
            bias, _, _ = bias_far(tq[jj] - tk[k][0:1, :], table, bottom)
            half = dots[u] * (0.5 * SCALE) + bias
            weights.append((half * jnp.tanh(half) + half).astype(bf16))
        adds = [jnp.dot(weights[u], values[got[u][1]], preferred_element_type=f32) for u in range(len(got))]
        for u in range(len(got)):
            acc[got[u][0]] += adds[u]
        return 0

    def near_step(i, _):
        got = unpack(near, i, NEAR_U)
        dots = [lax.dot_general(queries[j], keys[k], NT_DIMS, preferred_element_type=f32) for j, k, _ in got]
        weights = []
        for u, (jj, k, _) in enumerate(got):
            half = dots[u] * (0.5 * SCALE) + bias_near(tq[jj] - tk[k][0:1, :], table)
            weight = half * jnp.tanh(half) + half
            weights.append(jnp.where(keep_near(ids, start[jj], jj, k), weight, 0.0).astype(bf16))
        adds = [jnp.dot(weights[u], values[got[u][1]], preferred_element_type=f32) for u in range(len(got))]
        for u in range(len(got)):
            acc[got[u][0]] += adds[u]
        return 0

    lax.fori_loop(0, counts[0], far_step, 0)
    lax.fori_loop(0, counts[1], near_step, 0)
    for zz in range(4):
        out[zz, 0:T] = acc[2 * zz]
        out[zz, T:] = acc[2 * zz + 1]


def attend(ids, table, lengths, parts):
    return pl.pallas_call(
        forward_kernel,
        in_specs=[SMEM] * 3 + [VMEM] * 16,
        out_specs=[VMEM] + [SMEM] * 3 + [VMEM] * 4,
        out_shape=[sds((4, 256, T), f32), sds((LIST,), i32), sds((LIST,), i32), sds((8,), i32)]
        + [sds((TILES + 1, T, T), bf16)] * 2
        + [sds((QT + 1, T, T), bf16), sds((TILES + 1, 8, T), f32)],
        scratch_shapes=STAGE
        + [
            pltpu.VMEM((QT + 1, T, T), f32),
            pltpu.VMEM((8, T), f32),
            pltpu.VMEM((T, T), f32),
            pltpu.VMEM((8, T), f32),
            pltpu.VMEM((8, T), i32),
            pltpu.SMEM((8, T), i32),
            pltpu.SemaphoreType.DMA,
        ],
        compiler_params=params(VM_ATTEND),
        cost_estimate=cost(1e9 * 6, 6 << 20),
        name="attend",
    )(ids, table, lengths, *parts)


def middle_kernel(heads, gate, slope, grad_mix, mixed, grad_gate, grads):
    whole = jnp.concatenate([heads[h] for h in range(4)], axis=1)
    normed, inverse = norm_rows(whole)
    gates = gate[...].astype(f32)
    mixed[...] = (normed * gates).astype(bf16)
    back = grad_mix[...]
    grad_gate[...] = (back * normed * slope[...].astype(f32)).astype(bf16)
    grad = norm_back(back * gates, normed, inverse).astype(bf16)
    for h in range(4):
        grads[h] = grad[:, h * T : (h + 1) * T]


def middle(heads, gate, slope, grad_mix):
    whole = lambda shape: pl.BlockSpec(shape, lambda i: (0,) * len(shape))
    return pl.pallas_call(
        middle_kernel,
        grid=(1,),
        in_specs=[whole((4, 256, T)), whole((256, 512)), whole((256, 512)), whole((256, 512))],
        out_specs=[whole((256, 512)), whole((256, 512)), whole((4, 256, T))],
        out_shape=[sds((256, 512), bf16), sds((256, 512), bf16), sds((4, 256, T), bf16)],
        compiler_params=params(12),
        cost_estimate=cost(1 << 24, 3 << 20),
        name="middle",
    )(heads, gate, slope, grad_mix)


def output_kernel(ids, tokens, cot, out_proj, mixed, output, mine, *theirs):
    y, z, core, low, x = ids[0], ids[1], ids[2], ids[3] // 4, ids[3] % 4
    output[...] = (
        tokens[...].astype(f32) + jnp.dot(mixed[...], out_proj[...], preferred_element_type=f32)
    ).astype(bf16)
    r = lax.broadcasted_iota(i32, (512, 512), 1)
    c = lax.broadcasted_iota(i32, (512, 512), 0)
    r_x = ((r // 128) + x) % 4
    r_core = ((r // 64) % 2) ^ core
    r_z = (((r // 16) % 4) + z) % 4
    r_y = ((r // 8) % 2) ^ y
    source = (((r // 4) % 2) * 4 + r_x) * 64 + r_y * 32 + r_z * 8 + r_core * 4 + r % 4
    pick = jnp.where(c == source, 1.0, 0.0).astype(bf16)
    moved = jnp.dot(mixed[...], pick, preferred_element_type=f32).astype(bf16)
    part = lax.dot_general(moved, cot[...], TN_DIMS, preferred_element_type=f32)
    mine[...] = part[:T]
    for i in range(3):
        theirs[i][...] = part[(i + 1) * T : (i + 2) * T].astype(bf16)


def finish_output(ids, tokens, cot, out_proj, mixed):
    return pl.pallas_call(
        output_kernel,
        in_specs=[SMEM] + [VMEM] * 4,
        out_specs=[VMEM] * 5,
        out_shape=[sds((256, 1024), bf16), sds((T, 1024), f32)] + [sds((T, 1024), bf16)] * 3,
        compiler_params=params(24),
        cost_estimate=cost(6 * 256 * 512 * 1024, 5 << 20),
        name="finish_output",
    )(ids, in_hbm(tokens), in_hbm(cot), in_hbm(out_proj), mixed)


def backward_kernel(ids, table, lengths, far, near, counts, *refs):
    (keys, values, queries, tk), got_grads, outs = refs[:4], refs[4], refs[5:11]
    mine_s, mine_o, theirs_s, theirs_o, dq_out, rab_out = outs
    tq, start, grads, grads_t, queries_t, dq, dkt, dvt, rab = refs[11:]
    y, z, core = ids[0], ids[1], ids[2]
    stage_times(ids, lengths, tq, tk, start)
    for zz in range(4):
        for half in range(2):
            block = got_grads[zz, half * T : (half + 1) * T, :].astype(f32) * 0.5
            grads[2 * zz + half] = block.astype(bf16)
            grads_t[2 * zz + half] = jnp.transpose(block).astype(bf16)
    for jj in range(QT):
        queries_t[jj] = jnp.transpose(queries[jj].astype(f32)).astype(bf16)
    grads[QT] = jnp.zeros((T, T), bf16)
    grads_t[QT] = jnp.zeros((T, T), bf16)
    queries_t[QT] = jnp.zeros((T, T), bf16)
    dq[...] = jnp.zeros(dq.shape, f32)
    dkt[...] = jnp.zeros(dkt.shape, f32)
    dvt[...] = jnp.zeros(dvt.shape, f32)
    rab[...] = jnp.zeros(rab.shape, f32)

    def fold(values_):
        return jnp.sum(values_.reshape(T // 8, 8, T), axis=0)

    def front(got):
        dots = [lax.dot_general(queries[j], keys[k], NT_DIMS, preferred_element_type=f32) for j, k, _ in got]
        wides = [lax.dot_general(grads[j], values[k], NT_DIMS, preferred_element_type=f32) for j, k, _ in got]
        return dots, wides

    def score(half, wide, keep):
        t = jnp.tanh(half)
        weight = half * t + half
        d_score = wide * ((1.0 + t) * (1.0 + half * (1.0 - t)))
        if keep is not None:
            weight = jnp.where(keep, weight, 0.0)
            d_score = jnp.where(keep, d_score, 0.0)
        return weight.astype(bf16), d_score

    def back(got, weights, scores):
        a = [jnp.dot(scores[u], keys[got[u][1]], preferred_element_type=f32) for u in range(len(got))]
        b = [jnp.dot(queries_t[got[u][0]], scores[u], preferred_element_type=f32) for u in range(len(got))]
        c = [jnp.dot(grads_t[got[u][0]], weights[u], preferred_element_type=f32) for u in range(len(got))]
        for u, (jj, k, _) in enumerate(got):
            dq[jj] += a[u]
            dkt[k] += b[u]
            dvt[k] += c[u]

    def far_step(i, _):
        got = unpack(far, i, FAR_U)
        dots, wides = front(got)
        weights, scores, sums = [], [], []
        for u, (jj, k, bottom) in enumerate(got):
            bias, over1, over2 = bias_far(tq[jj] - tk[k][0:1, :], table, bottom)
            weight, d_score = score(dots[u] * (0.5 * SCALE) + bias, wides[u], None)
            weights.append(weight)
            scores.append(d_score.astype(bf16))
            sums.append((fold(d_score), fold(jnp.where(over1, d_score, 0.0)), fold(jnp.where(over2, d_score, 0.0))))
        back(got, weights, scores)
        for (jj, k, bottom), (sum0, sum1, sum2) in zip(got, sums):
            rab[bottom] += sum0 - sum1
            rab[bottom + 1] += sum1 - sum2
            rab[bottom + 2] += sum2
        return 0

    def near_step(i, _):
        got = unpack(near, i, NEAR_U)
        dots, wides = front(got)
        weights, scores = [], []
        sums = [jnp.zeros((8, T), f32)] * BUCKETS
        for u, (jj, k, _) in enumerate(got):
            gap = tq[jj] - tk[k][0:1, :]
            half = dots[u] * (0.5 * SCALE) + bias_near(gap, table)
            weight, d_score = score(half, wides[u], keep_near(ids, start[jj], jj, k))
            weights.append(weight)
            scores.append(d_score.astype(bf16))
            sums[0] = sums[0] + fold(d_score)
            for j in range(1, BUCKETS):
                sums[j] = sums[j] + fold(jnp.where(gap >= float(2**j - 1), d_score, 0.0))
        back(got, weights, scores)
        for j in range(BUCKETS - 1):
            rab[j] += sums[j] - sums[j + 1]
        rab[BUCKETS - 1] += sums[BUCKETS - 1]
        return 0

    lax.fori_loop(0, counts[0], far_step, 0)
    lax.fori_loop(0, counts[1], near_step, 0)
    for other in range(2):
        for s in range(4):
            base = (y if other == 0 else 1 - y) * 8 + ((z + s) % 4) * 2
            for side in range(2):
                dev = base + (core if side == 0 else 1 - core)
                ref = ((mine_s, theirs_s), (mine_o, theirs_o))[other][side]
                for half in range(2):
                    tile = dev if half == 0 else 2 * DEVS - 1 - dev
                    ref[s, 0:T, half * T : (half + 1) * T] = (dkt[tile] * SCALE).astype(bf16)
                    ref[s, T:, half * T : (half + 1) * T] = (dvt[tile] * 2.0).astype(bf16)
    for s in range(4):
        zz = (z + s) % 4
        for half in range(2):
            dq_out[s, :, half * T : (half + 1) * T] = (dq[2 * zz + half] * SCALE).astype(bf16)
    for b in range(16):
        if b < BUCKETS:
            rab_out[b : b + 1, :] = jnp.sum(rab[b], axis=0, keepdims=True)
        else:
            rab_out[b : b + 1, :] = jnp.zeros((1, T), f32)


def attend_back(ids, table, lengths, saved, grads):
    return pl.pallas_call(
        backward_kernel,
        in_specs=[SMEM] * 6 + [VMEM] * 5,
        out_specs=[VMEM] * 6,
        out_shape=[sds((4, 256, 256), bf16)] * 4 + [sds((4, T, 256), bf16), sds((16, T), f32)],
        scratch_shapes=STAGE
        + [
            pltpu.VMEM((QT + 1, T, T), bf16),
            pltpu.VMEM((QT + 1, T, T), bf16),
            pltpu.VMEM((QT + 1, T, T), bf16),
            pltpu.VMEM((QT + 1, T, T), f32),
            pltpu.VMEM((TILES + 1, T, T), f32),
            pltpu.VMEM((TILES + 1, T, T), f32),
            pltpu.VMEM((16, 8, T), f32),
        ],
        compiler_params=params(VM_BACK),
        cost_estimate=cost(1e9 * 12, 8 << 20),
        name="attend_back",
    )(ids, table, lengths, *saved[:3], *[in_hbm(part) for part in saved[3:]], grads)


def combine_kernel(mine_s, mine_o, got_s, got_o, dq, proj_own, proj_got, rab, rab_got, *outs):
    proj = proj_own[...] + proj_got[...].astype(f32)
    both = rab[...] + rab_got[...]
    high = both.astype(bf16)
    low = (both - high.astype(f32)).astype(bf16)
    for s in range(4):
        outs[s][0:256, :] = (mine_s[s].astype(f32) + got_s[s].astype(f32)).astype(bf16)
        outs[s][256:384, :] = dq[s]
        outs[4 + s][0:256, :] = (mine_o[s].astype(f32) + got_o[s].astype(f32)).astype(bf16)
        for other in range(2):
            block = proj[s * 16 + other * 8 : s * 16 + other * 8 + 8, :]
            block = jnp.concatenate([block[:, c * 256 : (c + 1) * 256] for c in range(4)], axis=0)
            base = 384 - 128 * other
            outs[4 * other + s][base : base + 32, :] = block.astype(bf16)
            outs[4 * other + s][base + 32 :, 0:T] = high
            outs[4 * other + s][base + 32 :, T:] = low


def combine(*parts):
    return pl.pallas_call(
        combine_kernel,
        in_specs=[VMEM] * 9,
        out_specs=[VMEM] * 8,
        out_shape=[sds((432, 256), bf16)] * 4 + [sds((304, 256), bf16)] * 4,
        compiler_params=params(24),
        cost_estimate=cost(1 << 20, 5 << 20),
        name="combine",
    )(*parts)


def collect_kernel(ids, *refs):
    ins, rabs, out = refs[:8], refs[8:16], refs[16]
    total = ins[0][...].astype(f32)
    for ref in ins[1:]:
        total = total + ref[...].astype(f32)
    for d in range(8):
        for c in range(4):
            rows = total[c * 8 + (d // 4) * 4 : c * 8 + (d // 4) * 4 + 4, :]
            out[d, 0:4, c * 256 : (c + 1) * 256] = jnp.where(ids[3] % 4 == d % 4, rows, 0.0)
    lane = lax.broadcasted_iota(i32, (16, T), 1)
    table = jnp.zeros((16, T), f32)
    for t in range(4):
        near, far = rabs[t][...].astype(f32), rabs[4 + t][...].astype(f32)
        near, far = near[:, :T] + near[:, T:], far[:, :T] + far[:, T:]
        first, second = jnp.where(ids[0] == 0, near, far), jnp.where(ids[0] == 0, far, near)
        head = (ids[1] + 4 - t) % 4
        table = jnp.where(lane == head, jnp.sum(first + second, axis=1, keepdims=True), table)
    turned = jnp.transpose(jnp.concatenate([table, jnp.zeros((T - 16, T), f32)], axis=0))
    for d in range(8):
        out[d, 4:, :T] = turned[0:4]
        out[d, 4:, T:] = jnp.zeros((4, 1024 - T), f32)


def collect(ids, same, other):
    return pl.pallas_call(
        collect_kernel,
        grid=(1,),
        in_specs=[SMEM]
        + [pl.BlockSpec((32, 256), lambda i: (12, 0))] * 4
        + [pl.BlockSpec((32, 256), lambda i: (8, 0))] * 4
        + [pl.BlockSpec((16, 256), lambda i: (26, 0))] * 4
        + [pl.BlockSpec((16, 256), lambda i: (18, 0))] * 4,
        out_specs=pl.BlockSpec((8, 8, 1024), lambda i: (0, 0, 0)),
        out_shape=sds((8, 8, 1024), f32),
        compiler_params=params(8),
        cost_estimate=cost(1 << 16, 1 << 18),
        name="collect",
    )(ids, *same, *other, *same, *other)


def final_kernel(ids, grad_gate, in_proj_hbm, tokens_hbm, cot_hbm, slope_hbm, *refs):
    same, other, grad_in = refs[:4], refs[4:8], refs[8]
    grad_pre, in_proj, tokens, cot, slope, sems = refs[9:]
    z = ids[1]
    first = pltpu.make_async_copy(slope_hbm, slope, sems.at[4])
    weights = [
        pltpu.make_async_copy(in_proj_hbm.at[pl.ds(i * 256, 256)], in_proj.at[i], sems.at[i])
        for i in range(4)
    ]
    lasts = [
        pltpu.make_async_copy(tokens_hbm, tokens, sems.at[5]),
        pltpu.make_async_copy(cot_hbm, cot, sems.at[6]),
    ]
    for copy in [first] + weights + lasts:
        copy.start()
    grad_pre[:, 0:512] = grad_gate[...]
    first.wait()
    for t in range(4):
        head = (z + 4 - t) % 4
        column = lambda kind: pl.ds(pl.multiple_of(kind * 512 + head * T, T), T)
        total = same[t][0:256, :].astype(f32) + other[t][0:256, :].astype(f32)
        for half in range(2):
            rows = slice(half * T, (half + 1) * T)
            key = jnp.transpose(total[0:T, rows])
            value = jnp.transpose(total[T:, rows])
            query = same[t][256:384, rows].astype(f32)
            for kind, part in ((1, value), (2, query), (3, key)):
                grad_pre[rows, column(kind)] = (
                    part * slope[rows, column(kind)].astype(f32)
                ).astype(bf16)
    parts = []
    for i in range(4):
        weights[i].wait()
        parts.append(
            lax.dot_general(grad_pre[...], in_proj[i], NT_DIMS, preferred_element_type=f32)
        )
    for copy in lasts:
        copy.wait()
    normed, inverse = norm_rows(tokens[...].astype(f32))
    upstream = jnp.concatenate(parts, axis=1)
    grad_in[...] = (cot[...].astype(f32) + norm_back(upstream, normed, inverse)).astype(bf16)


def finish_grad(ids, tokens, cot, in_proj, slope, grad_gate, same, other):
    whole = lambda shape: pl.BlockSpec(shape, lambda s: (0,) * len(shape))
    hbm = pl.BlockSpec(memory_space=pltpu.HBM)
    return pl.pallas_call(
        final_kernel,
        grid=(1,),
        in_specs=[SMEM, whole((256, 512)), hbm, hbm, hbm, hbm]
        + [whole((384, 256))] * 4
        + [whole((256, 256))] * 4,
        out_specs=whole((256, 1024)),
        out_shape=sds((256, 1024), bf16),
        scratch_shapes=[
            pltpu.VMEM((256, 2048), bf16),
            pltpu.VMEM((4, 256, 2048), bf16),
            pltpu.VMEM((256, 1024), bf16),
            pltpu.VMEM((256, 1024), bf16),
            pltpu.VMEM((256, 2048), bf16),
            pltpu.SemaphoreType.DMA((7,)),
        ],
        compiler_params=params(56),
        cost_estimate=cost(2 * 256 * 1024 * 2048, 8 << 20),
        name="finish_grad",
    )(ids, grad_gate, in_proj, tokens, cot, slope, *same, *other)


def move(y_xor, z_shift, core_xor):
    pairs = []
    for dev in range(DEVS):
        y, z, core = dev // 8, (dev // 2) % 4, dev % 2
        target = (y ^ y_xor) * 8 + ((z + z_shift) % 4) * 2 + (core ^ core_xor)
        pairs.append((dev, target))
    return pairs


def send(x, y_xor, z_shift, core_xor):
    return lax.ppermute(x, "ctx", move(y_xor, z_shift, core_xor))


OVER_Z = [[y * 8 + z * 2 + c for z in range(4)] for y in range(2) for c in range(2)]
OVER_X = [[low * 4 + x for x in range(4)] for low in range(2)]


def send_x(part, shift):
    return lax.ppermute(part, "dp", [(d, d // 4 * 4 + (d + shift) % 4) for d in range(8)])


def swap_z(part):
    return lax.all_to_all(part, "ctx", 0, 0, axis_index_groups=OVER_Z, tiled=True)


def on_device(tokens, cotangent, in_proj, out_proj, rab_time, seq_lengths, block_mask, time_bucket):
    ctx = lax.axis_index("ctx")
    y, z, core = ctx // 8, (ctx // 2) % 4, ctx % 2
    times = jnp.stack([time_bucket // T, time_bucket % T]).astype(bf16)
    near_tokens = jnp.concatenate([tokens, jnp.pad(times, ((0, 14), (0, 768)))], axis=0)
    far_tokens = send(near_tokens, 1, 0, 0)
    full = project(near_tokens, in_proj, block_mask)
    own = [full[0]] + [send(full[s], 0, s, 0) for s in (1, 2, 3)]
    pairs = project(far_tokens, in_proj)
    own, pairs = lax.optimization_barrier((own, pairs))
    across = [pairs[0]] + [send(pairs[s], 0, s, 0) for s in (1, 2, 3)]
    gate, slope, grad_mix = make_gates(tokens, in_proj, cotangent, out_proj)
    own_twin = [send(part, 0, 0, 1) for part in own]
    across_twin = [send(part, 0, 0, 1) for part in across]
    parts = own + own_twin + across + across_twin

    ids = jnp.stack([y, z, core, lax.axis_index("dp")]).astype(i32)
    lengths = seq_lengths.reshape(3)
    limits = [2.0**j - 1.0 for j in range(BUCKETS)] + [1e9] * 4
    head_bias = lax.dynamic_slice_in_dim(rab_time, z, 1, 1).reshape(BUCKETS) * 0.5
    table = jnp.concatenate([head_bias, jnp.zeros((4,), f32), jnp.array(limits, f32)])
    heads, *saved = attend(ids, table, lengths, parts)

    mixed, grad_gate, grads = middle(swap_z(heads), gate, slope, grad_mix)
    grads = swap_z(grads)
    output, proj, *proj_x = finish_output(ids, tokens, cotangent, out_proj, mixed)
    grads, proj_x = lax.optimization_barrier((grads, proj_x))
    proj_x = [send_x(proj_x[s - 1], s) for s in (1, 2, 3)]

    mine_s, mine_o, theirs_s, theirs_o, dq, rab = attend_back(ids, table, lengths, saved, grads)
    got_o = send(theirs_o, 0, 0, 1)
    got_s = send(theirs_s, 0, 0, 1)
    rab_got = send(rab, 0, 0, 1)
    for part in proj_x:
        proj = proj + part.astype(f32)
    proj_own, proj_got = proj[:64], send(proj[64:].astype(bf16), 0, 0, 1)
    messages = combine(mine_s, mine_o, got_s, got_o, dq, proj_own, proj_got, rab, rab_got)
    same = [messages[0]] + [send(messages[s], 0, s, 0) for s in (1, 2, 3)]
    other = [send(messages[4 + s], 1, s, 0) for s in range(4)]
    lines = lax.all_to_all(collect(ids, same, other), "dp", 0, 0, tiled=True)
    sums = jnp.sum(lines, axis=0)
    grad_in = finish_grad(ids, tokens, cotangent, in_proj, slope, grad_gate, same, other)
    return output, grad_in, sums[:4], sums[4:, :BUCKETS].T


def solution(mesh):
    rows = P(("dp", "ctx"), None)
    placed = (rows, rows, P(), P(), P(), P("dp", None), P("dp", "ctx", None), P(("dp", "ctx")))
    return jax.shard_map(
        on_device,
        mesh=mesh,
        in_specs=placed,
        out_specs=(rows, rows, rows, P()),
        check_vma=False,
    )
```

```python
import functools
import math

import jax
import jax.numpy as jnp
from jax import lax
from jax.experimental import pallas as pl
from jax.experimental.pallas import tpu as pltpu
from jax.sharding import PartitionSpec as P

f32 = jnp.float32
bf16 = jnp.bfloat16
i32 = jnp.int32
T = 128
EPS = 1e-05
HEADS = 4
BUCKETS = 12
DEVS = 16
TILES = 32
QT = 8
SCALE = 1.0 / math.sqrt(128.0)
LIST = 160
FAR_U = 8
NEAR_U = 4
NEAR_FLAG = 32768
DUMMY = QT + 16 * TILES
VM_ATTEND = 20
VM_BACK = 24
VMEM = pl.BlockSpec(memory_space=pltpu.VMEM)
SMEM = pl.BlockSpec(memory_space=pltpu.SMEM)
NT_DIMS = (((1,), (1,)), ((), ()))
TN_DIMS = (((0,), (0,)), ((), ()))


def params(mib=24):
    return pltpu.CompilerParams(vmem_limit_bytes=mib * 1024 * 1024)


def cost(flops, size):
    return pl.CostEstimate(flops=int(flops), bytes_accessed=int(size), transcendentals=0)


def sds(shape, dtype):
    return jax.ShapeDtypeStruct(shape, dtype)


def norm_rows(values):
    centre = jnp.mean(values, axis=-1, keepdims=True)
    shifted = values - centre
    spread = jnp.mean(shifted * shifted, axis=-1, keepdims=True)
    inverse = lax.rsqrt(spread + EPS)
    return shifted * inverse, inverse


def norm_back(upstream, normed, inverse):
    first = jnp.mean(upstream, axis=-1, keepdims=True)
    second = jnp.mean(upstream * normed, axis=-1, keepdims=True)
    return inverse * (upstream - first - normed * second)


def in_hbm(part):
    return pltpu.with_memory_space_constraint(part, pltpu.HBM)


def project_kernel(own, tokens, *refs):
    weights, outs, normed = refs[own : 2 * own + 2], refs[2 * own + 2 : -1], refs[-1]
    head = pl.program_id(0)
    shift = (head + 4 - (lax.axis_index("ctx") // 2) % 4) % 4

    @pl.when(head == 0)
    def _():
        normed[...] = norm_rows(tokens[0:256, :].astype(f32))[0].astype(bf16)

    wide = jnp.concatenate([w[...] for w in weights], axis=1)
    half = 0.5 * jnp.dot(normed[...], wide, preferred_element_type=f32)
    act = (half * jnp.tanh(half) + half).astype(bf16)
    meta = tokens[256:, 0:256]
    if own:
        mask, blank = refs[0], jnp.zeros((1, T - TILES), f32)
        row = [mask[0, 0:1].astype(f32), blank, mask[0, 1:2].astype(f32), blank]
        rows = [meta[0:2].astype(f32), jnp.concatenate(row, axis=1), jnp.zeros((13, 256), f32)]
        meta = jnp.concatenate(rows, axis=0).astype(bf16)
    for which in range(4):

        @pl.when(shift == which)
        def _(which=which):
            outs[which][0:256, :] = act
            outs[which][256:, 0:256] = meta
            if own:
                outs[which][256:, 256:] = jnp.zeros((16, T), bf16)


def project(tokens, in_proj, mask=None):
    own = mask is not None
    width = 384 if own else 256

    def column(kind):
        return pl.BlockSpec((1024, T), lambda h: (0, kind * HEADS + h))

    whole = lambda shape: pl.BlockSpec(shape, lambda h: (0,) * len(shape))
    kinds = (3, 1, 2) if own else (3, 1)
    return pl.pallas_call(
        functools.partial(project_kernel, int(own)),
        grid=(HEADS,),
        in_specs=[whole((272, 1024))] + [whole((1, 2, TILES))] * own + [column(kind) for kind in kinds],
        out_specs=[whole((272, width))] * 4,
        out_shape=[sds((272, width), bf16)] * 4,
        scratch_shapes=[pltpu.VMEM((256, 1024), bf16)],
        compiler_params=params(12),
        cost_estimate=cost(2 * 256 * 1024 * 4 * width, 5 << 20),
        name="project_own" if own else "project_other",
    )(tokens, *([in_hbm(mask)] if own else []), *[in_hbm(in_proj)] * len(kinds))


def gates_kernel(tokens, in_proj, cot, out_proj, gate, slope, grad_mix, normed):
    kind = pl.program_id(0)

    @pl.when(kind == 0)
    def _():
        normed[...] = norm_rows(tokens[...].astype(f32))[0].astype(bf16)
        grad_mix[...] = lax.dot_general(cot[...], out_proj[...], NT_DIMS, preferred_element_type=f32)

    pre = jnp.dot(normed[...], in_proj[...], preferred_element_type=f32)
    sig = 0.5 * jnp.tanh(0.5 * pre) + 0.5
    slope[...] = (sig * (1.0 + pre * (1.0 - sig))).astype(bf16)

    @pl.when(kind == 0)
    def _():
        gate[...] = (pre * sig).astype(bf16)


def make_gates(tokens, in_proj, cot, out_proj):
    whole = lambda shape: pl.BlockSpec(shape, lambda s: (0,) * len(shape))
    return pl.pallas_call(
        gates_kernel,
        grid=(4,),
        in_specs=[
            whole((256, 1024)),
            pl.BlockSpec((1024, 512), lambda s: (0, s)),
            whole((256, 1024)),
            whole((512, 1024)),
        ],
        out_specs=[whole((256, 512)), pl.BlockSpec((256, 512), lambda s: (0, s)), whole((256, 512))],
        out_shape=[
            pltpu.VMEM((256, 512), bf16),
            pltpu.VMEM((256, 2048), bf16),
            pltpu.VMEM((256, 512), f32),
        ],
        scratch_shapes=[pltpu.VMEM((256, 1024), bf16)],
        compiler_params=params(16),
        cost_estimate=cost(2 * 256 * 1024 * 2048, 7 << 20),
        name="gates",
    )(in_hbm(tokens), in_hbm(in_proj), in_hbm(cot), in_hbm(out_proj))


def bias_far(gap, table, bottom):
    first = table[bottom]
    second = table[bottom + 1]
    third = table[bottom + 2]
    limit1 = table[16 + bottom + 1]
    limit2 = table[16 + bottom + 2]
    over1 = gap >= limit1
    over2 = gap >= limit2
    return jnp.where(over2, third, jnp.where(over1, second, first)), over1, over2


def bias_near(gap, table):
    bias = jnp.full(gap.shape, table[0], f32)
    for j in range(1, BUCKETS):
        bias = jnp.where(gap >= float(2**j - 1), table[j], bias)
    return bias


def keep_near(ids, start, jj, k):
    tile = query_tile(ids, jj)
    row = lax.broadcasted_iota(i32, (T, T), 0)
    col = lax.broadcasted_iota(i32, (T, T), 1)
    later = (col - row) <= (tile - k) * T
    return later & ((col + k * T) >= start)


STAGE = [pltpu.VMEM((QT + 1, T, T), f32), pltpu.VMEM((QT + 1, T, T), i32)]


def query_tile(ids, jj):
    dev = ids[0] * 8 + (jj // 2) * 2 + ids[2]
    return jnp.where(jj % 2 == 0, dev, 2 * DEVS - 1 - dev)


def starts_of(lengths, pos):
    end0 = lengths[0]
    end1 = lengths[0] + lengths[1]
    return jnp.where(pos >= end1, end1, jnp.where(pos >= end0, end0, 0))


def stage(ids, ins, keys, values, queries, tk, flags, times):
    y, z, core = ids[0], ids[1], ids[2]
    for group in range(4):
        for t in range(4):
            ref = ins[group * 4 + t]
            zz = (z + 4 - t) % 4
            dev = (y if group < 2 else 1 - y) * 8 + zz * 2 + (core if group % 2 == 0 else 1 - core)
            keys[dev] = ref[0:T, 0:T]
            values[dev] = ref[0:T, T : 2 * T]
            keys[2 * DEVS - 1 - dev] = ref[T : 2 * T, 0:T]
            values[2 * DEVS - 1 - dev] = ref[T : 2 * T, T : 2 * T]
            head = ref[256:272, 0:256].astype(f32)
            moments = head[0:1] * 128.0 + head[1:2]
            tk[dev] = jnp.broadcast_to(moments[:, :T], (8, T))
            tk[2 * DEVS - 1 - dev] = jnp.broadcast_to(moments[:, T:], (8, T))
            times[pl.ds(dev, 1), :] = moments[:, :T]
            times[pl.ds(2 * DEVS - 1 - dev, 1), :] = moments[:, T:]
            if group == 0:
                queries[2 * zz] = ref[0:T, 2 * T :]
                queries[2 * zz + 1] = ref[T : 2 * T, 2 * T :]
                flags[pl.ds(2 * zz, 1), :] = head[2:3, :T]
                flags[pl.ds(2 * zz + 1, 1), :] = head[2:3, T:]
    keys[TILES] = jnp.zeros((T, T), bf16)
    values[TILES] = jnp.zeros((T, T), bf16)
    queries[QT] = jnp.zeros((T, T), bf16)
    tk[TILES] = jnp.zeros((8, T), f32)


def stage_times(ids, lengths, tq, tk, start):
    tq[QT] = jnp.zeros((T, T), f32)
    start[QT] = jnp.zeros((T, T), i32)
    rows = lax.broadcasted_iota(i32, (T, T), 0)
    for jj in range(QT):
        tile = query_tile(ids, jj)
        tq[jj] = jnp.transpose(jnp.broadcast_to(tk[tile][0:1, :], (T, T)))
        start[jj] = starts_of(lengths, rows + tile * T)


def make_lists(ids, lengths, flags, times, q_times, codes, codes_smem, sem, far, near, counts):
    def level(gap):
        total = jnp.zeros(gap.shape, i32)
        for j in range(1, BUCKETS):
            total = total + jnp.where(gap >= float(2**j - 1), 1, 0)
        return total

    for jj in range(QT):
        q_times[jj : jj + 1, :] = times[pl.ds(query_tile(ids, jj), 1), :]
    turned = jnp.transpose(times[...])
    k_first, k_last = turned[0:1, :], turned[T - 1 :, :]
    q_first, q_last = q_times[:, 0:1], q_times[:, T - 1 :]
    jj = lax.broadcasted_iota(i32, (8, T), 0)
    kk = lax.broadcasted_iota(i32, (8, T), 1)
    tile = query_tile(ids, jj)
    low = starts_of(lengths, tile * T)
    high = starts_of(lengths, tile * T + T - 1)
    bottom = level(jnp.maximum(q_first - k_last, 0.0))
    top = level(q_last - k_first)
    row = lax.broadcasted_iota(i32, (T, T), 0)
    col = lax.broadcasted_iota(i32, (T, T), 1)
    turn = jnp.where(row == jnp.where(col < DEVS, 2 * col, 4 * DEVS - 1 - 2 * col), 1.0, 0.0).astype(bf16)
    ordered = jnp.dot(flags[...].astype(bf16), turn, preferred_element_type=f32)
    allowed = (ordered > 0.5) & (kk <= tile) & (kk * T + T - 1 >= low)
    plain = (kk < tile) & (kk * T >= high) & (top - bottom <= 2)
    entry = jj + 16 * kk
    codes[...] = jnp.where(
        allowed, jnp.where(plain, entry + 1024 * bottom, entry + NEAR_FLAG), -1
    )
    copy = pltpu.make_async_copy(codes, codes_smem, sem)
    copy.start()
    copy.wait()

    def query_step(jj, sizes):
        tile = query_tile(ids, jj)

        def key_step(k, sizes):
            n_far, n_near = sizes
            code = codes_smem[jj, k]
            far[n_far] = code
            near[n_near] = code & (NEAR_FLAG - 1)
            is_near = code >= NEAR_FLAG
            is_far = (code >= 0) & jnp.logical_not(is_near)
            return n_far + is_far.astype(i32), n_near + is_near.astype(i32)

        return lax.fori_loop(starts_of(lengths, tile * T) // T, tile + 1, key_step, sizes)

    n_far, n_near = lax.fori_loop(0, QT, query_step, (jnp.int32(0), jnp.int32(0)))
    for pad in range(FAR_U):
        far[n_far + pad] = DUMMY
    for pad in range(NEAR_U):
        near[n_near + pad] = DUMMY
    counts[0] = (n_far + FAR_U - 1) // FAR_U
    counts[1] = (n_near + NEAR_U - 1) // NEAR_U


def unpack(ref, i, count):
    got = []
    for u in range(count):
        entry = ref[i * count + u]
        got.append((entry & 15, (entry >> 4) & 63, entry >> 10))
    return got


def forward_kernel(ids, table, lengths, *refs):
    ins, (out, far, near, counts, keys, values, queries, tk) = refs[:16], refs[16:24]
    tq, start, acc, flags, times, q_times, codes, codes_smem, sem = refs[24:]
    times[...] = jnp.zeros(times.shape, f32)
    stage(ids, ins, keys, values, queries, tk, flags, times)
    stage_times(ids, lengths, tq, tk, start)
    make_lists(ids, lengths, flags, times, q_times, codes, codes_smem, sem, far, near, counts)
    acc[...] = jnp.zeros(acc.shape, f32)

    def far_step(i, _):
        got = unpack(far, i, FAR_U)
        dots = [lax.dot_general(queries[j], keys[k], NT_DIMS, preferred_element_type=f32) for j, k, _ in got]
        weights = []
        for u, (jj, k, bottom) in enumerate(got):
            bias, _, _ = bias_far(tq[jj] - tk[k][0:1, :], table, bottom)
            half = dots[u] * (0.5 * SCALE) + bias
            weights.append((half * jnp.tanh(half) + half).astype(bf16))
        adds = [jnp.dot(weights[u], values[got[u][1]], preferred_element_type=f32) for u in range(len(got))]
        for u in range(len(got)):
            acc[got[u][0]] += adds[u]
        return 0

    def near_step(i, _):
        got = unpack(near, i, NEAR_U)
        dots = [lax.dot_general(queries[j], keys[k], NT_DIMS, preferred_element_type=f32) for j, k, _ in got]
        weights = []
        for u, (jj, k, _) in enumerate(got):
            half = dots[u] * (0.5 * SCALE) + bias_near(tq[jj] - tk[k][0:1, :], table)
            weight = half * jnp.tanh(half) + half
            weights.append(jnp.where(keep_near(ids, start[jj], jj, k), weight, 0.0).astype(bf16))
        adds = [jnp.dot(weights[u], values[got[u][1]], preferred_element_type=f32) for u in range(len(got))]
        for u in range(len(got)):
            acc[got[u][0]] += adds[u]
        return 0

    lax.fori_loop(0, counts[0], far_step, 0)
    lax.fori_loop(0, counts[1], near_step, 0)
    for zz in range(4):
        out[zz, 0:T] = acc[2 * zz]
        out[zz, T:] = acc[2 * zz + 1]


def attend(ids, table, lengths, parts):
    return pl.pallas_call(
        forward_kernel,
        in_specs=[SMEM] * 3 + [VMEM] * 16,
        out_specs=[VMEM] + [SMEM] * 3 + [VMEM] * 4,
        out_shape=[sds((4, 256, T), f32), sds((LIST,), i32), sds((LIST,), i32), sds((8,), i32)]
        + [pltpu.HBM((TILES + 1, T, T), bf16)] * 2
        + [pltpu.HBM((QT + 1, T, T), bf16), pltpu.HBM((TILES + 1, 8, T), f32)],
        scratch_shapes=STAGE
        + [
            pltpu.VMEM((QT + 1, T, T), f32),
            pltpu.VMEM((8, T), f32),
            pltpu.VMEM((T, T), f32),
            pltpu.VMEM((8, T), f32),
            pltpu.VMEM((8, T), i32),
            pltpu.SMEM((8, T), i32),
            pltpu.SemaphoreType.DMA,
        ],
        compiler_params=params(VM_ATTEND),
        cost_estimate=cost(1e9 * 6, 6 << 20),
        name="attend",
    )(ids, table, lengths, *parts)


def middle_kernel(heads, gate, slope, grad_mix, mixed, grad_gate, grads):
    whole = jnp.concatenate([heads[h] for h in range(4)], axis=1)
    normed, inverse = norm_rows(whole)
    gates = gate[...].astype(f32)
    mixed[...] = (normed * gates).astype(bf16)
    back = grad_mix[...]
    grad_gate[...] = (back * normed * slope[...].astype(f32)).astype(bf16)
    grad = norm_back(back * gates, normed, inverse).astype(bf16)
    for h in range(4):
        grads[h] = grad[:, h * T : (h + 1) * T]


def middle(heads, gate, slope, grad_mix):
    whole = lambda shape: pl.BlockSpec(shape, lambda i: (0,) * len(shape))
    return pl.pallas_call(
        middle_kernel,
        grid=(1,),
        in_specs=[whole((4, 256, T)), whole((256, 512)), whole((256, 512)), whole((256, 512))],
        out_specs=[whole((256, 512)), whole((256, 512)), whole((4, 256, T))],
        out_shape=[
            pltpu.HBM((256, 512), bf16),
            pltpu.HBM((256, 512), bf16),
            sds((4, 256, T), bf16),
        ],
        compiler_params=params(12),
        cost_estimate=cost(1 << 24, 3 << 20),
        name="middle",
    )(heads, gate, slope, grad_mix)


def output_kernel(ids, tokens, cot, out_proj, mixed, output, mine, *theirs):
    y, z, core, low, x = ids[0], ids[1], ids[2], ids[3] // 4, ids[3] % 4
    output[...] = (
        tokens[...].astype(f32) + jnp.dot(mixed[...], out_proj[...], preferred_element_type=f32)
    ).astype(bf16)
    r = lax.broadcasted_iota(i32, (512, 512), 1)
    c = lax.broadcasted_iota(i32, (512, 512), 0)
    r_x = ((r // 128) + x) % 4
    r_core = ((r // 64) % 2) ^ core
    r_z = (((r // 16) % 4) + z) % 4
    r_y = ((r // 8) % 2) ^ y
    source = (((r // 4) % 2) * 4 + r_x) * 64 + r_y * 32 + r_z * 8 + r_core * 4 + r % 4
    pick = jnp.where(c == source, 1.0, 0.0).astype(bf16)
    moved = jnp.dot(mixed[...], pick, preferred_element_type=f32).astype(bf16)
    part = lax.dot_general(moved, cot[...], TN_DIMS, preferred_element_type=f32)
    mine[...] = part[:T]
    for i in range(3):
        theirs[i][...] = part[(i + 1) * T : (i + 2) * T].astype(bf16)


def finish_output(ids, tokens, cot, out_proj, mixed):
    return pl.pallas_call(
        output_kernel,
        in_specs=[SMEM] + [VMEM] * 4,
        out_specs=[VMEM] * 5,
        out_shape=[sds((256, 1024), bf16), sds((T, 1024), f32)] + [sds((T, 1024), bf16)] * 3,
        compiler_params=params(24),
        cost_estimate=cost(6 * 256 * 512 * 1024, 5 << 20),
        name="finish_output",
    )(ids, in_hbm(tokens), in_hbm(cot), in_hbm(out_proj), in_hbm(mixed))


def backward_kernel(ids, table, lengths, far, near, counts, *refs):
    (keys, values, queries, tk), got_grads, outs = refs[:4], refs[4], refs[5:11]
    mine_s, mine_o, theirs_s, theirs_o, dq_out, rab_out = outs
    tq, start, grads, grads_t, queries_t, dq, dkt, dvt, rab = refs[11:]
    y, z, core = ids[0], ids[1], ids[2]
    stage_times(ids, lengths, tq, tk, start)
    for zz in range(4):
        for half in range(2):
            block = got_grads[zz, half * T : (half + 1) * T, :].astype(f32) * 0.5
            grads[2 * zz + half] = block.astype(bf16)
            grads_t[2 * zz + half] = jnp.transpose(block).astype(bf16)
    for jj in range(QT):
        queries_t[jj] = jnp.transpose(queries[jj].astype(f32)).astype(bf16)
    grads[QT] = jnp.zeros((T, T), bf16)
    grads_t[QT] = jnp.zeros((T, T), bf16)
    queries_t[QT] = jnp.zeros((T, T), bf16)
    dq[...] = jnp.zeros(dq.shape, f32)
    dkt[...] = jnp.zeros(dkt.shape, f32)
    dvt[...] = jnp.zeros(dvt.shape, f32)
    rab[...] = jnp.zeros(rab.shape, f32)

    def fold(values_):
        return jnp.sum(values_.reshape(T // 8, 8, T), axis=0)

    def front(got):
        dots = [lax.dot_general(queries[j], keys[k], NT_DIMS, preferred_element_type=f32) for j, k, _ in got]
        wides = [lax.dot_general(grads[j], values[k], NT_DIMS, preferred_element_type=f32) for j, k, _ in got]
        return dots, wides

    def score(half, wide, keep):
        t = jnp.tanh(half)
        weight = half * t + half
        d_score = wide * ((1.0 + t) * (1.0 + half * (1.0 - t)))
        if keep is not None:
            weight = jnp.where(keep, weight, 0.0)
            d_score = jnp.where(keep, d_score, 0.0)
        return weight.astype(bf16), d_score

    def back(got, weights, scores):
        a = [jnp.dot(scores[u], keys[got[u][1]], preferred_element_type=f32) for u in range(len(got))]
        b = [jnp.dot(queries_t[got[u][0]], scores[u], preferred_element_type=f32) for u in range(len(got))]
        c = [jnp.dot(grads_t[got[u][0]], weights[u], preferred_element_type=f32) for u in range(len(got))]
        for u, (jj, k, _) in enumerate(got):
            dq[jj] += a[u]
            dkt[k] += b[u]
            dvt[k] += c[u]

    def far_step(i, _):
        got = unpack(far, i, FAR_U)
        dots, wides = front(got)
        weights, scores, sums = [], [], []
        for u, (jj, k, bottom) in enumerate(got):
            bias, over1, over2 = bias_far(tq[jj] - tk[k][0:1, :], table, bottom)
            weight, d_score = score(dots[u] * (0.5 * SCALE) + bias, wides[u], None)
            weights.append(weight)
            scores.append(d_score.astype(bf16))
            sums.append((fold(d_score), fold(jnp.where(over1, d_score, 0.0)), fold(jnp.where(over2, d_score, 0.0))))
        back(got, weights, scores)
        for (jj, k, bottom), (sum0, sum1, sum2) in zip(got, sums):
            rab[bottom] += sum0 - sum1
            rab[bottom + 1] += sum1 - sum2
            rab[bottom + 2] += sum2
        return 0

    def near_step(i, _):
        got = unpack(near, i, NEAR_U)
        dots, wides = front(got)
        weights, scores = [], []
        sums = [jnp.zeros((8, T), f32)] * BUCKETS
        for u, (jj, k, _) in enumerate(got):
            gap = tq[jj] - tk[k][0:1, :]
            half = dots[u] * (0.5 * SCALE) + bias_near(gap, table)
            weight, d_score = score(half, wides[u], keep_near(ids, start[jj], jj, k))
            weights.append(weight)
            scores.append(d_score.astype(bf16))
            sums[0] = sums[0] + fold(d_score)
            for j in range(1, BUCKETS):
                sums[j] = sums[j] + fold(jnp.where(gap >= float(2**j - 1), d_score, 0.0))
        back(got, weights, scores)
        for j in range(BUCKETS - 1):
            rab[j] += sums[j] - sums[j + 1]
        rab[BUCKETS - 1] += sums[BUCKETS - 1]
        return 0

    lax.fori_loop(0, counts[0], far_step, 0)
    lax.fori_loop(0, counts[1], near_step, 0)
    for other in range(2):
        for s in range(4):
            base = (y if other == 0 else 1 - y) * 8 + ((z + s) % 4) * 2
            for side in range(2):
                dev = base + (core if side == 0 else 1 - core)
                ref = ((mine_s, theirs_s), (mine_o, theirs_o))[other][side]
                for half in range(2):
                    tile = dev if half == 0 else 2 * DEVS - 1 - dev
                    ref[s, 0:T, half * T : (half + 1) * T] = (dkt[tile] * SCALE).astype(bf16)
                    ref[s, T:, half * T : (half + 1) * T] = (dvt[tile] * 2.0).astype(bf16)
    for s in range(4):
        zz = (z + s) % 4
        for half in range(2):
            dq_out[s, :, half * T : (half + 1) * T] = (dq[2 * zz + half] * SCALE).astype(bf16)
    for b in range(16):
        if b < BUCKETS:
            rab_out[b : b + 1, :] = jnp.sum(rab[b], axis=0, keepdims=True)
        else:
            rab_out[b : b + 1, :] = jnp.zeros((1, T), f32)


def attend_back(ids, table, lengths, saved, grads):
    return pl.pallas_call(
        backward_kernel,
        in_specs=[SMEM] * 6 + [VMEM] * 5,
        out_specs=[VMEM] * 6,
        out_shape=[sds((4, 256, 256), bf16)] * 4 + [sds((4, T, 256), bf16), sds((16, T), f32)],
        scratch_shapes=STAGE
        + [
            pltpu.VMEM((QT + 1, T, T), bf16),
            pltpu.VMEM((QT + 1, T, T), bf16),
            pltpu.VMEM((QT + 1, T, T), bf16),
            pltpu.VMEM((QT + 1, T, T), f32),
            pltpu.VMEM((TILES + 1, T, T), f32),
            pltpu.VMEM((TILES + 1, T, T), f32),
            pltpu.VMEM((16, 8, T), f32),
        ],
        compiler_params=params(VM_BACK),
        cost_estimate=cost(1e9 * 12, 8 << 20),
        name="attend_back",
    )(ids, table, lengths, *saved[:3], *[in_hbm(part) for part in saved[3:]], grads)


def combine_kernel(mine_s, mine_o, got_s, got_o, dq, proj_own, proj_got, rab, rab_got, *outs):
    proj = proj_own[...] + proj_got[...].astype(f32)
    both = rab[...] + rab_got[...]
    high = both.astype(bf16)
    low = (both - high.astype(f32)).astype(bf16)
    for s in range(4):
        outs[s][0:256, :] = (mine_s[s].astype(f32) + got_s[s].astype(f32)).astype(bf16)
        outs[s][256:384, :] = dq[s]
        outs[4 + s][0:256, :] = (mine_o[s].astype(f32) + got_o[s].astype(f32)).astype(bf16)
        for other in range(2):
            block = proj[s * 16 + other * 8 : s * 16 + other * 8 + 8, :]
            block = jnp.concatenate([block[:, c * 256 : (c + 1) * 256] for c in range(4)], axis=0)
            base = 384 - 128 * other
            outs[4 * other + s][base : base + 32, :] = block.astype(bf16)
            outs[4 * other + s][base + 32 :, 0:T] = high
            outs[4 * other + s][base + 32 :, T:] = low


def combine(*parts):
    return pl.pallas_call(
        combine_kernel,
        in_specs=[VMEM] * 9,
        out_specs=[VMEM] * 8,
        out_shape=[sds((432, 256), bf16)] * 4 + [sds((304, 256), bf16)] * 4,
        compiler_params=params(24),
        cost_estimate=cost(1 << 20, 5 << 20),
        name="combine",
    )(*parts)


def collect_kernel(ids, *refs):
    ins, rabs, out = refs[:8], refs[8:16], refs[16]
    total = ins[0][...].astype(f32)
    for ref in ins[1:]:
        total = total + ref[...].astype(f32)
    for d in range(8):
        for c in range(4):
            rows = total[c * 8 + (d // 4) * 4 : c * 8 + (d // 4) * 4 + 4, :]
            out[d, 0:4, c * 256 : (c + 1) * 256] = jnp.where(ids[3] % 4 == d % 4, rows, 0.0)
    lane = lax.broadcasted_iota(i32, (16, T), 1)
    table = jnp.zeros((16, T), f32)
    for t in range(4):
        near, far = rabs[t][...].astype(f32), rabs[4 + t][...].astype(f32)
        near, far = near[:, :T] + near[:, T:], far[:, :T] + far[:, T:]
        first, second = jnp.where(ids[0] == 0, near, far), jnp.where(ids[0] == 0, far, near)
        head = (ids[1] + 4 - t) % 4
        table = jnp.where(lane == head, jnp.sum(first + second, axis=1, keepdims=True), table)
    turned = jnp.transpose(jnp.concatenate([table, jnp.zeros((T - 16, T), f32)], axis=0))
    for d in range(8):
        out[d, 4:, :T] = turned[0:4]
        out[d, 4:, T:] = jnp.zeros((4, 1024 - T), f32)


def collect(ids, same, other):
    return pl.pallas_call(
        collect_kernel,
        grid=(1,),
        in_specs=[SMEM]
        + [pl.BlockSpec((32, 256), lambda i: (12, 0))] * 4
        + [pl.BlockSpec((32, 256), lambda i: (8, 0))] * 4
        + [pl.BlockSpec((16, 256), lambda i: (26, 0))] * 4
        + [pl.BlockSpec((16, 256), lambda i: (18, 0))] * 4,
        out_specs=pl.BlockSpec((8, 8, 1024), lambda i: (0, 0, 0)),
        out_shape=sds((8, 8, 1024), f32),
        compiler_params=params(8),
        cost_estimate=cost(1 << 16, 1 << 18),
        name="collect",
    )(ids, *same, *other, *same, *other)


def lines_kernel(lines, proj_grad, rab_grad):
    total = lines[0]
    for d in range(1, 8):
        total = total + lines[d]
    proj_grad[...] = total[0:4]
    rab_grad[...] = total[4:, 0:BUCKETS]


def add_lines(lines):
    return pl.pallas_call(
        lines_kernel,
        in_specs=[VMEM],
        out_specs=[VMEM] * 2,
        out_shape=[sds((4, 1024), f32), sds((HEADS, BUCKETS), f32)],
        compiler_params=params(8),
        cost_estimate=cost(1 << 16, 1 << 18),
        name="add_lines",
    )(lines)


def ready_kernel(tokens, cot, in_proj, normed, inverse, cot_out, in_proj_out, sems):
    copies = [
        pltpu.make_async_copy(in_proj, in_proj_out, sems.at[0]),
        pltpu.make_async_copy(cot, cot_out, sems.at[1]),
    ]
    for copy in copies:
        copy.start()
    shaped, scale = norm_rows(tokens[...].astype(f32))
    normed[...] = shaped
    inverse[...] = jnp.broadcast_to(scale, (256, T))
    for copy in copies:
        copy.wait()


def make_ready(tokens, cot, in_proj):
    hbm = pl.BlockSpec(memory_space=pltpu.HBM)
    return pl.pallas_call(
        ready_kernel,
        in_specs=[VMEM, hbm, hbm],
        out_specs=[VMEM] * 4,
        out_shape=[
            pltpu.VMEM((256, 1024), f32),
            pltpu.VMEM((256, T), f32),
            pltpu.VMEM((256, 1024), bf16),
            pltpu.VMEM((1024, 2048), bf16),
        ],
        scratch_shapes=[pltpu.SemaphoreType.DMA((2,))],
        compiler_params=params(16),
        cost_estimate=cost(1 << 22, 6 << 20),
        name="ready",
    )(in_hbm(tokens), in_hbm(cot), in_hbm(in_proj))


def final_kernel(ids, grad_gate, slope, normed, inverse, cot, in_proj, *refs):
    same, other, grad_in, grad_pre = refs[:4], refs[4:8], refs[8], refs[9]
    z = ids[1]
    grad_pre[:, 0:512] = grad_gate[...]
    for t in range(4):
        head = (z + 4 - t) % 4
        column = lambda kind: pl.ds(pl.multiple_of(kind * 512 + head * T, T), T)
        total = same[t][0:256, :].astype(f32) + other[t][0:256, :].astype(f32)
        for half in range(2):
            rows = slice(half * T, (half + 1) * T)
            key = jnp.transpose(total[0:T, rows])
            value = jnp.transpose(total[T:, rows])
            query = same[t][256:384, rows].astype(f32)
            for kind, part in ((1, value), (2, query), (3, key)):
                grad_pre[rows, column(kind)] = (
                    part * slope[rows, column(kind)].astype(f32)
                ).astype(bf16)
    upstream = lax.dot_general(grad_pre[...], in_proj[...], NT_DIMS, preferred_element_type=f32)
    back = norm_back(upstream, normed[...], inverse[:, 0:1])
    grad_in[...] = (cot[...].astype(f32) + back).astype(bf16)


def finish_grad(ids, ready, slope, grad_gate, same, other):
    return pl.pallas_call(
        final_kernel,
        in_specs=[SMEM] + [VMEM] * 14,
        out_specs=VMEM,
        out_shape=sds((256, 1024), bf16),
        scratch_shapes=[pltpu.VMEM((256, 2048), bf16)],
        compiler_params=params(24),
        cost_estimate=cost(2 * 256 * 1024 * 2048, 8 << 20),
        name="finish_grad",
    )(ids, grad_gate, slope, *ready, *same, *other)


def move(y_xor, z_shift, core_xor):
    pairs = []
    for dev in range(DEVS):
        y, z, core = dev // 8, (dev // 2) % 4, dev % 2
        target = (y ^ y_xor) * 8 + ((z + z_shift) % 4) * 2 + (core ^ core_xor)
        pairs.append((dev, target))
    return pairs


def send(x, y_xor, z_shift, core_xor):
    return lax.ppermute(x, "ctx", move(y_xor, z_shift, core_xor))


OVER_Z = [[y * 8 + z * 2 + c for z in range(4)] for y in range(2) for c in range(2)]
OVER_X = [[low * 4 + x for x in range(4)] for low in range(2)]


def send_x(part, shift):
    return lax.ppermute(part, "dp", [(d, d // 4 * 4 + (d + shift) % 4) for d in range(8)])


def swap_z(part):
    return lax.all_to_all(part, "ctx", 0, 0, axis_index_groups=OVER_Z, tiled=True)


def on_device(tokens, cotangent, in_proj, out_proj, rab_time, seq_lengths, block_mask, time_bucket):
    ctx = lax.axis_index("ctx")
    y, z, core = ctx // 8, (ctx // 2) % 4, ctx % 2
    times = jnp.stack([time_bucket // T, time_bucket % T]).astype(bf16)
    near_tokens = jnp.concatenate([tokens, jnp.pad(times, ((0, 14), (0, 768)))], axis=0)
    far_tokens = send(near_tokens, 1, 0, 0)
    full = project(near_tokens, in_proj, block_mask)
    own = [full[0]] + [send(full[s], 0, s, 0) for s in (1, 2, 3)]
    pairs = project(far_tokens, in_proj)
    across = [pairs[0]] + [send(pairs[s], 0, s, 0) for s in (1, 2, 3)]
    own, across[1] = lax.optimization_barrier((own, across[1]))
    gate, slope, grad_mix = make_gates(tokens, in_proj, cotangent, out_proj)
    own_twin = [send(part, 0, 0, 1) for part in own]
    across_twin = [send(part, 0, 0, 1) for part in across]
    parts = own + own_twin + across + across_twin

    ids = jnp.stack([y, z, core, lax.axis_index("dp")]).astype(i32)
    lengths = seq_lengths.reshape(3)
    limits = [2.0**j - 1.0 for j in range(BUCKETS)] + [1e9] * 4
    head_bias = lax.dynamic_slice_in_dim(rab_time, z, 1, 1).reshape(BUCKETS) * 0.5
    table = jnp.concatenate([head_bias, jnp.zeros((4,), f32), jnp.array(limits, f32)])
    heads, *saved = attend(ids, table, lengths, parts)

    mixed, grad_gate, grads = middle(swap_z(heads), gate, slope, grad_mix)
    grads = swap_z(grads)
    output, proj, *proj_x = finish_output(ids, tokens, cotangent, out_proj, mixed)
    grads, proj_x = lax.optimization_barrier((grads, proj_x))
    proj_x = [send_x(proj_x[s - 1], s) for s in (1, 2, 3)]

    mine_s, mine_o, theirs_s, theirs_o, dq, rab = attend_back(ids, table, lengths, saved, grads)
    got_o = send(theirs_o, 0, 0, 1)
    got_s = send(theirs_s, 0, 0, 1)
    rab_got = send(rab, 0, 0, 1)
    for part in proj_x:
        proj = proj + part.astype(f32)
    proj_own, proj_got = proj[:64], send(proj[64:].astype(bf16), 0, 0, 1)
    messages = combine(mine_s, mine_o, got_s, got_o, dq, proj_own, proj_got, rab, rab_got)
    messages, late_cot = lax.optimization_barrier((messages, cotangent))
    ready = make_ready(tokens, late_cot, in_proj)
    same = [messages[0]] + [send(messages[s], 0, s, 0) for s in (1, 2, 3)]
    other = [send(messages[4 + s], 1, s, 0) for s in range(4)]
    lines = lax.all_to_all(collect(ids, same, other), "dp", 0, 0, tiled=True)
    proj_grad, rab_grad = add_lines(lines)
    grad_in = finish_grad(ids, ready, slope, grad_gate, same, other)
    return output, grad_in, proj_grad, rab_grad.T


def solution(mesh):
    rows = P(("dp", "ctx"), None)
    placed = (rows, rows, P(), P(), P(), P("dp", None), P("dp", "ctx", None), P(("dp", "ctx")))
    return jax.shard_map(
        on_device,
        mesh=mesh,
        in_specs=placed,
        out_specs=(rows, rows, rows, P()),
        check_vma=False,
    )
```

```python
import functools
import math

import jax
import jax.numpy as jnp
from jax import lax
from jax.experimental import pallas as pl
from jax.experimental.pallas import tpu as pltpu
from jax.sharding import PartitionSpec as P

f32 = jnp.float32
bf16 = jnp.bfloat16
i32 = jnp.int32
T = 128
EPS = 1e-05
HEADS = 4
BUCKETS = 12
DEVS = 16
TILES = 32
QT = 8
SCALE = 1.0 / math.sqrt(128.0)
LIST = 160
FAR_U = 8
NEAR_U = 8
NEAR_FLAG = 32768
DUMMY = QT + 16 * TILES
VM_ATTEND = 20
VM_BACK = 24
VMEM = pl.BlockSpec(memory_space=pltpu.VMEM)
SMEM = pl.BlockSpec(memory_space=pltpu.SMEM)
NT_DIMS = (((1,), (1,)), ((), ()))
TN_DIMS = (((0,), (0,)), ((), ()))


def params(mib=24):
    return pltpu.CompilerParams(vmem_limit_bytes=mib * 1024 * 1024)


def cost(flops, size):
    return pl.CostEstimate(flops=int(flops), bytes_accessed=int(size), transcendentals=0)


def sds(shape, dtype):
    return jax.ShapeDtypeStruct(shape, dtype)


def norm_rows(values):
    centre = jnp.mean(values, axis=-1, keepdims=True)
    shifted = values - centre
    spread = jnp.mean(shifted * shifted, axis=-1, keepdims=True)
    inverse = lax.rsqrt(spread + EPS)
    return shifted * inverse, inverse


def norm_back(upstream, normed, inverse):
    first = jnp.mean(upstream, axis=-1, keepdims=True)
    second = jnp.mean(upstream * normed, axis=-1, keepdims=True)
    return inverse * (upstream - first - normed * second)


def in_hbm(part):
    return pltpu.with_memory_space_constraint(part, pltpu.HBM)


def pack_kernel(tokens, moments, out):
    out[0:256, :] = tokens[...]
    time = moments[...].reshape(1, 256)
    rows = jnp.concatenate([time // T, time % T, jnp.zeros((14, 256), i32)], axis=0)
    out[256:, 0:256] = rows.astype(f32).astype(bf16)
    out[256:, 256:] = jnp.zeros((16, 768), bf16)


def pack(tokens, moments):
    return pl.pallas_call(
        pack_kernel,
        in_specs=[VMEM] * 2,
        out_specs=VMEM,
        out_shape=sds((272, 1024), bf16),
        compiler_params=params(8),
        cost_estimate=cost(1 << 16, 1 << 20),
        name="pack",
    )(in_hbm(tokens), in_hbm(moments))


def project_kernel(own, tokens, *refs):
    weights, outs, normed = refs[own : 2 * own + 2], refs[2 * own + 2 : -1], refs[-1]
    head = pl.program_id(0)
    shift = (head + 4 - (lax.axis_index("ctx") // 2) % 4) % 4

    @pl.when(head == 0)
    def _():
        normed[...] = norm_rows(tokens[0:256, :].astype(f32))[0].astype(bf16)

    wide = jnp.concatenate([w[...] for w in weights], axis=1)
    half = 0.5 * jnp.dot(normed[...], wide, preferred_element_type=f32)
    act = (half * jnp.tanh(half) + half).astype(bf16)
    meta = tokens[256:, 0:256]
    if own:
        mask, blank = refs[0], jnp.zeros((1, T - TILES), f32)
        row = [mask[0, 0:1].astype(f32), blank, mask[0, 1:2].astype(f32), blank]
        rows = [meta[0:2].astype(f32), jnp.concatenate(row, axis=1), jnp.zeros((13, 256), f32)]
        meta = jnp.concatenate(rows, axis=0).astype(bf16)
    for which in range(4):

        @pl.when(shift == which)
        def _(which=which):
            outs[which][0:256, :] = act
            outs[which][256:, 0:256] = meta
            if own:
                outs[which][256:, 256:] = jnp.zeros((16, T), bf16)


def project(tokens, in_proj, mask=None):
    own = mask is not None
    width = 384 if own else 256

    def column(kind):
        return pl.BlockSpec((1024, T), lambda h: (0, kind * HEADS + h))

    whole = lambda shape: pl.BlockSpec(shape, lambda h: (0,) * len(shape))
    kinds = (3, 1, 2) if own else (3, 1)
    return pl.pallas_call(
        functools.partial(project_kernel, int(own)),
        grid=(HEADS,),
        in_specs=[whole((272, 1024))] + [whole((1, 2, TILES))] * own + [column(kind) for kind in kinds],
        out_specs=[whole((272, width))] * 4,
        out_shape=[sds((272, width), bf16)] * 4,
        scratch_shapes=[pltpu.VMEM((256, 1024), bf16)],
        compiler_params=params(12),
        cost_estimate=cost(2 * 256 * 1024 * 4 * width, 5 << 20),
        name="project_own" if own else "project_other",
    )(tokens, *([in_hbm(mask)] if own else []), *[in_hbm(in_proj)] * len(kinds))


def gates_kernel(tokens, in_proj, cot, out_proj, gate, slope, grad_mix, normed):
    kind = pl.program_id(0)

    @pl.when(kind == 0)
    def _():
        normed[...] = norm_rows(tokens[...].astype(f32))[0].astype(bf16)
        grad_mix[...] = lax.dot_general(cot[...], out_proj[...], NT_DIMS, preferred_element_type=f32)

    pre = jnp.dot(normed[...], in_proj[...], preferred_element_type=f32)
    sig = 0.5 * jnp.tanh(0.5 * pre) + 0.5
    slope[...] = (sig * (1.0 + pre * (1.0 - sig))).astype(bf16)

    @pl.when(kind == 0)
    def _():
        gate[...] = (pre * sig).astype(bf16)


def make_gates(tokens, in_proj, cot, out_proj):
    whole = lambda shape: pl.BlockSpec(shape, lambda s: (0,) * len(shape))
    return pl.pallas_call(
        gates_kernel,
        grid=(4,),
        in_specs=[
            whole((256, 1024)),
            pl.BlockSpec((1024, 512), lambda s: (0, s)),
            whole((256, 1024)),
            whole((512, 1024)),
        ],
        out_specs=[whole((256, 512)), pl.BlockSpec((256, 512), lambda s: (0, s)), whole((256, 512))],
        out_shape=[
            pltpu.VMEM((256, 512), bf16),
            pltpu.VMEM((256, 2048), bf16),
            pltpu.VMEM((256, 512), f32),
        ],
        scratch_shapes=[pltpu.VMEM((256, 1024), bf16)],
        compiler_params=params(16),
        cost_estimate=cost(2 * 256 * 1024 * 2048, 7 << 20),
        name="gates",
    )(in_hbm(tokens), in_hbm(in_proj), in_hbm(cot), in_hbm(out_proj))


def bias_far(gap, table, bottom):
    first = table[bottom]
    second = table[bottom + 1]
    third = table[bottom + 2]
    limit1 = table[16 + bottom + 1]
    limit2 = table[16 + bottom + 2]
    over1 = gap >= limit1
    over2 = gap >= limit2
    return jnp.where(over2, third, jnp.where(over1, second, first)), over1, over2


def bias_near(gap, table):
    bias = jnp.full(gap.shape, table[0], f32)
    for j in range(1, BUCKETS):
        bias = jnp.where(gap >= float(2**j - 1), table[j], bias)
    return bias


def keep_near(ids, start, jj, k):
    tile = query_tile(ids, jj)
    row = lax.broadcasted_iota(i32, (T, T), 0)
    col = lax.broadcasted_iota(i32, (T, T), 1)
    later = (col - row) <= (tile - k) * T
    return later & ((col + k * T) >= start)


STAGE = [pltpu.VMEM((QT + 1, T, T), f32), pltpu.VMEM((QT + 1, T, T), i32)]


def query_tile(ids, jj):
    dev = ids[0] * 8 + (jj // 2) * 2 + ids[2]
    return jnp.where(jj % 2 == 0, dev, 2 * DEVS - 1 - dev)


def starts_of(lengths, pos):
    end0 = lengths[0]
    end1 = lengths[0] + lengths[1]
    return jnp.where(pos >= end1, end1, jnp.where(pos >= end0, end0, 0))


def stage(ids, ins, keys, values, queries, tk, flags, times):
    y, z, core = ids[0], ids[1], ids[2]
    for group in range(4):
        for t in range(4):
            ref = ins[group * 4 + t]
            zz = (z + 4 - t) % 4
            dev = (y if group < 2 else 1 - y) * 8 + zz * 2 + (core if group % 2 == 0 else 1 - core)
            keys[dev] = ref[0:T, 0:T]
            values[dev] = ref[0:T, T : 2 * T]
            keys[2 * DEVS - 1 - dev] = ref[T : 2 * T, 0:T]
            values[2 * DEVS - 1 - dev] = ref[T : 2 * T, T : 2 * T]
            head = ref[256:272, 0:256].astype(f32)
            moments = head[0:1] * 128.0 + head[1:2]
            tk[dev] = jnp.broadcast_to(moments[:, :T], (8, T))
            tk[2 * DEVS - 1 - dev] = jnp.broadcast_to(moments[:, T:], (8, T))
            times[pl.ds(dev, 1), :] = moments[:, :T]
            times[pl.ds(2 * DEVS - 1 - dev, 1), :] = moments[:, T:]
            if group == 0:
                queries[2 * zz] = ref[0:T, 2 * T :]
                queries[2 * zz + 1] = ref[T : 2 * T, 2 * T :]
                flags[pl.ds(2 * zz, 1), :] = head[2:3, :T]
                flags[pl.ds(2 * zz + 1, 1), :] = head[2:3, T:]
    keys[TILES] = jnp.zeros((T, T), bf16)
    values[TILES] = jnp.zeros((T, T), bf16)
    queries[QT] = jnp.zeros((T, T), bf16)
    tk[TILES] = jnp.zeros((8, T), f32)


def stage_times(ids, lengths, tq, tk, start):
    tq[QT] = jnp.zeros((T, T), f32)
    start[QT] = jnp.zeros((T, T), i32)
    rows = lax.broadcasted_iota(i32, (T, T), 0)
    for jj in range(QT):
        tile = query_tile(ids, jj)
        tq[jj] = jnp.transpose(jnp.broadcast_to(tk[tile][0:1, :], (T, T)))
        start[jj] = starts_of(lengths, rows + tile * T)


def make_lists(ids, lengths, flags, times, q_times, codes, codes_smem, sem, far, near, counts):
    def level(gap):
        total = jnp.zeros(gap.shape, i32)
        for j in range(1, BUCKETS):
            total = total + jnp.where(gap >= float(2**j - 1), 1, 0)
        return total

    for jj in range(QT):
        q_times[jj : jj + 1, :] = times[pl.ds(query_tile(ids, jj), 1), :]
    turned = jnp.transpose(times[...])
    k_first, k_last = turned[0:1, :], turned[T - 1 :, :]
    q_first, q_last = q_times[:, 0:1], q_times[:, T - 1 :]
    jj = lax.broadcasted_iota(i32, (8, T), 0)
    kk = lax.broadcasted_iota(i32, (8, T), 1)
    tile = query_tile(ids, jj)
    low = starts_of(lengths, tile * T)
    high = starts_of(lengths, tile * T + T - 1)
    bottom = level(jnp.maximum(q_first - k_last, 0.0))
    top = level(q_last - k_first)
    row = lax.broadcasted_iota(i32, (T, T), 0)
    col = lax.broadcasted_iota(i32, (T, T), 1)
    turn = jnp.where(row == jnp.where(col < DEVS, 2 * col, 4 * DEVS - 1 - 2 * col), 1.0, 0.0).astype(bf16)
    ordered = jnp.dot(flags[...].astype(bf16), turn, preferred_element_type=f32)
    allowed = (ordered > 0.5) & (kk <= tile) & (kk * T + T - 1 >= low)
    plain = (kk < tile) & (kk * T >= high) & (top - bottom <= 2)
    entry = jj + 16 * kk
    codes[...] = jnp.where(
        allowed, jnp.where(plain, entry + 1024 * bottom, entry + NEAR_FLAG), -1
    )
    copy = pltpu.make_async_copy(codes, codes_smem, sem)
    copy.start()
    copy.wait()

    def query_step(jj, sizes):
        tile = query_tile(ids, jj)

        def key_step(k, sizes):
            n_far, n_near = sizes
            code = codes_smem[jj, k]
            far[n_far] = code
            near[n_near] = code & (NEAR_FLAG - 1)
            is_near = code >= NEAR_FLAG
            is_far = (code >= 0) & jnp.logical_not(is_near)
            return n_far + is_far.astype(i32), n_near + is_near.astype(i32)

        return lax.fori_loop(starts_of(lengths, tile * T) // T, tile + 1, key_step, sizes)

    n_far, n_near = lax.fori_loop(0, QT, query_step, (jnp.int32(0), jnp.int32(0)))
    for pad in range(FAR_U):
        far[n_far + pad] = DUMMY
    for pad in range(NEAR_U):
        near[n_near + pad] = DUMMY
    counts[0] = (n_far + FAR_U - 1) // FAR_U
    counts[1] = (n_near + NEAR_U - 1) // NEAR_U


def unpack(ref, i, count):
    got = []
    for u in range(count):
        entry = ref[i * count + u]
        got.append((entry & 15, (entry >> 4) & 63, entry >> 10))
    return got


def forward_kernel(ids, table, lengths, *refs):
    ins, (out, far, near, counts, keys, values, queries, tk) = refs[:16], refs[16:24]
    tq, start, acc, flags, times, q_times, codes, codes_smem, sem = refs[24:]
    times[...] = jnp.zeros(times.shape, f32)
    stage(ids, ins, keys, values, queries, tk, flags, times)
    stage_times(ids, lengths, tq, tk, start)
    make_lists(ids, lengths, flags, times, q_times, codes, codes_smem, sem, far, near, counts)
    acc[...] = jnp.zeros(acc.shape, f32)

    def far_step(i, _):
        got = unpack(far, i, FAR_U)
        dots = [lax.dot_general(queries[j], keys[k], NT_DIMS, preferred_element_type=f32) for j, k, _ in got]
        weights = []
        for u, (jj, k, bottom) in enumerate(got):
            bias, _, _ = bias_far(tq[jj] - tk[k][0:1, :], table, bottom)
            half = dots[u] * (0.5 * SCALE) + bias
            weights.append((half * jnp.tanh(half) + half).astype(bf16))
        adds = [jnp.dot(weights[u], values[got[u][1]], preferred_element_type=f32) for u in range(len(got))]
        for u in range(len(got)):
            acc[got[u][0]] += adds[u]
        return 0

    def near_step(i, _):
        got = unpack(near, i, NEAR_U)
        dots = [lax.dot_general(queries[j], keys[k], NT_DIMS, preferred_element_type=f32) for j, k, _ in got]
        weights = []
        for u, (jj, k, _) in enumerate(got):
            half = dots[u] * (0.5 * SCALE) + bias_near(tq[jj] - tk[k][0:1, :], table)
            weight = half * jnp.tanh(half) + half
            weights.append(jnp.where(keep_near(ids, start[jj], jj, k), weight, 0.0).astype(bf16))
        adds = [jnp.dot(weights[u], values[got[u][1]], preferred_element_type=f32) for u in range(len(got))]
        for u in range(len(got)):
            acc[got[u][0]] += adds[u]
        return 0

    lax.fori_loop(0, counts[0], far_step, 0)
    lax.fori_loop(0, counts[1], near_step, 0)
    for zz in range(4):
        out[zz, 0:T] = acc[2 * zz]
        out[zz, T:] = acc[2 * zz + 1]


def attend(ids, table, lengths, parts):
    return pl.pallas_call(
        forward_kernel,
        in_specs=[SMEM] * 3 + [VMEM] * 16,
        out_specs=[VMEM] + [SMEM] * 3 + [VMEM] * 4,
        out_shape=[sds((4, 256, T), f32), sds((LIST,), i32), sds((LIST,), i32), sds((8,), i32)]
        + [pltpu.HBM((TILES + 1, T, T), bf16)] * 2
        + [pltpu.HBM((QT + 1, T, T), bf16), pltpu.HBM((TILES + 1, 8, T), f32)],
        scratch_shapes=STAGE
        + [
            pltpu.VMEM((QT + 1, T, T), f32),
            pltpu.VMEM((8, T), f32),
            pltpu.VMEM((T, T), f32),
            pltpu.VMEM((8, T), f32),
            pltpu.VMEM((8, T), i32),
            pltpu.SMEM((8, T), i32),
            pltpu.SemaphoreType.DMA,
        ],
        compiler_params=params(VM_ATTEND),
        cost_estimate=cost(1e9 * 6, 6 << 20),
        name="attend",
    )(ids, table, lengths, *parts)


def middle_kernel(heads, gate, slope, grad_mix, mixed, grad_gate, grads):
    whole = jnp.concatenate([heads[h] for h in range(4)], axis=1)
    normed, inverse = norm_rows(whole)
    gates = gate[...].astype(f32)
    mixed[...] = (normed * gates).astype(bf16)
    back = grad_mix[...]
    grad_gate[...] = (back * normed * slope[...].astype(f32)).astype(bf16)
    grad = norm_back(back * gates, normed, inverse).astype(bf16)
    for h in range(4):
        grads[h] = grad[:, h * T : (h + 1) * T]


def middle(heads, gate, slope, grad_mix):
    whole = lambda shape: pl.BlockSpec(shape, lambda i: (0,) * len(shape))
    return pl.pallas_call(
        middle_kernel,
        grid=(1,),
        in_specs=[whole((4, 256, T)), whole((256, 512)), whole((256, 512)), whole((256, 512))],
        out_specs=[whole((256, 512)), whole((256, 512)), whole((4, 256, T))],
        out_shape=[
            pltpu.HBM((256, 512), bf16),
            pltpu.HBM((256, 512), bf16),
            sds((4, 256, T), bf16),
        ],
        compiler_params=params(12),
        cost_estimate=cost(1 << 24, 3 << 20),
        name="middle",
    )(heads, gate, slope, grad_mix)


def output_kernel(ids, tokens, cot, out_proj, mixed, output, mine, *theirs):
    y, z, core, low, x = ids[0], ids[1], ids[2], ids[3] // 4, ids[3] % 4
    output[...] = (
        tokens[...].astype(f32) + jnp.dot(mixed[...], out_proj[...], preferred_element_type=f32)
    ).astype(bf16)
    r = lax.broadcasted_iota(i32, (512, 512), 1)
    c = lax.broadcasted_iota(i32, (512, 512), 0)
    r_x = ((r // 128) + x) % 4
    r_core = ((r // 64) % 2) ^ core
    r_z = (((r // 16) % 4) + z) % 4
    r_y = ((r // 8) % 2) ^ y
    source = (((r // 4) % 2) * 4 + r_x) * 64 + r_y * 32 + r_z * 8 + r_core * 4 + r % 4
    pick = jnp.where(c == source, 1.0, 0.0).astype(bf16)
    moved = jnp.dot(mixed[...], pick, preferred_element_type=f32).astype(bf16)
    part = lax.dot_general(moved, cot[...], TN_DIMS, preferred_element_type=f32)
    mine[...] = part[:T]
    for i in range(3):
        theirs[i][...] = part[(i + 1) * T : (i + 2) * T].astype(bf16)


def finish_output(ids, tokens, cot, out_proj, mixed):
    return pl.pallas_call(
        output_kernel,
        in_specs=[SMEM] + [VMEM] * 4,
        out_specs=[VMEM] * 5,
        out_shape=[sds((256, 1024), bf16), sds((T, 1024), f32)] + [sds((T, 1024), bf16)] * 3,
        compiler_params=params(24),
        cost_estimate=cost(6 * 256 * 512 * 1024, 5 << 20),
        name="finish_output",
    )(ids, in_hbm(tokens), in_hbm(cot), in_hbm(out_proj), in_hbm(mixed))


def backward_kernel(ids, table, lengths, far, near, counts, *refs):
    (keys, values, queries, tk), got_grads, outs = refs[:4], refs[4], refs[5:11]
    mine_s, mine_o, theirs_s, theirs_o, dq_out, rab_out = outs
    tq, start, grads, grads_t, queries_t, dq, dkt, dvt, rab = refs[11:]
    y, z, core = ids[0], ids[1], ids[2]
    stage_times(ids, lengths, tq, tk, start)
    for zz in range(4):
        for half in range(2):
            block = got_grads[zz, half * T : (half + 1) * T, :].astype(f32) * 0.5
            grads[2 * zz + half] = block.astype(bf16)
            grads_t[2 * zz + half] = jnp.transpose(block).astype(bf16)
    for jj in range(QT):
        queries_t[jj] = jnp.transpose(queries[jj].astype(f32)).astype(bf16)
    grads[QT] = jnp.zeros((T, T), bf16)
    grads_t[QT] = jnp.zeros((T, T), bf16)
    queries_t[QT] = jnp.zeros((T, T), bf16)
    dq[...] = jnp.zeros(dq.shape, f32)
    dkt[...] = jnp.zeros(dkt.shape, f32)
    dvt[...] = jnp.zeros(dvt.shape, f32)
    rab[...] = jnp.zeros(rab.shape, f32)

    def fold(values_):
        return jnp.sum(values_.reshape(T // 8, 8, T), axis=0)

    def front(got):
        dots = [lax.dot_general(queries[j], keys[k], NT_DIMS, preferred_element_type=f32) for j, k, _ in got]
        wides = [lax.dot_general(grads[j], values[k], NT_DIMS, preferred_element_type=f32) for j, k, _ in got]
        return dots, wides

    def score(half, wide, keep):
        t = jnp.tanh(half)
        weight = half * t + half
        d_score = wide * ((1.0 + t) * (1.0 + half * (1.0 - t)))
        if keep is not None:
            weight = jnp.where(keep, weight, 0.0)
            d_score = jnp.where(keep, d_score, 0.0)
        return weight.astype(bf16), d_score

    def back(got, weights, scores):
        a = [jnp.dot(scores[u], keys[got[u][1]], preferred_element_type=f32) for u in range(len(got))]
        b = [jnp.dot(queries_t[got[u][0]], scores[u], preferred_element_type=f32) for u in range(len(got))]
        c = [jnp.dot(grads_t[got[u][0]], weights[u], preferred_element_type=f32) for u in range(len(got))]
        for u, (jj, k, _) in enumerate(got):
            dq[jj] += a[u]
            dkt[k] += b[u]
            dvt[k] += c[u]

    def far_step(i, _):
        got = unpack(far, i, FAR_U)
        dots, wides = front(got)
        weights, scores, sums = [], [], []
        for u, (jj, k, bottom) in enumerate(got):
            bias, over1, over2 = bias_far(tq[jj] - tk[k][0:1, :], table, bottom)
            weight, d_score = score(dots[u] * (0.5 * SCALE) + bias, wides[u], None)
            weights.append(weight)
            scores.append(d_score.astype(bf16))
            sums.append((fold(d_score), fold(jnp.where(over1, d_score, 0.0)), fold(jnp.where(over2, d_score, 0.0))))
        back(got, weights, scores)
        for (jj, k, bottom), (sum0, sum1, sum2) in zip(got, sums):
            rab[bottom] += sum0 - sum1
            rab[bottom + 1] += sum1 - sum2
            rab[bottom + 2] += sum2
        return 0

    def near_step(i, _):
        got = unpack(near, i, NEAR_U)
        dots, wides = front(got)
        weights, scores = [], []
        sums = [jnp.zeros((8, T), f32)] * BUCKETS
        for u, (jj, k, _) in enumerate(got):
            gap = tq[jj] - tk[k][0:1, :]
            half = dots[u] * (0.5 * SCALE) + bias_near(gap, table)
            weight, d_score = score(half, wides[u], keep_near(ids, start[jj], jj, k))
            weights.append(weight)
            scores.append(d_score.astype(bf16))
            sums[0] = sums[0] + fold(d_score)
            for j in range(1, BUCKETS):
                sums[j] = sums[j] + fold(jnp.where(gap >= float(2**j - 1), d_score, 0.0))
        back(got, weights, scores)
        for j in range(BUCKETS - 1):
            rab[j] += sums[j] - sums[j + 1]
        rab[BUCKETS - 1] += sums[BUCKETS - 1]
        return 0

    lax.fori_loop(0, counts[0], far_step, 0)
    lax.fori_loop(0, counts[1], near_step, 0)
    for other in range(2):
        for s in range(4):
            base = (y if other == 0 else 1 - y) * 8 + ((z + s) % 4) * 2
            for side in range(2):
                dev = base + (core if side == 0 else 1 - core)
                ref = ((mine_s, theirs_s), (mine_o, theirs_o))[other][side]
                for half in range(2):
                    tile = dev if half == 0 else 2 * DEVS - 1 - dev
                    ref[s, 0:T, half * T : (half + 1) * T] = (dkt[tile] * SCALE).astype(bf16)
                    ref[s, T:, half * T : (half + 1) * T] = (dvt[tile] * 2.0).astype(bf16)
    for s in range(4):
        zz = (z + s) % 4
        for half in range(2):
            dq_out[s, :, half * T : (half + 1) * T] = (dq[2 * zz + half] * SCALE).astype(bf16)
    for b in range(16):
        if b < BUCKETS:
            rab_out[b : b + 1, :] = jnp.sum(rab[b], axis=0, keepdims=True)
        else:
            rab_out[b : b + 1, :] = jnp.zeros((1, T), f32)


def attend_back(ids, table, lengths, saved, grads):
    return pl.pallas_call(
        backward_kernel,
        in_specs=[SMEM] * 6 + [VMEM] * 5,
        out_specs=[VMEM] * 6,
        out_shape=[sds((4, 256, 256), bf16)] * 4 + [sds((4, T, 256), bf16), sds((16, T), f32)],
        scratch_shapes=STAGE
        + [
            pltpu.VMEM((QT + 1, T, T), bf16),
            pltpu.VMEM((QT + 1, T, T), bf16),
            pltpu.VMEM((QT + 1, T, T), bf16),
            pltpu.VMEM((QT + 1, T, T), f32),
            pltpu.VMEM((TILES + 1, T, T), f32),
            pltpu.VMEM((TILES + 1, T, T), f32),
            pltpu.VMEM((16, 8, T), f32),
        ],
        compiler_params=params(VM_BACK),
        cost_estimate=cost(1e9 * 12, 8 << 20),
        name="attend_back",
    )(ids, table, lengths, *saved[:3], *[in_hbm(part) for part in saved[3:]], grads)


def combine_kernel(mine_s, mine_o, got_s, got_o, dq, proj_own, proj_got, rab, rab_got, *outs):
    proj = proj_own[...] + proj_got[...].astype(f32)
    both = rab[...] + rab_got[...]
    high = both.astype(bf16)
    low = (both - high.astype(f32)).astype(bf16)
    for s in range(4):
        outs[s][0:256, :] = (mine_s[s].astype(f32) + got_s[s].astype(f32)).astype(bf16)
        outs[s][256:384, :] = dq[s]
        outs[4 + s][0:256, :] = (mine_o[s].astype(f32) + got_o[s].astype(f32)).astype(bf16)
        for other in range(2):
            block = proj[s * 16 + other * 8 : s * 16 + other * 8 + 8, :]
            block = jnp.concatenate([block[:, c * 256 : (c + 1) * 256] for c in range(4)], axis=0)
            base = 384 - 128 * other
            outs[4 * other + s][base : base + 32, :] = block.astype(bf16)
            outs[4 * other + s][base + 32 :, 0:T] = high
            outs[4 * other + s][base + 32 :, T:] = low


def combine(*parts):
    return pl.pallas_call(
        combine_kernel,
        in_specs=[VMEM] * 9,
        out_specs=[VMEM] * 8,
        out_shape=[sds((432, 256), bf16)] * 4 + [sds((304, 256), bf16)] * 4,
        compiler_params=params(24),
        cost_estimate=cost(1 << 20, 5 << 20),
        name="combine",
    )(*parts)


def collect_kernel(ids, *refs):
    ins, rabs, out = refs[:8], refs[8:16], refs[16]
    total = ins[0][...].astype(f32)
    for ref in ins[1:]:
        total = total + ref[...].astype(f32)
    for d in range(8):
        for c in range(4):
            rows = total[c * 8 + (d // 4) * 4 : c * 8 + (d // 4) * 4 + 4, :]
            out[d, 0:4, c * 256 : (c + 1) * 256] = jnp.where(ids[3] % 4 == d % 4, rows, 0.0)
    lane = lax.broadcasted_iota(i32, (16, T), 1)
    table = jnp.zeros((16, T), f32)
    for t in range(4):
        near, far = rabs[t][...].astype(f32), rabs[4 + t][...].astype(f32)
        near, far = near[:, :T] + near[:, T:], far[:, :T] + far[:, T:]
        first, second = jnp.where(ids[0] == 0, near, far), jnp.where(ids[0] == 0, far, near)
        head = (ids[1] + 4 - t) % 4
        table = jnp.where(lane == head, jnp.sum(first + second, axis=1, keepdims=True), table)
    turned = jnp.transpose(jnp.concatenate([table, jnp.zeros((T - 16, T), f32)], axis=0))
    for d in range(8):
        out[d, 4:, :T] = turned[0:4]
        out[d, 4:, T:] = jnp.zeros((4, 1024 - T), f32)


def collect(ids, same, other):
    return pl.pallas_call(
        collect_kernel,
        grid=(1,),
        in_specs=[SMEM]
        + [pl.BlockSpec((32, 256), lambda i: (12, 0))] * 4
        + [pl.BlockSpec((32, 256), lambda i: (8, 0))] * 4
        + [pl.BlockSpec((16, 256), lambda i: (26, 0))] * 4
        + [pl.BlockSpec((16, 256), lambda i: (18, 0))] * 4,
        out_specs=pl.BlockSpec((8, 8, 1024), lambda i: (0, 0, 0)),
        out_shape=sds((8, 8, 1024), f32),
        compiler_params=params(8),
        cost_estimate=cost(1 << 16, 1 << 18),
        name="collect",
    )(ids, *same, *other, *same, *other)


def lines_kernel(lines, proj_grad, rab_grad):
    total = lines[0]
    for d in range(1, 8):
        total = total + lines[d]
    proj_grad[...] = total[0:4]
    rab_grad[...] = total[4:, 0:BUCKETS]


def add_lines(lines):
    return pl.pallas_call(
        lines_kernel,
        in_specs=[VMEM],
        out_specs=[VMEM] * 2,
        out_shape=[sds((4, 1024), f32), sds((HEADS, BUCKETS), f32)],
        compiler_params=params(8),
        cost_estimate=cost(1 << 16, 1 << 18),
        name="add_lines",
    )(lines)


def ready_kernel(tokens, cot, in_proj, normed, inverse, cot_out, in_proj_out, sems):
    copies = [
        pltpu.make_async_copy(in_proj, in_proj_out, sems.at[0]),
        pltpu.make_async_copy(cot, cot_out, sems.at[1]),
    ]
    for copy in copies:
        copy.start()
    shaped, scale = norm_rows(tokens[...].astype(f32))
    normed[...] = shaped
    inverse[...] = jnp.broadcast_to(scale, (256, T))
    for copy in copies:
        copy.wait()


def make_ready(tokens, cot, in_proj):
    hbm = pl.BlockSpec(memory_space=pltpu.HBM)
    return pl.pallas_call(
        ready_kernel,
        in_specs=[VMEM, hbm, hbm],
        out_specs=[VMEM] * 4,
        out_shape=[
            pltpu.VMEM((256, 1024), f32),
            pltpu.VMEM((256, T), f32),
            pltpu.VMEM((256, 1024), bf16),
            pltpu.VMEM((1024, 2048), bf16),
        ],
        scratch_shapes=[pltpu.SemaphoreType.DMA((2,))],
        compiler_params=params(16),
        cost_estimate=cost(1 << 22, 6 << 20),
        name="ready",
    )(in_hbm(tokens), in_hbm(cot), in_hbm(in_proj))


def final_kernel(ids, grad_gate, slope, normed, inverse, cot, in_proj, *refs):
    same, other, grad_in, grad_pre = refs[:4], refs[4:8], refs[8], refs[9]
    z = ids[1]
    grad_pre[:, 0:512] = grad_gate[...]
    for t in range(4):
        head = (z + 4 - t) % 4
        column = lambda kind: pl.ds(pl.multiple_of(kind * 512 + head * T, T), T)
        total = same[t][0:256, :].astype(f32) + other[t][0:256, :].astype(f32)
        for half in range(2):
            rows = slice(half * T, (half + 1) * T)
            key = jnp.transpose(total[0:T, rows])
            value = jnp.transpose(total[T:, rows])
            query = same[t][256:384, rows].astype(f32)
            for kind, part in ((1, value), (2, query), (3, key)):
                grad_pre[rows, column(kind)] = (
                    part * slope[rows, column(kind)].astype(f32)
                ).astype(bf16)
    upstream = lax.dot_general(grad_pre[...], in_proj[...], NT_DIMS, preferred_element_type=f32)
    back = norm_back(upstream, normed[...], inverse[:, 0:1])
    grad_in[...] = (cot[...].astype(f32) + back).astype(bf16)


def finish_grad(ids, ready, slope, grad_gate, same, other):
    return pl.pallas_call(
        final_kernel,
        in_specs=[SMEM] + [VMEM] * 14,
        out_specs=VMEM,
        out_shape=sds((256, 1024), bf16),
        scratch_shapes=[pltpu.VMEM((256, 2048), bf16)],
        compiler_params=params(24),
        cost_estimate=cost(2 * 256 * 1024 * 2048, 8 << 20),
        name="finish_grad",
    )(ids, grad_gate, slope, *ready, *same, *other)


def move(y_xor, z_shift, core_xor):
    pairs = []
    for dev in range(DEVS):
        y, z, core = dev // 8, (dev // 2) % 4, dev % 2
        target = (y ^ y_xor) * 8 + ((z + z_shift) % 4) * 2 + (core ^ core_xor)
        pairs.append((dev, target))
    return pairs


def send(x, y_xor, z_shift, core_xor):
    return lax.ppermute(x, "ctx", move(y_xor, z_shift, core_xor))


OVER_Z = [[y * 8 + z * 2 + c for z in range(4)] for y in range(2) for c in range(2)]
OVER_X = [[low * 4 + x for x in range(4)] for low in range(2)]


def send_x(part, shift):
    return lax.ppermute(part, "dp", [(d, d // 4 * 4 + (d + shift) % 4) for d in range(8)])


def swap_z(part):
    return lax.all_to_all(part, "ctx", 0, 0, axis_index_groups=OVER_Z, tiled=True)


def on_device(tokens, cotangent, in_proj, out_proj, rab_time, seq_lengths, block_mask, time_bucket):
    ctx = lax.axis_index("ctx")
    y, z, core = ctx // 8, (ctx // 2) % 4, ctx % 2
    near_tokens = pack(tokens, time_bucket)
    far_tokens = send(near_tokens, 1, 0, 0)
    ids = jnp.stack([y, z, core, lax.axis_index("dp")]).astype(i32)
    lengths = seq_lengths.reshape(3)
    limits = [2.0**j - 1.0 for j in range(BUCKETS)] + [1e9] * 4
    head_bias = lax.dynamic_slice_in_dim(rab_time, z, 1, 1).reshape(BUCKETS) * 0.5
    table = jnp.concatenate([head_bias, jnp.zeros((4,), f32), jnp.array(limits, f32)])
    full = project(near_tokens, in_proj, block_mask)
    full, ids, table = lax.optimization_barrier((full, ids, table))
    own = [full[0]] + [send(full[s], 0, s, 0) for s in (1, 2, 3)]
    pairs = project(far_tokens, in_proj)
    across = [pairs[0]] + [send(pairs[s], 0, s, 0) for s in (1, 2, 3)]
    own, across[1] = lax.optimization_barrier((own, across[1]))
    gate, slope, grad_mix = make_gates(tokens, in_proj, cotangent, out_proj)
    own_twin = [send(part, 0, 0, 1) for part in own]
    across_twin = [send(part, 0, 0, 1) for part in across]
    parts = own + own_twin + across + across_twin

    heads, *saved = attend(ids, table, lengths, parts)

    mixed, grad_gate, grads = middle(swap_z(heads), gate, slope, grad_mix)
    grads = swap_z(grads)
    output, proj, *proj_x = finish_output(ids, tokens, cotangent, out_proj, mixed)
    grads, proj_x = lax.optimization_barrier((grads, proj_x))
    proj_x = [send_x(proj_x[s - 1], s) for s in (1, 2, 3)]

    mine_s, mine_o, theirs_s, theirs_o, dq, rab = attend_back(ids, table, lengths, saved, grads)
    got_o = send(theirs_o, 0, 0, 1)
    got_s = send(theirs_s, 0, 0, 1)
    rab_got = send(rab, 0, 0, 1)
    for part in proj_x:
        proj = proj + part.astype(f32)
    proj_own, proj_got = proj[:64], send(proj[64:].astype(bf16), 0, 0, 1)
    messages = combine(mine_s, mine_o, got_s, got_o, dq, proj_own, proj_got, rab, rab_got)
    messages, late_cot = lax.optimization_barrier((messages, cotangent))
    ready = make_ready(tokens, late_cot, in_proj)
    same = [messages[0]] + [send(messages[s], 0, s, 0) for s in (1, 2, 3)]
    other = [send(messages[4 + s], 1, s, 0) for s in range(4)]
    lines = lax.all_to_all(collect(ids, same, other), "dp", 0, 0, tiled=True)
    proj_grad, rab_grad = add_lines(lines)
    grad_in = finish_grad(ids, ready, slope, grad_gate, same, other)
    return output, grad_in, proj_grad, rab_grad.T


def solution(mesh):
    rows = P(("dp", "ctx"), None)
    placed = (rows, rows, P(), P(), P(), P("dp", None), P("dp", "ctx", None), P(("dp", "ctx")))
    return jax.shard_map(
        on_device,
        mesh=mesh,
        in_specs=placed,
        out_specs=(rows, rows, rows, P()),
        check_vma=False,
    )
```

```python
import functools
import math

import jax
import jax.numpy as jnp
from jax import lax
from jax.experimental import pallas as pl
from jax.experimental.pallas import tpu as pltpu
from jax.sharding import PartitionSpec as P

f32 = jnp.float32
bf16 = jnp.bfloat16
i32 = jnp.int32
T = 128
EPS = 1e-05
HEADS = 4
BUCKETS = 12
DEVS = 16
TILES = 32
QT = 8
SCALE = 1.0 / math.sqrt(128.0)
LIST = 160
FAR_U = 12
NEAR_U = 8
NEAR_FLAG = 32768
DUMMY = QT + 16 * TILES
VM_ATTEND = 20
VM_BACK = 24
VMEM = pl.BlockSpec(memory_space=pltpu.VMEM)
SMEM = pl.BlockSpec(memory_space=pltpu.SMEM)
NT_DIMS = (((1,), (1,)), ((), ()))
TN_DIMS = (((0,), (0,)), ((), ()))


def params(mib=24):
    return pltpu.CompilerParams(vmem_limit_bytes=mib * 1024 * 1024)


def cost(flops, size):
    return pl.CostEstimate(flops=int(flops), bytes_accessed=int(size), transcendentals=0)


def sds(shape, dtype):
    return jax.ShapeDtypeStruct(shape, dtype)


def norm_rows(values):
    centre = jnp.mean(values, axis=-1, keepdims=True)
    shifted = values - centre
    spread = jnp.mean(shifted * shifted, axis=-1, keepdims=True)
    inverse = lax.rsqrt(spread + EPS)
    return shifted * inverse, inverse


def norm_back(upstream, normed, inverse):
    first = jnp.mean(upstream, axis=-1, keepdims=True)
    second = jnp.mean(upstream * normed, axis=-1, keepdims=True)
    return inverse * (upstream - first - normed * second)


def in_hbm(part):
    return pltpu.with_memory_space_constraint(part, pltpu.HBM)


def pack_kernel(tokens, moments, out):
    out[0:256, :] = tokens[...]
    time = moments[...].reshape(1, 256)
    rows = jnp.concatenate([time // T, time % T, jnp.zeros((14, 256), i32)], axis=0)
    out[256:, 0:256] = rows.astype(f32).astype(bf16)
    out[256:, 256:] = jnp.zeros((16, 768), bf16)


def pack(tokens, moments):
    return pl.pallas_call(
        pack_kernel,
        in_specs=[VMEM] * 2,
        out_specs=VMEM,
        out_shape=sds((272, 1024), bf16),
        compiler_params=params(8),
        cost_estimate=cost(1 << 16, 1 << 20),
        name="pack",
    )(in_hbm(tokens), in_hbm(moments))


def project_kernel(own, tokens, *refs):
    weights, outs, normed = refs[own : 2 * own + 2], refs[2 * own + 2 : -1], refs[-1]
    head = pl.program_id(0)
    shift = (head + 4 - (lax.axis_index("ctx") // 2) % 4) % 4

    @pl.when(head == 0)
    def _():
        normed[...] = norm_rows(tokens[0:256, :].astype(f32))[0].astype(bf16)

    wide = jnp.concatenate([w[...] for w in weights], axis=1)
    half = 0.5 * jnp.dot(normed[...], wide, preferred_element_type=f32)
    act = (half * jnp.tanh(half) + half).astype(bf16)
    meta = tokens[256:, 0:256]
    if own:
        mask, blank = refs[0], jnp.zeros((1, T - TILES), f32)
        row = [mask[0, 0:1].astype(f32), blank, mask[0, 1:2].astype(f32), blank]
        rows = [meta[0:2].astype(f32), jnp.concatenate(row, axis=1), jnp.zeros((13, 256), f32)]
        meta = jnp.concatenate(rows, axis=0).astype(bf16)
    for which in range(4):

        @pl.when(shift == which)
        def _(which=which):
            outs[which][0:256, :] = act
            outs[which][256:, 0:256] = meta
            if own:
                outs[which][256:, 256:] = jnp.zeros((16, T), bf16)


def project(tokens, in_proj, mask=None):
    own = mask is not None
    width = 384 if own else 256

    def column(kind):
        return pl.BlockSpec((1024, T), lambda h: (0, kind * HEADS + h))

    whole = lambda shape: pl.BlockSpec(shape, lambda h: (0,) * len(shape))
    kinds = (3, 1, 2) if own else (3, 1)
    return pl.pallas_call(
        functools.partial(project_kernel, int(own)),
        grid=(HEADS,),
        in_specs=[whole((272, 1024))] + [whole((1, 2, TILES))] * own + [column(kind) for kind in kinds],
        out_specs=[whole((272, width))] * 4,
        out_shape=[sds((272, width), bf16)] * 4,
        scratch_shapes=[pltpu.VMEM((256, 1024), bf16)],
        compiler_params=params(12),
        cost_estimate=cost(2 * 256 * 1024 * 4 * width, 5 << 20),
        name="project_own" if own else "project_other",
    )(tokens, *([in_hbm(mask)] if own else []), *[in_hbm(in_proj)] * len(kinds))


def gates_kernel(tokens, in_proj, cot, out_proj, gate, slope, grad_mix, normed):
    kind = pl.program_id(0)

    @pl.when(kind == 0)
    def _():
        normed[...] = norm_rows(tokens[...].astype(f32))[0].astype(bf16)
        grad_mix[...] = lax.dot_general(cot[...], out_proj[...], NT_DIMS, preferred_element_type=f32)

    pre = jnp.dot(normed[...], in_proj[...], preferred_element_type=f32)
    sig = 0.5 * jnp.tanh(0.5 * pre) + 0.5
    slope[...] = (sig * (1.0 + pre * (1.0 - sig))).astype(bf16)

    @pl.when(kind == 0)
    def _():
        gate[...] = (pre * sig).astype(bf16)


def make_gates(tokens, in_proj, cot, out_proj):
    whole = lambda shape: pl.BlockSpec(shape, lambda s: (0,) * len(shape))
    return pl.pallas_call(
        gates_kernel,
        grid=(4,),
        in_specs=[
            whole((256, 1024)),
            pl.BlockSpec((1024, 512), lambda s: (0, s)),
            whole((256, 1024)),
            whole((512, 1024)),
        ],
        out_specs=[whole((256, 512)), pl.BlockSpec((256, 512), lambda s: (0, s)), whole((256, 512))],
        out_shape=[
            pltpu.VMEM((256, 512), bf16),
            pltpu.VMEM((256, 2048), bf16),
            pltpu.VMEM((256, 512), f32),
        ],
        scratch_shapes=[pltpu.VMEM((256, 1024), bf16)],
        compiler_params=params(16),
        cost_estimate=cost(2 * 256 * 1024 * 2048, 7 << 20),
        name="gates",
    )(in_hbm(tokens), in_hbm(in_proj), in_hbm(cot), in_hbm(out_proj))


def bias_far(gap, table, bottom):
    first = table[bottom]
    second = table[bottom + 1]
    third = table[bottom + 2]
    limit1 = table[16 + bottom + 1]
    limit2 = table[16 + bottom + 2]
    over1 = gap >= limit1
    over2 = gap >= limit2
    return jnp.where(over2, third, jnp.where(over1, second, first)), over1, over2


def bias_near(gap, table):
    bias = jnp.full(gap.shape, table[0], f32)
    for j in range(1, BUCKETS):
        bias = jnp.where(gap >= float(2**j - 1), table[j], bias)
    return bias


def keep_near(ids, start, jj, k):
    tile = query_tile(ids, jj)
    row = lax.broadcasted_iota(i32, (T, T), 0)
    col = lax.broadcasted_iota(i32, (T, T), 1)
    later = (col - row) <= (tile - k) * T
    return later & ((col + k * T) >= start)


STAGE = [pltpu.VMEM((QT + 1, T, T), f32), pltpu.VMEM((QT + 1, T, T), i32)]


def query_tile(ids, jj):
    dev = ids[0] * 8 + (jj // 2) * 2 + ids[2]
    return jnp.where(jj % 2 == 0, dev, 2 * DEVS - 1 - dev)


def starts_of(lengths, pos):
    end0 = lengths[0]
    end1 = lengths[0] + lengths[1]
    return jnp.where(pos >= end1, end1, jnp.where(pos >= end0, end0, 0))


def stage(ids, ins, keys, values, queries, tk, flags, times):
    y, z, core = ids[0], ids[1], ids[2]
    for group in range(4):
        for t in range(4):
            ref = ins[group * 4 + t]
            zz = (z + 4 - t) % 4
            dev = (y if group < 2 else 1 - y) * 8 + zz * 2 + (core if group % 2 == 0 else 1 - core)
            keys[dev] = ref[0:T, 0:T]
            values[dev] = ref[0:T, T : 2 * T]
            keys[2 * DEVS - 1 - dev] = ref[T : 2 * T, 0:T]
            values[2 * DEVS - 1 - dev] = ref[T : 2 * T, T : 2 * T]
            head = ref[256:272, 0:256].astype(f32)
            moments = head[0:1] * 128.0 + head[1:2]
            tk[dev] = jnp.broadcast_to(moments[:, :T], (8, T))
            tk[2 * DEVS - 1 - dev] = jnp.broadcast_to(moments[:, T:], (8, T))
            times[pl.ds(dev, 1), :] = moments[:, :T]
            times[pl.ds(2 * DEVS - 1 - dev, 1), :] = moments[:, T:]
            if group == 0:
                queries[2 * zz] = ref[0:T, 2 * T :]
                queries[2 * zz + 1] = ref[T : 2 * T, 2 * T :]
                flags[pl.ds(2 * zz, 1), :] = head[2:3, :T]
                flags[pl.ds(2 * zz + 1, 1), :] = head[2:3, T:]
    keys[TILES] = jnp.zeros((T, T), bf16)
    values[TILES] = jnp.zeros((T, T), bf16)
    queries[QT] = jnp.zeros((T, T), bf16)
    tk[TILES] = jnp.zeros((8, T), f32)


def stage_times(ids, lengths, tq, tk, start):
    tq[QT] = jnp.zeros((T, T), f32)
    start[QT] = jnp.zeros((T, T), i32)
    rows = lax.broadcasted_iota(i32, (T, T), 0)
    for jj in range(QT):
        tile = query_tile(ids, jj)
        tq[jj] = jnp.transpose(jnp.broadcast_to(tk[tile][0:1, :], (T, T)))
        start[jj] = starts_of(lengths, rows + tile * T)


def make_lists(ids, lengths, flags, times, q_times, codes, codes_smem, sem, far, near, counts):
    def level(gap):
        total = jnp.zeros(gap.shape, i32)
        for j in range(1, BUCKETS):
            total = total + jnp.where(gap >= float(2**j - 1), 1, 0)
        return total

    for jj in range(QT):
        q_times[jj : jj + 1, :] = times[pl.ds(query_tile(ids, jj), 1), :]
    turned = jnp.transpose(times[...])
    k_first, k_last = turned[0:1, :], turned[T - 1 :, :]
    q_first, q_last = q_times[:, 0:1], q_times[:, T - 1 :]
    jj = lax.broadcasted_iota(i32, (8, T), 0)
    kk = lax.broadcasted_iota(i32, (8, T), 1)
    tile = query_tile(ids, jj)
    low = starts_of(lengths, tile * T)
    high = starts_of(lengths, tile * T + T - 1)
    bottom = level(jnp.maximum(q_first - k_last, 0.0))
    top = level(q_last - k_first)
    row = lax.broadcasted_iota(i32, (T, T), 0)
    col = lax.broadcasted_iota(i32, (T, T), 1)
    turn = jnp.where(row == jnp.where(col < DEVS, 2 * col, 4 * DEVS - 1 - 2 * col), 1.0, 0.0).astype(bf16)
    ordered = jnp.dot(flags[...].astype(bf16), turn, preferred_element_type=f32)
    allowed = (ordered > 0.5) & (kk <= tile) & (kk * T + T - 1 >= low)
    plain = (kk < tile) & (kk * T >= high) & (top - bottom <= 2)
    entry = jj + 16 * kk
    codes[...] = jnp.where(
        allowed, jnp.where(plain, entry + 1024 * bottom, entry + NEAR_FLAG), -1
    )
    copy = pltpu.make_async_copy(codes, codes_smem, sem)
    copy.start()
    copy.wait()

    def query_step(jj, sizes):
        tile = query_tile(ids, jj)

        def key_step(k, sizes):
            n_far, n_near = sizes
            code = codes_smem[jj, k]
            far[n_far] = code
            near[n_near] = code & (NEAR_FLAG - 1)
            is_near = code >= NEAR_FLAG
            is_far = (code >= 0) & jnp.logical_not(is_near)
            return n_far + is_far.astype(i32), n_near + is_near.astype(i32)

        return lax.fori_loop(starts_of(lengths, tile * T) // T, tile + 1, key_step, sizes)

    n_far, n_near = lax.fori_loop(0, QT, query_step, (jnp.int32(0), jnp.int32(0)))
    for pad in range(FAR_U):
        far[n_far + pad] = DUMMY
    for pad in range(NEAR_U):
        near[n_near + pad] = DUMMY
    counts[0] = (n_far + FAR_U - 1) // FAR_U
    counts[1] = (n_near + NEAR_U - 1) // NEAR_U


def unpack(ref, i, count):
    got = []
    for u in range(count):
        entry = ref[i * count + u]
        got.append((entry & 15, (entry >> 4) & 63, entry >> 10))
    return got


def forward_kernel(ids, table, lengths, *refs):
    ins, (out, far, near, counts, keys, values, queries, tk) = refs[:16], refs[16:24]
    tq, start, acc, flags, times, q_times, codes, codes_smem, sem = refs[24:]
    times[...] = jnp.zeros(times.shape, f32)
    stage(ids, ins, keys, values, queries, tk, flags, times)
    stage_times(ids, lengths, tq, tk, start)
    make_lists(ids, lengths, flags, times, q_times, codes, codes_smem, sem, far, near, counts)
    acc[...] = jnp.zeros(acc.shape, f32)

    def far_step(i, _):
        got = unpack(far, i, FAR_U)
        dots = [lax.dot_general(queries[j], keys[k], NT_DIMS, preferred_element_type=f32) for j, k, _ in got]
        weights = []
        for u, (jj, k, bottom) in enumerate(got):
            bias, _, _ = bias_far(tq[jj] - tk[k][0:1, :], table, bottom)
            half = dots[u] * (0.5 * SCALE) + bias
            weights.append((half * jnp.tanh(half) + half).astype(bf16))
        adds = [jnp.dot(weights[u], values[got[u][1]], preferred_element_type=f32) for u in range(len(got))]
        for u in range(len(got)):
            acc[got[u][0]] += adds[u]
        return 0

    def near_step(i, _):
        got = unpack(near, i, NEAR_U)
        dots = [lax.dot_general(queries[j], keys[k], NT_DIMS, preferred_element_type=f32) for j, k, _ in got]
        weights = []
        for u, (jj, k, _) in enumerate(got):
            half = dots[u] * (0.5 * SCALE) + bias_near(tq[jj] - tk[k][0:1, :], table)
            weight = half * jnp.tanh(half) + half
            weights.append(jnp.where(keep_near(ids, start[jj], jj, k), weight, 0.0).astype(bf16))
        adds = [jnp.dot(weights[u], values[got[u][1]], preferred_element_type=f32) for u in range(len(got))]
        for u in range(len(got)):
            acc[got[u][0]] += adds[u]
        return 0

    lax.fori_loop(0, counts[0], far_step, 0)
    lax.fori_loop(0, counts[1], near_step, 0)
    for zz in range(4):
        out[zz, 0:T] = acc[2 * zz]
        out[zz, T:] = acc[2 * zz + 1]


def attend(ids, table, lengths, parts):
    return pl.pallas_call(
        forward_kernel,
        in_specs=[SMEM] * 3 + [VMEM] * 16,
        out_specs=[VMEM] + [SMEM] * 3 + [VMEM] * 4,
        out_shape=[sds((4, 256, T), f32), sds((LIST,), i32), sds((LIST,), i32), sds((8,), i32)]
        + [pltpu.HBM((TILES + 1, T, T), bf16)] * 2
        + [pltpu.HBM((QT + 1, T, T), bf16), pltpu.HBM((TILES + 1, 8, T), f32)],
        scratch_shapes=STAGE
        + [
            pltpu.VMEM((QT + 1, T, T), f32),
            pltpu.VMEM((8, T), f32),
            pltpu.VMEM((T, T), f32),
            pltpu.VMEM((8, T), f32),
            pltpu.VMEM((8, T), i32),
            pltpu.SMEM((8, T), i32),
            pltpu.SemaphoreType.DMA,
        ],
        compiler_params=params(VM_ATTEND),
        cost_estimate=cost(1e9 * 6, 6 << 20),
        name="attend",
    )(ids, table, lengths, *parts)


def middle_kernel(heads, gate, slope, grad_mix, mixed, grad_gate, grads):
    whole = jnp.concatenate([heads[h] for h in range(4)], axis=1)
    normed, inverse = norm_rows(whole)
    gates = gate[...].astype(f32)
    mixed[...] = (normed * gates).astype(bf16)
    back = grad_mix[...]
    grad_gate[...] = (back * normed * slope[...].astype(f32)).astype(bf16)
    grad = norm_back(back * gates, normed, inverse).astype(bf16)
    for h in range(4):
        grads[h] = grad[:, h * T : (h + 1) * T]


def middle(heads, gate, slope, grad_mix):
    whole = lambda shape: pl.BlockSpec(shape, lambda i: (0,) * len(shape))
    return pl.pallas_call(
        middle_kernel,
        grid=(1,),
        in_specs=[whole((4, 256, T)), whole((256, 512)), whole((256, 512)), whole((256, 512))],
        out_specs=[whole((256, 512)), whole((256, 512)), whole((4, 256, T))],
        out_shape=[
            pltpu.HBM((256, 512), bf16),
            pltpu.HBM((256, 512), bf16),
            sds((4, 256, T), bf16),
        ],
        compiler_params=params(12),
        cost_estimate=cost(1 << 24, 3 << 20),
        name="middle",
    )(heads, gate, slope, grad_mix)


def output_kernel(ids, tokens, cot, out_proj, mixed, output, mine, *theirs):
    y, z, core, low, x = ids[0], ids[1], ids[2], ids[3] // 4, ids[3] % 4
    output[...] = (
        tokens[...].astype(f32) + jnp.dot(mixed[...], out_proj[...], preferred_element_type=f32)
    ).astype(bf16)
    r = lax.broadcasted_iota(i32, (512, 512), 1)
    c = lax.broadcasted_iota(i32, (512, 512), 0)
    r_x = ((r // 128) + x) % 4
    r_core = ((r // 64) % 2) ^ core
    r_z = (((r // 16) % 4) + z) % 4
    r_y = ((r // 8) % 2) ^ y
    source = (((r // 4) % 2) * 4 + r_x) * 64 + r_y * 32 + r_z * 8 + r_core * 4 + r % 4
    pick = jnp.where(c == source, 1.0, 0.0).astype(bf16)
    moved = jnp.dot(mixed[...], pick, preferred_element_type=f32).astype(bf16)
    part = lax.dot_general(moved, cot[...], TN_DIMS, preferred_element_type=f32)
    mine[...] = part[:T]
    for i in range(3):
        theirs[i][...] = part[(i + 1) * T : (i + 2) * T].astype(bf16)


def finish_output(ids, tokens, cot, out_proj, mixed):
    return pl.pallas_call(
        output_kernel,
        in_specs=[SMEM] + [VMEM] * 4,
        out_specs=[VMEM] * 5,
        out_shape=[sds((256, 1024), bf16), sds((T, 1024), f32)] + [sds((T, 1024), bf16)] * 3,
        compiler_params=params(24),
        cost_estimate=cost(6 * 256 * 512 * 1024, 5 << 20),
        name="finish_output",
    )(ids, in_hbm(tokens), in_hbm(cot), in_hbm(out_proj), in_hbm(mixed))


def backward_kernel(ids, table, lengths, far, near, counts, *refs):
    (keys, values, queries, tk), got_grads, outs = refs[:4], refs[4], refs[5:11]
    mine_s, mine_o, theirs_s, theirs_o, dq_out, rab_out = outs
    tq, start, grads, grads_t, queries_t, dq, dkt, dvt, rab = refs[11:]
    y, z, core = ids[0], ids[1], ids[2]
    stage_times(ids, lengths, tq, tk, start)
    for zz in range(4):
        for half in range(2):
            block = got_grads[zz, half * T : (half + 1) * T, :].astype(f32) * 0.5
            grads[2 * zz + half] = block.astype(bf16)
            grads_t[2 * zz + half] = jnp.transpose(block).astype(bf16)
    for jj in range(QT):
        queries_t[jj] = jnp.transpose(queries[jj].astype(f32)).astype(bf16)
    grads[QT] = jnp.zeros((T, T), bf16)
    grads_t[QT] = jnp.zeros((T, T), bf16)
    queries_t[QT] = jnp.zeros((T, T), bf16)
    dq[...] = jnp.zeros(dq.shape, f32)
    dkt[...] = jnp.zeros(dkt.shape, f32)
    dvt[...] = jnp.zeros(dvt.shape, f32)
    rab[...] = jnp.zeros(rab.shape, f32)

    def fold(values_):
        return jnp.sum(values_.reshape(T // 8, 8, T), axis=0)

    def front(got):
        dots = [lax.dot_general(queries[j], keys[k], NT_DIMS, preferred_element_type=f32) for j, k, _ in got]
        wides = [lax.dot_general(grads[j], values[k], NT_DIMS, preferred_element_type=f32) for j, k, _ in got]
        return dots, wides

    def score(half, wide, keep):
        t = jnp.tanh(half)
        weight = half * t + half
        d_score = wide * ((1.0 + t) * (1.0 + half * (1.0 - t)))
        if keep is not None:
            weight = jnp.where(keep, weight, 0.0)
            d_score = jnp.where(keep, d_score, 0.0)
        return weight.astype(bf16), d_score

    def back(got, weights, scores):
        a = [jnp.dot(scores[u], keys[got[u][1]], preferred_element_type=f32) for u in range(len(got))]
        b = [jnp.dot(queries_t[got[u][0]], scores[u], preferred_element_type=f32) for u in range(len(got))]
        c = [jnp.dot(grads_t[got[u][0]], weights[u], preferred_element_type=f32) for u in range(len(got))]
        for u, (jj, k, _) in enumerate(got):
            dq[jj] += a[u]
            dkt[k] += b[u]
            dvt[k] += c[u]

    def far_step(i, _):
        got = unpack(far, i, FAR_U)
        dots, wides = front(got)
        weights, scores, sums = [], [], []
        for u, (jj, k, bottom) in enumerate(got):
            bias, over1, over2 = bias_far(tq[jj] - tk[k][0:1, :], table, bottom)
            weight, d_score = score(dots[u] * (0.5 * SCALE) + bias, wides[u], None)
            weights.append(weight)
            scores.append(d_score.astype(bf16))
            sums.append((fold(d_score), fold(jnp.where(over1, d_score, 0.0)), fold(jnp.where(over2, d_score, 0.0))))
        back(got, weights, scores)
        for (jj, k, bottom), (sum0, sum1, sum2) in zip(got, sums):
            rab[bottom] += sum0 - sum1
            rab[bottom + 1] += sum1 - sum2
            rab[bottom + 2] += sum2
        return 0

    def near_step(i, _):
        got = unpack(near, i, NEAR_U)
        dots, wides = front(got)
        weights, scores = [], []
        sums = [jnp.zeros((8, T), f32)] * BUCKETS
        for u, (jj, k, _) in enumerate(got):
            gap = tq[jj] - tk[k][0:1, :]
            half = dots[u] * (0.5 * SCALE) + bias_near(gap, table)
            weight, d_score = score(half, wides[u], keep_near(ids, start[jj], jj, k))
            weights.append(weight)
            scores.append(d_score.astype(bf16))
            sums[0] = sums[0] + fold(d_score)
            for j in range(1, BUCKETS):
                sums[j] = sums[j] + fold(jnp.where(gap >= float(2**j - 1), d_score, 0.0))
        back(got, weights, scores)
        for j in range(BUCKETS - 1):
            rab[j] += sums[j] - sums[j + 1]
        rab[BUCKETS - 1] += sums[BUCKETS - 1]
        return 0

    lax.fori_loop(0, counts[0], far_step, 0)
    lax.fori_loop(0, counts[1], near_step, 0)
    for other in range(2):
        for s in range(4):
            base = (y if other == 0 else 1 - y) * 8 + ((z + s) % 4) * 2
            for side in range(2):
                dev = base + (core if side == 0 else 1 - core)
                ref = ((mine_s, theirs_s), (mine_o, theirs_o))[other][side]
                for half in range(2):
                    tile = dev if half == 0 else 2 * DEVS - 1 - dev
                    ref[s, 0:T, half * T : (half + 1) * T] = (dkt[tile] * SCALE).astype(bf16)
                    ref[s, T:, half * T : (half + 1) * T] = (dvt[tile] * 2.0).astype(bf16)
    for s in range(4):
        zz = (z + s) % 4
        for half in range(2):
            dq_out[s, :, half * T : (half + 1) * T] = (dq[2 * zz + half] * SCALE).astype(bf16)
    for b in range(16):
        if b < BUCKETS:
            rab_out[b : b + 1, :] = jnp.sum(rab[b], axis=0, keepdims=True)
        else:
            rab_out[b : b + 1, :] = jnp.zeros((1, T), f32)


def attend_back(ids, table, lengths, saved, grads):
    return pl.pallas_call(
        backward_kernel,
        in_specs=[SMEM] * 6 + [VMEM] * 5,
        out_specs=[VMEM] * 6,
        out_shape=[sds((4, 256, 256), bf16)] * 4 + [sds((4, T, 256), bf16), sds((16, T), f32)],
        scratch_shapes=STAGE
        + [
            pltpu.VMEM((QT + 1, T, T), bf16),
            pltpu.VMEM((QT + 1, T, T), bf16),
            pltpu.VMEM((QT + 1, T, T), bf16),
            pltpu.VMEM((QT + 1, T, T), f32),
            pltpu.VMEM((TILES + 1, T, T), f32),
            pltpu.VMEM((TILES + 1, T, T), f32),
            pltpu.VMEM((16, 8, T), f32),
        ],
        compiler_params=params(VM_BACK),
        cost_estimate=cost(1e9 * 12, 8 << 20),
        name="attend_back",
    )(ids, table, lengths, *saved[:3], *[in_hbm(part) for part in saved[3:]], grads)


def combine_kernel(mine_s, mine_o, got_s, got_o, dq, proj_own, proj_got, rab, rab_got, *outs):
    proj = proj_own[...] + proj_got[...].astype(f32)
    both = rab[...] + rab_got[...]
    high = both.astype(bf16)
    low = (both - high.astype(f32)).astype(bf16)
    for s in range(4):
        outs[s][0:256, :] = (mine_s[s].astype(f32) + got_s[s].astype(f32)).astype(bf16)
        outs[s][256:384, :] = dq[s]
        outs[4 + s][0:256, :] = (mine_o[s].astype(f32) + got_o[s].astype(f32)).astype(bf16)
        for other in range(2):
            block = proj[s * 16 + other * 8 : s * 16 + other * 8 + 8, :]
            block = jnp.concatenate([block[:, c * 256 : (c + 1) * 256] for c in range(4)], axis=0)
            base = 384 - 128 * other
            outs[4 * other + s][base : base + 32, :] = block.astype(bf16)
            outs[4 * other + s][base + 32 :, 0:T] = high
            outs[4 * other + s][base + 32 :, T:] = low


def combine(*parts):
    return pl.pallas_call(
        combine_kernel,
        in_specs=[VMEM] * 9,
        out_specs=[VMEM] * 8,
        out_shape=[sds((432, 256), bf16)] * 4 + [sds((304, 256), bf16)] * 4,
        compiler_params=params(24),
        cost_estimate=cost(1 << 20, 5 << 20),
        name="combine",
    )(*parts)


def collect_kernel(ids, *refs):
    ins, rabs, out = refs[:8], refs[8:16], refs[16]
    total = ins[0][...].astype(f32)
    for ref in ins[1:]:
        total = total + ref[...].astype(f32)
    for d in range(8):
        for c in range(4):
            rows = total[c * 8 + (d // 4) * 4 : c * 8 + (d // 4) * 4 + 4, :]
            out[d, 0:4, c * 256 : (c + 1) * 256] = jnp.where(ids[3] % 4 == d % 4, rows, 0.0)
    lane = lax.broadcasted_iota(i32, (16, T), 1)
    table = jnp.zeros((16, T), f32)
    for t in range(4):
        near, far = rabs[t][...].astype(f32), rabs[4 + t][...].astype(f32)
        near, far = near[:, :T] + near[:, T:], far[:, :T] + far[:, T:]
        first, second = jnp.where(ids[0] == 0, near, far), jnp.where(ids[0] == 0, far, near)
        head = (ids[1] + 4 - t) % 4
        table = jnp.where(lane == head, jnp.sum(first + second, axis=1, keepdims=True), table)
    turned = jnp.transpose(jnp.concatenate([table, jnp.zeros((T - 16, T), f32)], axis=0))
    for d in range(8):
        out[d, 4:, :T] = turned[0:4]
        out[d, 4:, T:] = jnp.zeros((4, 1024 - T), f32)


def collect(ids, same, other):
    return pl.pallas_call(
        collect_kernel,
        grid=(1,),
        in_specs=[SMEM]
        + [pl.BlockSpec((32, 256), lambda i: (12, 0))] * 4
        + [pl.BlockSpec((32, 256), lambda i: (8, 0))] * 4
        + [pl.BlockSpec((16, 256), lambda i: (26, 0))] * 4
        + [pl.BlockSpec((16, 256), lambda i: (18, 0))] * 4,
        out_specs=pl.BlockSpec((8, 8, 1024), lambda i: (0, 0, 0)),
        out_shape=sds((8, 8, 1024), f32),
        compiler_params=params(8),
        cost_estimate=cost(1 << 16, 1 << 18),
        name="collect",
    )(ids, *same, *other, *same, *other)


def lines_kernel(lines, proj_grad, rab_grad):
    total = lines[0]
    for d in range(1, 8):
        total = total + lines[d]
    proj_grad[...] = total[0:4]
    rab_grad[...] = total[4:, 0:BUCKETS]


def add_lines(lines):
    return pl.pallas_call(
        lines_kernel,
        in_specs=[VMEM],
        out_specs=[VMEM] * 2,
        out_shape=[sds((4, 1024), f32), sds((HEADS, BUCKETS), f32)],
        compiler_params=params(8),
        cost_estimate=cost(1 << 16, 1 << 18),
        name="add_lines",
    )(lines)


def ready_kernel(tokens, cot, in_proj, normed, inverse, cot_out, in_proj_out, sems):
    copies = [
        pltpu.make_async_copy(in_proj, in_proj_out, sems.at[0]),
        pltpu.make_async_copy(cot, cot_out, sems.at[1]),
    ]
    for copy in copies:
        copy.start()
    shaped, scale = norm_rows(tokens[...].astype(f32))
    normed[...] = shaped
    inverse[...] = jnp.broadcast_to(scale, (256, T))
    for copy in copies:
        copy.wait()


def make_ready(tokens, cot, in_proj):
    hbm = pl.BlockSpec(memory_space=pltpu.HBM)
    return pl.pallas_call(
        ready_kernel,
        in_specs=[VMEM, hbm, hbm],
        out_specs=[VMEM] * 4,
        out_shape=[
            pltpu.VMEM((256, 1024), f32),
            pltpu.VMEM((256, T), f32),
            pltpu.VMEM((256, 1024), bf16),
            pltpu.VMEM((1024, 2048), bf16),
        ],
        scratch_shapes=[pltpu.SemaphoreType.DMA((2,))],
        compiler_params=params(16),
        cost_estimate=cost(1 << 22, 6 << 20),
        name="ready",
    )(in_hbm(tokens), in_hbm(cot), in_hbm(in_proj))


def final_kernel(ids, grad_gate, slope, normed, inverse, cot, in_proj, *refs):
    same, other, grad_in, grad_pre = refs[:4], refs[4:8], refs[8], refs[9]
    z = ids[1]
    grad_pre[:, 0:512] = grad_gate[...]
    for t in range(4):
        head = (z + 4 - t) % 4
        column = lambda kind: pl.ds(pl.multiple_of(kind * 512 + head * T, T), T)
        total = same[t][0:256, :].astype(f32) + other[t][0:256, :].astype(f32)
        for half in range(2):
            rows = slice(half * T, (half + 1) * T)
            key = jnp.transpose(total[0:T, rows])
            value = jnp.transpose(total[T:, rows])
            query = same[t][256:384, rows].astype(f32)
            for kind, part in ((1, value), (2, query), (3, key)):
                grad_pre[rows, column(kind)] = (
                    part * slope[rows, column(kind)].astype(f32)
                ).astype(bf16)
    upstream = lax.dot_general(grad_pre[...], in_proj[...], NT_DIMS, preferred_element_type=f32)
    back = norm_back(upstream, normed[...], inverse[:, 0:1])
    grad_in[...] = (cot[...].astype(f32) + back).astype(bf16)


def finish_grad(ids, ready, slope, grad_gate, same, other):
    return pl.pallas_call(
        final_kernel,
        in_specs=[SMEM] + [VMEM] * 14,
        out_specs=VMEM,
        out_shape=sds((256, 1024), bf16),
        scratch_shapes=[pltpu.VMEM((256, 2048), bf16)],
        compiler_params=params(24),
        cost_estimate=cost(2 * 256 * 1024 * 2048, 8 << 20),
        name="finish_grad",
    )(ids, grad_gate, slope, *ready, *same, *other)


def move(y_xor, z_shift, core_xor):
    pairs = []
    for dev in range(DEVS):
        y, z, core = dev // 8, (dev // 2) % 4, dev % 2
        target = (y ^ y_xor) * 8 + ((z + z_shift) % 4) * 2 + (core ^ core_xor)
        pairs.append((dev, target))
    return pairs


def send(x, y_xor, z_shift, core_xor):
    return lax.ppermute(x, "ctx", move(y_xor, z_shift, core_xor))


OVER_Z = [[y * 8 + z * 2 + c for z in range(4)] for y in range(2) for c in range(2)]
OVER_X = [[low * 4 + x for x in range(4)] for low in range(2)]


def send_x(part, shift):
    return lax.ppermute(part, "dp", [(d, d // 4 * 4 + (d + shift) % 4) for d in range(8)])


def swap_z(part):
    return lax.all_to_all(part, "ctx", 0, 0, axis_index_groups=OVER_Z, tiled=True)


def on_device(tokens, cotangent, in_proj, out_proj, rab_time, seq_lengths, block_mask, time_bucket):
    ctx = lax.axis_index("ctx")
    y, z, core = ctx // 8, (ctx // 2) % 4, ctx % 2
    near_tokens = pack(tokens, time_bucket)
    far_tokens = send(near_tokens, 1, 0, 0)
    ids = jnp.stack([y, z, core, lax.axis_index("dp")]).astype(i32)
    lengths = seq_lengths.reshape(3)
    limits = [2.0**j - 1.0 for j in range(BUCKETS)] + [1e9] * 4
    head_bias = lax.dynamic_slice_in_dim(rab_time, z, 1, 1).reshape(BUCKETS) * 0.5
    table = jnp.concatenate([head_bias, jnp.zeros((4,), f32), jnp.array(limits, f32)])
    full = project(near_tokens, in_proj, block_mask)
    full, ids, table = lax.optimization_barrier((full, ids, table))
    own = [full[0]] + [send(full[s], 0, s, 0) for s in (1, 2, 3)]
    pairs = project(far_tokens, in_proj)
    across = [pairs[0]] + [send(pairs[s], 0, s, 0) for s in (1, 2, 3)]
    own, across[1] = lax.optimization_barrier((own, across[1]))
    gate, slope, grad_mix = make_gates(tokens, in_proj, cotangent, out_proj)
    own_twin = [send(part, 0, 0, 1) for part in own]
    across_twin = [send(part, 0, 0, 1) for part in across]
    parts = own + own_twin + across + across_twin

    heads, *saved = attend(ids, table, lengths, parts)

    mixed, grad_gate, grads = middle(swap_z(heads), gate, slope, grad_mix)
    grads = swap_z(grads)
    output, proj, *proj_x = finish_output(ids, tokens, cotangent, out_proj, mixed)
    grads, _ = lax.optimization_barrier((grads, proj_x))
    proj_x = [send_x(proj_x[s - 1], s) for s in (1, 2, 3)]

    mine_s, mine_o, theirs_s, theirs_o, dq, rab = attend_back(ids, table, lengths, saved, grads)
    got_o = send(theirs_o, 0, 0, 1)
    got_s = send(theirs_s, 0, 0, 1)
    rab_got = send(rab, 0, 0, 1)
    for part in proj_x:
        proj = proj + part.astype(f32)
    proj_own, proj_got = proj[:64], send(proj[64:].astype(bf16), 0, 0, 1)
    messages = combine(mine_s, mine_o, got_s, got_o, dq, proj_own, proj_got, rab, rab_got)
    messages, late_cot = lax.optimization_barrier((messages, cotangent))
    ready = make_ready(tokens, late_cot, in_proj)
    same = [messages[0]] + [send(messages[s], 0, s, 0) for s in (1, 2, 3)]
    other = [send(messages[4 + s], 1, s, 0) for s in range(4)]
    lines = lax.all_to_all(collect(ids, same, other), "dp", 0, 0, tiled=True)
    proj_grad, rab_grad = add_lines(lines)
    grad_in = finish_grad(ids, ready, slope, grad_gate, same, other)
    return output, grad_in, proj_grad, rab_grad.T


def solution(mesh):
    rows = P(("dp", "ctx"), None)
    placed = (rows, rows, P(), P(), P(), P("dp", None), P("dp", "ctx", None), P(("dp", "ctx")))
    return jax.shard_map(
        on_device,
        mesh=mesh,
        in_specs=placed,
        out_specs=(rows, rows, rows, P()),
        check_vma=False,
    )
```
